128 devices in a mesh: head: 4 (over z_lo, core), band: 32 (over y, x, z_hi).
Axes of the slice: x: 4, y: 4, z: 4 (z_hi: 2, z_lo: 2; z = z_hi * 2 + z_lo), core: 2. Of those that a mesh axis runs over, the one named last changes fastest.
Arguments:
- queries: bfloat16 [2048, 5120], P('band', 'head'), may hold values from -20 to 20, as said below
- keys: bfloat16 [2048, 5120], P('band', 'head'), may hold values from -20 to 20, as said below
- values: bfloat16 [2048, 5120], P('band', 'head'), may hold values from -6 to 6
- w_first: bfloat16 [40, 128], replicated, may hold values from -1 to 1
- b_first: float32 [128], replicated, may hold values from -4 to 4
- w_second: bfloat16 [128, 64], replicated, may hold values from -0.5 to 0.5
- b_second: float32 [64], replicated, may hold values from -3 to 3
- rel_table: bfloat16 [65, 64], replicated, may hold values from -4 to 4
- chain_lengths: int32 [4], replicated, may hold values from 1 to 1024, 2048 in all
Outputs:
- context: bfloat16 [2048, 5120], P('band', 'head')
- pair: bfloat16 [64, 2048, 2048], P(None, 'band', 'head')
The draws below stay inside these ranges and needn't reach their ends.
Inputs may be any that keep to these rules, and one draw needn't show every extreme that they name: Entries of the queries stay within this range. Entries of the keys stay within this range. `chain_lengths`: the chain lengths sum to 2048; the longest chain has exactly 1024 residues.
All inputs are finite; a program needn't handle non-finite values.
Results may differ from the reference program's by a relative error of at most 0.012.
Values may be sent and summed in bfloat16 or wider, within the bound.
No kernel may reach another device: no remote copies, remote signals or barrier semaphores. Data moves between devices by JAX's collectives and lax.ppermute only.
A program may use at most 128 MiB of HBM per device.

```python
import math
import jax
import jax.numpy as jnp
import numpy as np
from jax import lax

HEADS = 40
HEAD_DIM = 128
PAIR_HID = 128
PAIR_OUT = 64
CLIP = 32
GAP = 512
CHAINS = 4
SEQ = 2048
BINS = 65


def draw_queries(key, part):
    key = jax.random.fold_in(key, 11)
    drawn = jnp.clip(jax.random.normal(key, (SEQ, HEADS * HEAD_DIM), jnp.float32) * 1.25, -5.0, 5.0)
    return drawn.astype(jnp.bfloat16)


def draw_keys(key, part):
    key = jax.random.fold_in(key, 23)
    drawn = jnp.clip(jax.random.normal(key, (SEQ, HEADS * HEAD_DIM), jnp.float32) * 1.25, -5.0, 5.0)
    return drawn.astype(jnp.bfloat16)


def level_of(key, dims, pieces, smallest, high):
    level, own = 1.0, jax.random.fold_in(key, 6)
    for axis_at, shards_of in pieces:
        steps = jnp.exp(jax.random.uniform(jax.random.fold_in(own, axis_at), (shards_of,), jnp.float32, smallest / len(pieces), high / len(pieces)))
        level = level * jnp.repeat(steps, dims[axis_at] // shards_of).reshape([-1 if axis == axis_at else 1 for axis in range(len(dims))])
    return level


def split_up(count, total, most, slope):
    loads = [(1 << 20) // math.isqrt(standing ** slope) + 1 for standing in range(2, count + 1)]
    rest, holding = total - most - (count - 1), [1] * (count - 1)
    while rest > 0:
        movable = [i for i in range(count - 1) if holding[i] < most]
        whole, remaining = sum([loads[i] for i in movable]), rest
        for i in movable:
            addition = min(most - holding[i], max(1, remaining * loads[i] // whole), rest)
            holding[i] = holding[i] + addition
            rest = rest - addition
    return np.array([most] + holding)


def ragged_sizes(key, number_of, total, most, lean):
    if number_of == 2:
        one = jax.random.randint(key, (), max(1, total - most), min(most, total - 1) + 1)
        return jnp.stack([one, total - one])
    tallies = jnp.asarray(split_up(number_of, total, most, lean), jnp.int32)
    couples = (number_of - 1) // 2
    donor, taker = tallies[1:1 + 2 * couples:2], tallies[2:2 + 2 * couples:2]
    room = jnp.minimum(donor - 1, most - taker)
    passed = jax.random.randint(jax.random.fold_in(key, 1), (couples,), 0, 1 << 20) % (room + 1)
    tallies = tallies.at[1:1 + 2 * couples:2].set(donor - passed).at[2:2 + 2 * couples:2].set(taker + passed)
    return tallies[jax.random.permutation(jax.random.fold_in(key, 2), number_of)]


def normal_values(own_key, dims, width, reach, shards=(), kind=jnp.bfloat16):
    array = width * jax.random.normal(own_key, dims, jnp.float32)
    if shards:
        array = array * level_of(own_key, dims, shards, -0.22, 0.18)
    return jnp.clip(array, -reach, reach).astype(kind)


def setup_inputs(seed: int = 0) -> dict:
    streams_of = jax.random.split(jax.random.key(seed), 10)
    queries = draw_queries(jax.random.fold_in(streams_of[9], 71), 0)
    keys = draw_keys(jax.random.fold_in(streams_of[9], 71), 0)
    values = normal_values(streams_of[2], (SEQ, HEADS * HEAD_DIM), 1.0, 6.0, ((0, 32), (1, 4)))
    w_first = normal_values(streams_of[3], (HEADS, PAIR_HID), HEADS ** -0.5, 1.0)
    b_first = normal_values(streams_of[4], (PAIR_HID,), 1.0, 4.0, (), jnp.float32)
    w_second = normal_values(streams_of[5], (PAIR_HID, PAIR_OUT), PAIR_HID ** -0.5, 0.5)
    b_second = normal_values(streams_of[6], (PAIR_OUT,), 0.5, 3.0, (), jnp.float32)
    rel_table = normal_values(streams_of[7], (BINS, PAIR_OUT), 1.0, 4.0)
    chain_lengths = ragged_sizes(streams_of[8], CHAINS, SEQ, SEQ // 2, 2).astype(jnp.int32)
    return dict(queries=queries, keys=keys, values=values, w_first=w_first, b_first=b_first, w_second=w_second, b_second=b_second, rel_table=rel_table, chain_lengths=chain_lengths)


def residue_index(positions, chain_lengths):
    chain_ends = jnp.cumsum(chain_lengths)[:-1]
    crossed = lax.optimization_barrier(jnp.sum((positions[:, None] >= chain_ends[None, :]).astype(jnp.int32), axis=1))
    return positions + GAP * crossed

def reference(queries, keys, values, w_first, b_first, w_second, b_second, rel_table, chain_lengths):
    block_rows = math.gcd(SEQ, 128)
    blocks = SEQ // block_rows
    score_scale = 1.0 / math.sqrt(HEAD_DIM)
    query_all = queries.astype(jnp.float32).reshape(SEQ, HEADS, HEAD_DIM)
    key_all = keys.astype(jnp.float32).reshape(SEQ, HEADS, HEAD_DIM)
    value_all = values.astype(jnp.float32).reshape(SEQ, HEADS, HEAD_DIM)
    first_weight = w_first.astype(jnp.float32)
    second_weight = w_second.astype(jnp.float32)
    table_wide = rel_table.astype(jnp.float32)

    def statistics(index):
        start = (index * block_rows).astype(jnp.int32)
        query_rows = lax.dynamic_slice_in_dim(query_all, start, block_rows, 0)
        scores = jnp.einsum('qhd,khd->hqk', query_rows, key_all) * score_scale
        top = lax.optimization_barrier(jnp.max(scores, axis=2))
        total = lax.optimization_barrier(jnp.sum(jnp.exp(scores - top[:, :, None]), axis=2))
        return (top, total)
    tops, totals = lax.map(statistics, jnp.arange(blocks, dtype=jnp.int32))
    row_max = jnp.transpose(tops, (1, 0, 2)).reshape(HEADS, SEQ)
    row_sum = jnp.transpose(totals, (1, 0, 2)).reshape(HEADS, SEQ)
    residue = residue_index(jnp.arange(SEQ, dtype=jnp.int32), chain_lengths)

    def one_block(index):
        start = (index * block_rows).astype(jnp.int32)
        query_rows = lax.dynamic_slice_in_dim(query_all, start, block_rows, 0)
        key_rows = lax.dynamic_slice_in_dim(key_all, start, block_rows, 0)
        top = lax.dynamic_slice_in_dim(row_max, start, block_rows, 1)
        total = lax.dynamic_slice_in_dim(row_sum, start, block_rows, 1)
        scores = jnp.einsum('qhd,khd->hqk', query_rows, key_all) * score_scale
        maps = (jnp.exp(scores - top[:, :, None]) / total[:, :, None]).astype(jnp.bfloat16)
        context = jnp.einsum('hqk,khd->qhd', maps.astype(jnp.float32), value_all)
        context = context.reshape(block_rows, HEADS * HEAD_DIM).astype(jnp.bfloat16)
        turned = jnp.einsum('khd,qhd->hkq', key_rows, query_all) * score_scale
        mirrored = (jnp.exp(turned - row_max[:, None, :]) / row_sum[:, None, :]).astype(jnp.bfloat16)
        symmetric = ((maps.astype(jnp.float32) + mirrored.astype(jnp.float32)) * (0.5 * SEQ)).astype(jnp.bfloat16)
        hidden = jnp.einsum('hnc,hk->knc', symmetric.astype(jnp.float32), first_weight) + b_first[:, None, None]
        hidden = jnp.maximum(hidden, 0.0).astype(jnp.bfloat16)
        projected = jnp.einsum('knc,ko->onc', hidden.astype(jnp.float32), second_weight)
        residue_rows = lax.dynamic_slice_in_dim(residue, start, block_rows, 0)
        bins = jnp.clip(residue[None, :] - residue_rows[:, None], -CLIP, CLIP) + CLIP
        relative = jnp.transpose(table_wide[bins], (2, 0, 1))
        pair = (projected + b_second[:, None, None] + relative).astype(jnp.bfloat16)
        return (context, pair)
    contexts, pairs = lax.map(one_block, jnp.arange(blocks, dtype=jnp.int32))
    context = contexts.reshape(SEQ, HEADS * HEAD_DIM)
    pair = jnp.transpose(pairs, (1, 0, 2, 3)).reshape(PAIR_OUT, SEQ, SEQ)
    return (context, pair)
```

```python
import functools
import itertools
import math

import jax
import jax.numpy as jnp
from jax import lax
from jax.experimental import pallas as pl
from jax.experimental.pallas import tpu as pltpu
from jax.sharding import PartitionSpec as P

HEAD_DIM = 128
CLIP = 32
GAP = 512
BINS = 65
GROUP = 5
WIDE = GROUP * HEAD_DIM
BLOCK = 128
HALF = 64
TILE = 512
ROWS = 16
SCALE = math.log2(math.e) / math.sqrt(HEAD_DIM)
AXES = ("head", "band")
MIB = 1 << 20


def place(y, x, z, c):
    return c * 32 + y * 8 + x * 2 + z


def moves(to):
    return [
        (place(y, x, z, c), place(*to(y, x, z, c)))
        for c, y, x, z in itertools.product(range(4), range(4), range(4), range(2))
    ]


def send(value, to):
    return lax.ppermute(value, AXES, moves(to))


def nt(a, b):
    return lax.dot_general(a, b, (((1,), (1,)), ((), ())), preferred_element_type=jnp.float32)


def fetch(where, row_blocks, column_blocks, rows_ref, columns_ref, sems):
    y, x, z, c = (where[i] for i in range(4))
    copies = []
    for d in range(4):
        away = lax.rem(lax.bitwise_xor(c, d) - y + 4, 4)
        for part in range(2):
            start = pl.multiple_of(away * BLOCK + lax.bitwise_xor(z, part) * HALF, HALF)
            copies.append(
                pltpu.make_async_copy(
                    row_blocks[d].at[pl.ds(part * HALF, HALF), pl.ds(0, 2 * WIDE)],
                    rows_ref.at[pl.ds(start, HALF)],
                    sems.at[2 * d + part],
                )
            )
        start = pl.multiple_of(lax.rem(x - d + 4, 4) * BLOCK, BLOCK)
        copies.append(
            pltpu.make_async_copy(
                column_blocks[d], columns_ref.at[pl.ds(start, BLOCK)], sems.at[8 + d]
            )
        )
    for copy in copies:
        copy.start()
    for copy in copies:
        copy.wait()


def head(ref, part, h, rows=slice(None)):
    return ref[rows, part * WIDE + h * HEAD_DIM : part * WIDE + (h + 1) * HEAD_DIM]


def stats_kernel(where, *refs):
    row_blocks, column_blocks = refs[0:4], refs[4:8]
    by_row, by_column, rows_ref, columns_ref, sems = refs[8:]
    fetch(where, row_blocks, column_blocks, rows_ref, columns_ref, sems)
    by_row[...] = jnp.zeros_like(by_row)
    by_column[...] = jnp.zeros_like(by_column)
    for h in range(GROUP):
        for out, left, right in (
            (by_row, head(columns_ref, 1, h), head(rows_ref, 0, h)),
            (by_column, head(rows_ref, 1, h), head(columns_ref, 0, h)),
        ):
            scores = nt(left, right) * SCALE
            top = jnp.max(scores, axis=0, keepdims=True)
            out[h : h + 1, :] = top
            out[8 + h : 9 + h, :] = jnp.sum(jnp.exp2(scores - top), axis=0, keepdims=True)


def merged(refs):
    top = functools.reduce(jnp.maximum, [ref[0:8, :] for ref in refs])
    total = sum(ref[8:16, :] * jnp.exp2(ref[0:8, :] - top) for ref in refs)
    return top, total


def turned(value):
    return jnp.transpose(jnp.concatenate([value] * 16, axis=0))


def symmetric_kernel(where, *refs):
    row_blocks, column_blocks, row_stats, column_stats = refs[0:4], refs[4:8], refs[8:12], refs[12:16]
    outs = refs[16:24]
    rows_ref, columns_ref, sems = refs[24:]
    fetch(where, row_blocks, column_blocks, rows_ref, columns_ref, sems)
    row_top, row_total = merged(row_stats)
    column_top, column_total = merged(column_stats)
    row_top, row_gain = turned(row_top), turned(1024.0 / row_total)
    column_gain = 1024.0 / column_total
    for h in range(GROUP):
        straight = nt(head(rows_ref, 0, h), head(columns_ref, 1, h)) * SCALE
        mirrored = nt(head(rows_ref, 1, h), head(columns_ref, 0, h)) * SCALE
        summed = (
            jnp.exp2(straight - row_top[:, h : h + 1]) * row_gain[:, h : h + 1]
            + jnp.exp2(mirrored - column_top[h : h + 1, :]) * column_gain[h : h + 1, :]
        ).astype(jnp.bfloat16)
        for p in range(8):
            outs[p][h] = summed[p * HALF : (p + 1) * HALF]


def context_kernel(where, *refs):
    row_blocks, column_blocks, row_stats = refs[0:4], refs[4:8], refs[8:12]
    outs = refs[12:16]
    rows_ref, columns_ref, held, sems = refs[16:]
    fetch(where, row_blocks, column_blocks, rows_ref, columns_ref, sems)
    row_top, row_total = merged(row_stats)
    row_top, row_gain = turned(row_top), turned(1.0 / row_total)
    for h in range(GROUP):
        straight = nt(head(rows_ref, 0, h), head(columns_ref, 1, h)) * SCALE
        maps = jnp.exp2(straight - row_top[:, h : h + 1]) * row_gain[:, h : h + 1]
        part = jnp.dot(
            maps.astype(jnp.bfloat16), head(columns_ref, 2, h), preferred_element_type=jnp.float32
        )
        held[:, h * HEAD_DIM : (h + 1) * HEAD_DIM] = part.astype(jnp.bfloat16)
    y, c = where[0], where[3]
    for d in range(4):
        away = lax.rem(lax.bitwise_xor(c, d) - y + 4, 4)
        outs[d][...] = held[pl.ds(pl.multiple_of(away * BLOCK, BLOCK), BLOCK), :]


def relative_kernel(row_residue, column_residue, table, out):
    bins = (
        jnp.clip(column_residue[...] - row_residue[...], -CLIP, CLIP) + CLIP
    )
    for half in range(2):
        own = bins[half * 8 : half * 8 + 8]
        levels = lax.broadcasted_iota(jnp.int32, (72, 8, TILE), 0)
        spread = (own[None] == levels).astype(jnp.float32).reshape(72 * 8, TILE)
        part = jnp.dot(
            table[...], spread.astype(jnp.bfloat16), preferred_element_type=jnp.float32
        )
        part = part.reshape(-1, 8, TILE)
        if half == 0:
            first = part
    out[...] = jnp.concatenate([first, part], axis=1).astype(jnp.bfloat16)


def pair_kernel(*refs):
    tiles = refs[0:8]
    first, first_bias, second, second_bias, relative, out = refs[8:]
    loaded = [ref[...].astype(jnp.float32) for ref in tiles]
    halves = []
    for half in range(2):
        stacked = jnp.concatenate(
            [t[:, half * 8 : half * 8 + 8, :].reshape(GROUP * 8, TILE) for t in loaded], axis=0
        ).astype(jnp.bfloat16)
        hidden = jnp.dot(first[...], stacked, preferred_element_type=jnp.float32)
        hidden = jnp.maximum(hidden + jnp.concatenate([first_bias[...]] * 4, axis=1), 0.0)
        projected = jnp.dot(
            second[...], hidden.astype(jnp.bfloat16), preferred_element_type=jnp.float32
        )
        projected = projected + jnp.concatenate([second_bias[...]] * 4, axis=1)
        halves.append(projected.reshape(-1, 8, TILE))
    out[...] = (
        jnp.concatenate(halves, axis=1) + relative[...].astype(jnp.float32)
    ).astype(jnp.bfloat16)


SMEM = pl.BlockSpec(memory_space=pltpu.SMEM)
ANY = pl.BlockSpec(memory_space=pl.ANY)
VMEM = pl.BlockSpec(memory_space=pltpu.VMEM)


def params(mib):
    return pltpu.CompilerParams(vmem_limit_bytes=mib * MIB)


def blocks_scratch():
    return [
        pltpu.VMEM((TILE, 2 * WIDE), jnp.bfloat16),
        pltpu.VMEM((TILE, 3 * WIDE), jnp.bfloat16),
    ]


def shape(dims, kind=jnp.bfloat16):
    return jax.ShapeDtypeStruct(dims, kind)


def local(queries, keys, values, w_first, b_first, w_second, b_second, rel_table, chain_lengths):
    band, c = lax.axis_index("band"), lax.axis_index("head")
    y, x, z = band // 8, (band // 2) % 4, band % 2
    where = jnp.stack([y, x, z, c]).astype(jnp.int32)
    hid, outs = w_first.shape[1], w_second.shape[1]

    chain_ends = jnp.cumsum(chain_lengths)[:-1]

    def residue_index(positions):
        crossed = jnp.sum((positions[:, None] >= chain_ends[None, :]).astype(jnp.int32), axis=1)
        return positions + GAP * crossed

    row_residue = residue_index(band * HALF + jnp.arange(HALF, dtype=jnp.int32))[:, None]
    column_residue = residue_index(c * TILE + jnp.arange(TILE, dtype=jnp.int32))[None, :]
    eye = jnp.eye(8, dtype=jnp.bfloat16)

    def spread(matrix):
        wide = matrix[:, None, :, None] * eye[None, :, None, :]
        return wide.reshape(matrix.shape[0] * 8, matrix.shape[1] * 8)

    table = spread(jnp.pad(rel_table, ((0, 72 - BINS), (0, 0))).T)
    relative = pl.pallas_call(
        relative_kernel,
        grid=(HALF // ROWS,),
        in_specs=[
            pl.BlockSpec((ROWS, 1), lambda i: (i, 0)),
            pl.BlockSpec((1, TILE), lambda i: (0, 0)),
            pl.BlockSpec((outs * 8, 72 * 8), lambda i: (0, 0)),
        ],
        out_specs=pl.BlockSpec((outs, ROWS, TILE), lambda i: (0, i, 0)),
        out_shape=shape((outs, HALF, TILE)),
        compiler_params=params(40),
        name="relative",
    )(row_residue, column_residue, table)

    near = jnp.concatenate([queries[:, :WIDE], keys[:, :WIDE], values[:, :WIDE]], axis=1)
    far = jnp.concatenate([queries[:, WIDE:], keys[:, WIDE:], values[:, WIDE:]], axis=1)
    same = send(jnp.where(z == 0, near, far), lambda y, x, z, c: (c, x, z, y))
    other = send(jnp.where(z == 0, far, near), lambda y, x, z, c: (c, x, 1 - z, y))
    block = jnp.where(
        z == 0,
        jnp.concatenate([same, other], axis=0),
        jnp.concatenate([other, same], axis=0),
    )

    column_blocks = [block] + [
        send(block, lambda y, x, z, c, d=d: (y, (x + d) % 4, z, c)) for d in (1, 2, 3)
    ]
    narrow = block[:, : 2 * WIDE]
    row_blocks = [narrow] + [send(narrow, lambda y, x, z, c, d=d: (y, x, z, c ^ d)) for d in (1, 2, 3)]
    blocks = row_blocks + column_blocks

    by_row, by_column = pl.pallas_call(
        stats_kernel,
        in_specs=[SMEM] + [ANY] * 8,
        out_specs=[VMEM, VMEM],
        out_shape=[shape((16, TILE), jnp.float32)] * 2,
        scratch_shapes=blocks_scratch() + [pltpu.SemaphoreType.DMA((12,))],
        compiler_params=params(40),
        name="stats",
    )(where, *blocks)
    row_stats = [by_row] + [send(by_row, lambda y, x, z, c, d=d: (y, x, z, c ^ d)) for d in (1, 2, 3)]
    column_stats = [by_column] + [
        send(by_column, lambda y, x, z, c, d=d: (y, (x + d) % 4, z, c)) for d in (1, 2, 3)
    ]

    tiles = pl.pallas_call(
        symmetric_kernel,
        in_specs=[SMEM] + [ANY] * 8 + [VMEM] * 8,
        out_specs=[VMEM] * 8,
        out_shape=[shape((GROUP, HALF, TILE))] * 8,
        scratch_shapes=blocks_scratch() + [pltpu.SemaphoreType.DMA((12,))],
        compiler_params=params(40),
        name="symmetric",
    )(where, *blocks, *row_stats, *column_stats)
    received = [
        tiles[p]
        if p == 0
        else send(tiles[p], lambda y, x, z, c, p=p: ((y + p // 2) % 4, x, z ^ (p % 2), c))
        for p in range(8)
    ]

    partials = pl.pallas_call(
        context_kernel,
        in_specs=[SMEM] + [ANY] * 8 + [VMEM] * 4,
        out_specs=[VMEM] * 4,
        out_shape=[shape((BLOCK, WIDE))] * 4,
        scratch_shapes=blocks_scratch()
        + [pltpu.VMEM((TILE, WIDE), jnp.bfloat16), pltpu.SemaphoreType.DMA((12,))],
        compiler_params=params(40),
        name="context",
    )(where, *blocks, *row_stats)
    summed = partials[0].astype(jnp.float32)
    for d in (1, 2, 3):
        summed = summed + send(partials[d], lambda y, x, z, c, d=d: (y, x, z, c ^ d)).astype(jnp.float32)
    summed = summed.astype(jnp.bfloat16)
    same = send(summed[:HALF], lambda y, x, z, c: (c, x, z, y))
    other = send(summed[HALF:], lambda y, x, z, c: (c, x, 1 - z, y))
    context = jnp.where(
        z == 0,
        jnp.concatenate([same, other], axis=1),
        jnp.concatenate([other, same], axis=1),
    )

    order = jnp.stack([2 * ((y - p // 2) % 4) + z * (1 - p % 2) + (1 - z) * (p % 2) for p in range(8)])
    first = spread(jnp.take(w_first.reshape(8, GROUP, hid), order, axis=0).reshape(8 * GROUP, hid).T)
    second = spread(w_second.T)
    first_bias = jnp.broadcast_to(b_first[:, None, None], (hid, 8, 128)).reshape(hid * 8, 128)
    second_bias = jnp.broadcast_to(b_second[:, None, None], (outs, 8, 128)).reshape(outs * 8, 128)
    pair = pl.pallas_call(
        pair_kernel,
        grid=(HALF // ROWS,),
        in_specs=[pl.BlockSpec((GROUP, ROWS, TILE), lambda i: (0, i, 0))] * 8
        + [
            pl.BlockSpec((hid * 8, 8 * GROUP * 8), lambda i: (0, 0)),
            pl.BlockSpec((hid * 8, 128), lambda i: (0, 0)),
            pl.BlockSpec((outs * 8, hid * 8), lambda i: (0, 0)),
            pl.BlockSpec((outs * 8, 128), lambda i: (0, 0)),
            pl.BlockSpec((outs, ROWS, TILE), lambda i: (0, i, 0)),
        ],
        out_specs=pl.BlockSpec((outs, ROWS, TILE), lambda i: (0, i, 0)),
        out_shape=shape((outs, HALF, TILE)),
        compiler_params=params(40),
        name="pair",
    )(*received, first, first_bias, second, second_bias, relative)
    return (context, pair)


def solution(mesh):
    return jax.shard_map(
        local,
        mesh=mesh,
        in_specs=(
            P("band", "head"),
            P("band", "head"),
            P("band", "head"),
            P(),
            P(),
            P(),
            P(),
            P(),
            P(),
        ),
        out_specs=(P("band", "head"), P(None, "band", "head")),
        check_vma=False,
    )
```

```python
import functools
import itertools
import math

import jax
import jax.numpy as jnp
from jax import lax
from jax.experimental import pallas as pl
from jax.experimental.pallas import tpu as pltpu
from jax.sharding import PartitionSpec as P

HEAD_DIM = 128
CLIP = 32
GAP = 512
BINS = 65
GROUP = 5
WIDE = GROUP * HEAD_DIM
BLOCK = 128
HALF = 64
TILE = 512
ROWS = 16
SCALE = math.log2(math.e) / math.sqrt(HEAD_DIM)
AXES = ("head", "band")
MIB = 1 << 20


def place(y, x, z, c):
    return c * 32 + y * 8 + x * 2 + z


def moves(to):
    return [
        (place(y, x, z, c), place(*to(y, x, z, c)))
        for c, y, x, z in itertools.product(range(4), range(4), range(4), range(2))
    ]


def send(value, to):
    return lax.ppermute(value, AXES, moves(to))


def over_columns_of(values):
    return [send(values[d], lambda y, x, z, c, d=d: (y, (x + d) % 4, z, c)) for d in (1, 2, 3)]


def over_columns(value):
    return over_columns_of([value] * 4)


def over_rows(value):
    return [send(value, lambda y, x, z, c, d=d: (y, x, z, c ^ d)) for d in (1, 2, 3)]


def nt(a, b):
    return lax.dot_general(a, b, (((1,), (1,)), ((), ())), preferred_element_type=jnp.float32)


def fetch(where, row_blocks, column_blocks, rows_ref, columns_ref, sems):
    y, x, z, c = (where[i] for i in range(4))
    copies = []
    for d in range(4):
        away = lax.rem(lax.bitwise_xor(c, d) - y + 4, 4)
        for part in range(2):
            start = pl.multiple_of(away * BLOCK + lax.bitwise_xor(z, part) * HALF, HALF)
            copies.append(
                pltpu.make_async_copy(
                    row_blocks[d].at[pl.ds(part * HALF, HALF)],
                    rows_ref.at[pl.ds(start, HALF)],
                    sems.at[2 * d + part],
                )
            )
        start = pl.multiple_of(lax.rem(x - d + 4, 4) * BLOCK, BLOCK)
        copies.append(
            pltpu.make_async_copy(
                column_blocks[d], columns_ref.at[pl.ds(start, BLOCK)], sems.at[8 + d]
            )
        )
    for copy in copies:
        copy.start()
    for copy in copies:
        copy.wait()


def head(ref, part, h):
    return ref[:, part * WIDE + h * HEAD_DIM : part * WIDE + (h + 1) * HEAD_DIM]


def stats_kernel(where, *refs):
    by_row, by_column, row_lifted, column_lifted = refs[8:12]
    partials, (rows_ref, columns_ref, held, sems) = refs[12:16], refs[16:]
    fetch(where, refs[0:4], refs[4:8], rows_ref, columns_ref, sems)
    by_column[...] = jnp.zeros_like(by_column)
    lane = lax.broadcasted_iota(jnp.int32, (TILE, 128), 1)
    kept = jnp.zeros((TILE, 128), jnp.float32)
    for h in range(GROUP):
        scores = nt(head(rows_ref, 0, h), head(columns_ref, 1, h)) * SCALE
        top = jnp.max(scores, axis=1, keepdims=True)
        lifted = jnp.exp2(scores - top)
        row_lifted[h] = lifted.astype(jnp.bfloat16)
        kept = jnp.where(lane == h, top, kept)
        kept = jnp.where(lane == 8 + h, jnp.sum(lifted, axis=1, keepdims=True), kept)
        scores = nt(head(rows_ref, 1, h), head(columns_ref, 0, h)) * SCALE
        top = jnp.max(scores, axis=0, keepdims=True)
        lifted = jnp.exp2(scores - top)
        by_column[h : h + 1, :] = top
        by_column[8 + h : 9 + h, :] = jnp.sum(lifted, axis=0, keepdims=True)
        lifted = lifted.astype(jnp.bfloat16)
        column_lifted[h] = lifted
        part = lax.dot_general(
            head(rows_ref, 2, h),
            lifted,
            (((0,), (0,)), ((), ())),
            preferred_element_type=jnp.float32,
        )
        held[h * HEAD_DIM : (h + 1) * HEAD_DIM, :] = part.astype(jnp.bfloat16)
    by_row[...] = jnp.transpose(kept)[0:16]
    for d in range(4):
        owner = lax.rem(where[1] + d, 4)
        partials[d][...] = held[:, pl.ds(pl.multiple_of(owner * BLOCK, BLOCK), BLOCK)]


def factors(refs):
    top = functools.reduce(jnp.maximum, [ref[0:8, :] for ref in refs])
    total = sum(ref[8:16, :] * jnp.exp2(ref[0:8, :] - top) for ref in refs)
    return jnp.exp2(refs[0][0:8, :] - top) / total


def turned(value):
    return jnp.transpose(jnp.concatenate([value] * 16, axis=0))


def symmetric_kernel(where, *refs):
    row_stats, column_stats = refs[0:4], refs[4:8]
    row_lifted, column_lifted, out = refs[8:]
    by_row = turned(factors(row_stats) * 1024.0)
    by_column = factors(column_stats) * 1024.0
    y, z = where[0], where[2]
    for p in range(8):
        owner = lax.rem(y + p // 2, 4) * 2 + lax.bitwise_xor(z, p % 2)
        here = slice(p * HALF, (p + 1) * HALF)
        for h in range(GROUP):
            out[owner, h] = (
                row_lifted[h, here].astype(jnp.float32) * by_row[here, h : h + 1]
                + column_lifted[h, here].astype(jnp.float32) * by_column[h : h + 1, :]
            ).astype(jnp.bfloat16)


def context_kernel(where, *refs):
    column_stats, partials = refs[0:4], refs[4:8]
    same, other, held = refs[8:]
    here = pl.ds(pl.multiple_of(where[1] * BLOCK, BLOCK), BLOCK)
    tops = [ref[0:8, here] for ref in column_stats]
    top = functools.reduce(jnp.maximum, tops)
    scales = [jnp.exp2(own - top) for own in tops]
    total = sum(ref[8:16, here] * scale for ref, scale in zip(column_stats, scales))
    scales = [scale / total for scale in scales]
    for h in range(GROUP):
        at = slice(h * HEAD_DIM, (h + 1) * HEAD_DIM)
        summed = sum(
            ref[at, :].astype(jnp.float32) * scale[h : h + 1, :]
            for ref, scale in zip(partials, scales)
        )
        held[:, at] = jnp.transpose(summed).astype(jnp.bfloat16)
    z = where[2]
    same[...] = held[pl.ds(pl.multiple_of(z * HALF, HALF), HALF), :]
    other[...] = held[pl.ds(pl.multiple_of((1 - z) * HALF, HALF), HALF), :]


def one_hot(indices, axis):
    return (indices == lax.broadcasted_iota(jnp.int32, indices.shape, axis)).astype(jnp.float32)


def expanded(matrix, row_of, row_lane, column_of, column_lane, left, right):
    k, m = matrix.shape
    one = one_hot(row_of(lax.broadcasted_iota(jnp.int32, (left, m), 0)), 1)
    tall = nt(one.astype(jnp.bfloat16), matrix).astype(jnp.bfloat16)
    one = one_hot(column_of(lax.broadcasted_iota(jnp.int32, (k, right), 1)), 0)
    wide = jnp.dot(tall, one.astype(jnp.bfloat16), preferred_element_type=jnp.float32)
    at_row = row_lane(lax.broadcasted_iota(jnp.int32, (left, right), 0))
    at_column = column_lane(lax.broadcasted_iota(jnp.int32, (left, right), 1))
    return jnp.where(at_row == at_column, wide, 0.0).astype(jnp.bfloat16)


def repeated(bias, row_of, left):
    one = one_hot(row_of(lax.broadcasted_iota(jnp.int32, (left, bias.shape[0]), 0)), 1)
    wide = jnp.broadcast_to(bias[...], (bias.shape[0], 128))
    return jnp.dot(one, wide, precision=lax.Precision.HIGHEST, preferred_element_type=jnp.float32)


def spread_kernel(
    first, first_bias, second, second_bias, table, first_out, first_bias_out, second_out,
    second_bias_out, table_out,
):
    by_eight, eight = lambda r: r // 8, lambda r: r % 8
    by_four, four = lambda r: r // 4, lambda r: r % 4
    hid, outs = first.shape[1], second.shape[1]
    channel = lambda r: r % (hid * 4) // 4
    first_out[...] = expanded(
        first[...],
        channel,
        lambda r: r // (hid * 4) * 4 + r % 4,
        by_eight,
        eight,
        hid * 8,
        first_out.shape[1],
    )
    first_bias_out[...] = repeated(first_bias, channel, hid * 8)
    second_out[: outs * 4] = expanded(second[...], by_four, four, by_four, four, outs * 4, hid * 4)
    second_out[outs * 4 :] = expanded(
        second[...], lambda r: r // 4 + 1 - r // 4 % 2 * 2, four, by_four, four, outs * 4, hid * 4
    )
    second_bias_out[...] = repeated(second_bias, by_eight, outs * 8)
    table_out[...] = expanded(
        table[...], by_eight, eight, by_eight, eight, outs * 8, table_out.shape[1]
    )


def relative_kernel(where, lengths, table, out):
    ends = [lengths[0], lengths[0] + lengths[1], lengths[0] + lengths[1] + lengths[2]]

    def residue(positions):
        return positions + GAP * sum((positions >= end).astype(jnp.int32) for end in ends)

    band = where[0] * 8 + where[1] * 2 + where[2]
    first_row = band * HALF + pl.program_id(0) * ROWS
    levels = lax.broadcasted_iota(jnp.int32, (72, 8, TILE), 0)
    columns = residue(where[3] * TILE + lax.broadcasted_iota(jnp.int32, (8, TILE), 1))
    halves = []
    for half in range(ROWS // 8):
        rows = residue(first_row + half * 8 + lax.broadcasted_iota(jnp.int32, (8, TILE), 0))
        bins = jnp.clip(columns - rows, -CLIP, CLIP) + CLIP
        spread = (bins[None] == levels).astype(jnp.float32).reshape(72 * 8, TILE)
        part = jnp.dot(
            table[...], spread.astype(jnp.bfloat16), preferred_element_type=jnp.float32
        )
        halves.append(part.reshape(-1, 8, TILE))
    out[...] = jnp.concatenate(halves, axis=1).astype(jnp.bfloat16)


def pair_kernel(
    where, tiles, first, first_bias, second, second_bias, relative, same, other, out, context
):
    z = where[2]

    @pl.when(pl.program_id(0) == 0)
    def _():
        context[:, pl.ds(pl.multiple_of(z * WIDE, WIDE), WIDE)] = same[...]
        context[:, pl.ds(pl.multiple_of((1 - z) * WIDE, WIDE), WIDE)] = other[...]

    loaded = tiles[...].astype(jnp.float32)
    outs, hid = second.shape[0] // 8, first.shape[0] // 8
    upper = lax.broadcasted_iota(jnp.int32, (outs // 2, 8, TILE), 1) < 4
    halves = []
    for half in range(ROWS // 8):
        stacked = loaded[:, half * 8 : half * 8 + 8, :].reshape(-1, TILE).astype(jnp.bfloat16)
        hidden = jnp.dot(first[...], stacked, preferred_element_type=jnp.float32)
        hidden = jnp.maximum(hidden + jnp.concatenate([first_bias[...]] * 4, axis=1), 0.0)
        hidden = hidden.astype(jnp.bfloat16)
        low, high = (
            jnp.dot(
                second[part * outs * 4 : (part + 1) * outs * 4],
                hidden[part * hid * 4 : (part + 1) * hid * 4],
                preferred_element_type=jnp.float32,
            ).reshape(outs // 2, 8, TILE)
            for part in range(2)
        )
        even = jnp.where(upper, low, high)
        odd = pltpu.roll(jnp.where(upper, high, low), 4, 1)
        projected = jnp.stack([even, odd], axis=1).reshape(outs, 8, TILE)
        halves.append(
            projected + jnp.concatenate([second_bias[...]] * 4, axis=1).reshape(outs, 8, TILE)
        )
    out[...] = (
        jnp.concatenate(halves, axis=1) + relative[...].astype(jnp.float32)
    ).astype(jnp.bfloat16)


SMEM = pl.BlockSpec(memory_space=pltpu.SMEM)
ANY = pl.BlockSpec(memory_space=pl.ANY)
VMEM = pl.BlockSpec(memory_space=pltpu.VMEM)


def params(mib):
    return pltpu.CompilerParams(vmem_limit_bytes=mib * MIB)


def in_hbm(value):
    return pltpu.with_memory_space_constraint(value, pltpu.HBM)


def vmem(rows, columns):
    return pltpu.VMEM((rows, columns), jnp.bfloat16)


def shape(dims, kind=jnp.bfloat16):
    return jax.ShapeDtypeStruct(dims, kind)


def local(queries, keys, values, w_first, b_first, w_second, b_second, rel_table, chain_lengths):
    band, c = lax.axis_index("band"), lax.axis_index("head")
    y, x, z = band // 8, (band // 2) % 4, band % 2
    where = jnp.stack([y, x, z, c]).astype(jnp.int32)
    hid, outs = w_first.shape[1], w_second.shape[1]

    first, first_bias, second, second_bias, table = pl.pallas_call(
        spread_kernel,
        in_specs=[VMEM] * 5,
        out_specs=[VMEM] * 5,
        out_shape=[
            pltpu.HBM((hid * 8, 8 * GROUP * 8), jnp.bfloat16),
            pltpu.HBM((hid * 8, 128), jnp.float32),
            pltpu.HBM((outs * 8, hid * 4), jnp.bfloat16),
            pltpu.HBM((outs * 8, 128), jnp.float32),
            shape((outs * 8, 72 * 8)),
        ],
        compiler_params=params(6),
        name="spread",
    )(w_first, b_first[:, None], w_second, b_second[:, None], jnp.pad(rel_table, ((0, 72 - BINS), (0, 0))))

    near = jnp.concatenate([queries[:, :WIDE], keys[:, :WIDE], values[:, :WIDE]], axis=1)
    far = jnp.concatenate([queries[:, WIDE:], keys[:, WIDE:], values[:, WIDE:]], axis=1)
    same = send(jnp.where(z == 0, near, far), lambda y, x, z, c: (c, x, z, y))
    other = send(jnp.where(z == 0, far, near), lambda y, x, z, c: (c, x, 1 - z, y))
    block = jnp.where(
        z == 0,
        jnp.concatenate([same, other], axis=0),
        jnp.concatenate([other, same], axis=0),
    )

    block, first, first_bias, second, second_bias, table = lax.optimization_barrier(
        (block, first, first_bias, second, second_bias, table)
    )
    narrow = block[:, : 2 * WIDE]

    column_blocks = [narrow] + over_columns(narrow)
    row_blocks = [block] + over_rows(block)

    relative = pl.pallas_call(
        relative_kernel,
        grid=(HALF // ROWS,),
        in_specs=[SMEM, SMEM, pl.BlockSpec((outs * 8, 72 * 8), lambda i: (0, 0))],
        out_specs=pl.BlockSpec((outs, ROWS, TILE), lambda i: (0, i, 0)),
        out_shape=pltpu.HBM((outs, HALF, TILE), jnp.bfloat16),
        compiler_params=params(8),
        name="relative",
    )(where, chain_lengths, table)
    where, relative = lax.optimization_barrier((where, relative))

    by_row, by_column, row_lifted, column_lifted, *partials = pl.pallas_call(
        stats_kernel,
        in_specs=[SMEM] + [ANY] * 8,
        out_specs=[VMEM] * 8,
        out_shape=[shape((16, TILE), jnp.float32)] * 2
        + [shape((GROUP, TILE, TILE))] * 2
        + [pltpu.HBM((WIDE, BLOCK), jnp.bfloat16)]
        + [shape((WIDE, BLOCK))] * 3,
        scratch_shapes=[
            vmem(TILE, 3 * WIDE),
            vmem(TILE, 2 * WIDE),
            vmem(WIDE, TILE),
            pltpu.SemaphoreType.DMA((12,)),
        ],
        compiler_params=params(12),
        name="stats",
    )(where, *row_blocks, *column_blocks)
    row_stats = [by_row] + over_rows(by_row)
    column_stats = [by_column] + over_columns(by_column)

    tiles = pl.pallas_call(
        symmetric_kernel,
        in_specs=[SMEM] + [VMEM] * 10,
        out_specs=VMEM,
        out_shape=shape((8, GROUP, HALF, TILE)),
        compiler_params=params(8),
        name="symmetric",
    )(where, *row_stats, *column_stats, row_lifted, column_lifted)
    where, tiles = lax.optimization_barrier((where, tiles))
    groups = [[y * 8 + x * 2 + z for y in range(4) for z in range(2)] for x in range(4)]
    received = lax.all_to_all(
        tiles, "band", split_axis=0, concat_axis=0, axis_index_groups=groups, tiled=True
    ).reshape(8 * GROUP, HALF, TILE)

    same, other = pl.pallas_call(
        context_kernel,
        in_specs=[SMEM] + [VMEM] * 8,
        out_specs=[VMEM] * 2,
        out_shape=[shape((HALF, WIDE))] * 2,
        scratch_shapes=[vmem(BLOCK, WIDE)],
        compiler_params=params(4),
        name="context",
    )(where, *column_stats, in_hbm(partials[0]), *over_columns_of(partials))
    same = send(same, lambda y, x, z, c: (c, x, z, y))
    other = send(other, lambda y, x, z, c: (c, x, 1 - z, y))

    pair, context = pl.pallas_call(
        pair_kernel,
        grid=(HALF // ROWS,),
        in_specs=[
            SMEM,
            pl.BlockSpec((8 * GROUP, ROWS, TILE), lambda i: (0, i, 0)),
            pl.BlockSpec((hid * 8, 8 * GROUP * 8), lambda i: (0, 0)),
            pl.BlockSpec((hid * 8, 128), lambda i: (0, 0)),
            pl.BlockSpec((outs * 8, hid * 4), lambda i: (0, 0)),
            pl.BlockSpec((outs * 8, 128), lambda i: (0, 0)),
            pl.BlockSpec((outs, ROWS, TILE), lambda i: (0, i, 0)),
            pl.BlockSpec((HALF, WIDE), lambda i: (0, 0)),
            pl.BlockSpec((HALF, WIDE), lambda i: (0, 0)),
        ],
        out_specs=[
            pl.BlockSpec((outs, ROWS, TILE), lambda i: (0, i, 0)),
            pl.BlockSpec((HALF, 2 * WIDE), lambda i: (0, 0)),
        ],
        out_shape=[shape((outs, HALF, TILE)), shape((HALF, 2 * WIDE))],
        compiler_params=params(13),
        name="pair",
    )(
        where,
        received,
        *(in_hbm(a) for a in (first, first_bias, second, second_bias, relative, same, other)),
    )
    return (context, pair)


def solution(mesh):
    return jax.shard_map(
        local,
        mesh=mesh,
        in_specs=(
            P("band", "head"),
            P("band", "head"),
            P("band", "head"),
            P(),
            P(),
            P(),
            P(),
            P(),
            P(),
        ),
        out_specs=(P("band", "head"), P(None, "band", "head")),
        check_vma=False,
    )
```

```python
import functools
import itertools
import math

import jax
import jax.numpy as jnp
from jax import lax
from jax.experimental import pallas as pl
from jax.experimental.pallas import tpu as pltpu
from jax.sharding import PartitionSpec as P

HEAD_DIM = 128
CLIP = 32
GAP = 512
BINS = 65
GROUP = 5
WIDE = GROUP * HEAD_DIM
BLOCK = 128
HALF = 64
TILE = 512
ROWS = 16
ONES = 16
SCALE = math.log2(math.e) / math.sqrt(HEAD_DIM)
AXES = ("head", "band")
MIB = 1 << 20


def place(y, x, z, c):
    return c * 32 + y * 8 + x * 2 + z


def moves(to):
    return [
        (place(y, x, z, c), place(*to(y, x, z, c)))
        for c, y, x, z in itertools.product(range(4), range(4), range(4), range(2))
    ]


def send(value, to):
    return lax.ppermute(value, AXES, moves(to))


def over_columns_of(values):
    return [send(values[d], lambda y, x, z, c, d=d: (y, (x + d) % 4, z, c)) for d in (1, 2, 3)]


def over_columns(value):
    return over_columns_of([value] * 4)


def over_rows(value):
    return [send(value, lambda y, x, z, c, d=d: (y, x, z, c ^ d)) for d in (1, 2, 3)]


def nt(a, b):
    return lax.dot_general(a, b, (((1,), (1,)), ((), ())), preferred_element_type=jnp.float32)


def fetch(where, row_blocks, row_parts, column_blocks, column_part, sems):
    y, x, z, c = (where[i] for i in range(4))
    copies = []
    for d in range(4):
        away = lax.rem(lax.bitwise_xor(c, d) - y + 4, 4)
        for part in range(2):
            start = pl.multiple_of(away * BLOCK + lax.bitwise_xor(z, part) * HALF, HALF)
            for ref, at in row_parts:
                copies.append(
                    pltpu.make_async_copy(
                        row_blocks[d].at[pl.ds(part * HALF, HALF), pl.ds(at * WIDE, WIDE)],
                        ref.at[pl.ds(start, HALF)],
                        sems.at[len(copies)],
                    )
                )
    ref, at = column_part
    for block, d, skip in zip(column_blocks, (0, 1, 3, 2, 2), (0, 0, 0, 0, HALF)):
        rows = block.shape[0]
        start = pl.multiple_of(lax.rem(x - d + 4, 4) * BLOCK + skip, HALF)
        copies.append(
            pltpu.make_async_copy(
                block.at[:, pl.ds(at * WIDE, WIDE)],
                ref.at[pl.ds(start, rows)],
                sems.at[len(copies)],
            )
        )
    for copy in copies:
        copy.start()
    for copy in copies:
        copy.wait()


def head(ref, h):
    return ref[:, h * HEAD_DIM : (h + 1) * HEAD_DIM]


def row_kernel(where, *refs):
    by_row, lifted_out, queries, keys, sems = refs[9:]
    fetch(where, refs[0:4], [(queries, 0)], refs[4:9], (keys, 1), sems)
    lane = lax.broadcasted_iota(jnp.int32, (TILE, 128), 1)
    kept = jnp.zeros((TILE, 128), jnp.float32)
    for h in range(GROUP):
        scores = nt(head(queries, h), head(keys, h)) * SCALE
        top = jnp.max(scores, axis=1, keepdims=True)
        lifted = jnp.exp2(scores - top)
        lifted_out[h] = lifted.astype(jnp.bfloat16)
        kept = jnp.where(lane == h, top, kept)
        kept = jnp.where(lane == 8 + h, jnp.sum(lifted, axis=1, keepdims=True), kept)
    by_row[...] = jnp.transpose(kept)[0:16]


def column_kernel(where, *refs):
    by_column, lifted_out = refs[9:11]
    partials, (keys, values, queries, held, sems) = refs[11:15], refs[15:]
    fetch(where, refs[0:4], [(keys, 1), (values, 2)], refs[4:9], (queries, 0), sems)
    by_column[...] = jnp.zeros_like(by_column)
    for h in range(GROUP):
        scores = nt(head(keys, h), head(queries, h)) * SCALE
        top = jnp.max(scores, axis=0, keepdims=True)
        lifted = jnp.exp2(scores - top)
        by_column[h : h + 1, :] = top
        by_column[8 + h : 9 + h, :] = jnp.sum(lifted, axis=0, keepdims=True)
        lifted = lifted.astype(jnp.bfloat16)
        lifted_out[h] = lifted
        part = lax.dot_general(
            head(values, h), lifted, (((0,), (0,)), ((), ())), preferred_element_type=jnp.float32
        )
        held[h * HEAD_DIM : (h + 1) * HEAD_DIM, :] = part.astype(jnp.bfloat16)
    for d in range(4):
        owner = lax.rem(where[1] + d, 4)
        partials[d][...] = held[:, pl.ds(pl.multiple_of(owner * BLOCK, BLOCK), BLOCK)]


def factors(refs):
    top = functools.reduce(jnp.maximum, [ref[0:8, :] for ref in refs])
    total = sum(ref[8:16, :] * jnp.exp2(ref[0:8, :] - top) for ref in refs)
    return jnp.exp2(refs[0][0:8, :] - top) / total


def turned(value):
    return jnp.transpose(jnp.concatenate([value] * 16, axis=0))


def symmetric_kernel(where, *refs):
    row_stats, column_stats = refs[0:4], refs[4:8]
    row_lifted, column_lifted, out, held, sems = refs[8:]
    by_row = turned(factors(row_stats) * 1024.0)
    by_column = factors(column_stats) * 1024.0
    y, z = where[0], where[2]
    copies = []
    for p in range(8):
        owner = lax.rem(y + p // 2, 4) * 2 + lax.bitwise_xor(z, p % 2)
        here = slice(p * HALF, (p + 1) * HALF)
        for h in range(GROUP):
            held[p, h] = (
                row_lifted[h, here].astype(jnp.float32) * by_row[here, h : h + 1]
                + column_lifted[h, here].astype(jnp.float32) * by_column[h : h + 1, :]
            ).astype(jnp.bfloat16)
        copies.append(pltpu.make_async_copy(held.at[p], out.at[owner], sems.at[p]))
        copies[p].start()
    for copy in copies:
        copy.wait()


def context_kernel(where, *refs):
    column_stats, partials = refs[0:4], refs[4:8]
    same, other, held = refs[8:]
    here = pl.ds(pl.multiple_of(where[1] * BLOCK, BLOCK), BLOCK)
    tops = [ref[0:8, here] for ref in column_stats]
    top = functools.reduce(jnp.maximum, tops)
    scales = [jnp.exp2(own - top) for own in tops]
    total = sum(ref[8:16, here] * scale for ref, scale in zip(column_stats, scales))
    scales = [scale / total for scale in scales]
    for h in range(GROUP):
        at = slice(h * HEAD_DIM, (h + 1) * HEAD_DIM)
        summed = sum(
            ref[at, :].astype(jnp.float32) * scale[h : h + 1, :]
            for ref, scale in zip(partials, scales)
        )
        held[:, at] = jnp.transpose(summed).astype(jnp.bfloat16)
    z = where[2]
    same[...] = held[pl.ds(pl.multiple_of(z * HALF, HALF), HALF), :]
    other[...] = held[pl.ds(pl.multiple_of((1 - z) * HALF, HALF), HALF), :]


def one_hot(indices, axis):
    return (indices == lax.broadcasted_iota(jnp.int32, indices.shape, axis)).astype(jnp.float32)


def expanded(matrix, row_of, row_lane, column_of, column_lane, left, right):
    k, m = matrix.shape
    one = one_hot(row_of(lax.broadcasted_iota(jnp.int32, (left, m), 0)), 1)
    tall = nt(one.astype(jnp.bfloat16), matrix).astype(jnp.bfloat16)
    one = one_hot(column_of(lax.broadcasted_iota(jnp.int32, (k, right), 1)), 0)
    wide = jnp.dot(tall, one.astype(jnp.bfloat16), preferred_element_type=jnp.float32)
    at_row = row_lane(lax.broadcasted_iota(jnp.int32, (left, right), 0))
    at_column = column_lane(lax.broadcasted_iota(jnp.int32, (left, right), 1))
    return jnp.where(at_row == at_column, wide, 0.0).astype(jnp.bfloat16)


def repeated(bias, row_of, left):
    one = one_hot(row_of(lax.broadcasted_iota(jnp.int32, (left, bias.shape[0]), 0)), 1)
    wide = jnp.broadcast_to(bias[...], (bias.shape[0], 128))
    return jnp.dot(one, wide, precision=lax.Precision.HIGHEST, preferred_element_type=jnp.float32)


def spread_kernel(
    first, first_bias, second, second_bias, table, first_out, second_out, second_bias_out, table_out
):
    by_eight, eight = lambda r: r // 8, lambda r: r % 8
    by_four, four = lambda r: r // 4, lambda r: r % 4
    hid, outs = first.shape[1], second.shape[1]
    channel = lambda r: r % (hid * 4) // 4
    width = first.shape[0] * 8
    first_out[:, :width] = expanded(
        first[...],
        channel,
        lambda r: r // (hid * 4) * 4 + r % 4,
        by_eight,
        eight,
        hid * 8,
        width,
    )
    rest, parts = repeated(first_bias, channel, hid * 8)[:, :ONES], []
    for _ in range(3):
        parts.append(rest.astype(jnp.bfloat16).astype(jnp.float32))
        rest = rest - parts[-1]
    lane = lax.broadcasted_iota(jnp.int32, (hid * 8, ONES), 1)
    first_out[:, width:] = sum(
        jnp.where(lane == i, part, 0.0) for i, part in enumerate(parts)
    ).astype(jnp.bfloat16)
    second_out[: outs * 4] = expanded(second[...], by_four, four, by_four, four, outs * 4, hid * 4)
    second_out[outs * 4 :] = expanded(
        second[...], lambda r: r // 4 + 1 - r // 4 % 2 * 2, four, by_four, four, outs * 4, hid * 4
    )
    second_bias_out[...] = repeated(second_bias, by_eight, outs * 8)
    table_out[...] = expanded(
        table[...], by_eight, eight, by_eight, eight, outs * 8, table_out.shape[1]
    )


def relative_kernel(where, lengths, table, out):
    ends = [lengths[0], lengths[0] + lengths[1], lengths[0] + lengths[1] + lengths[2]]

    def residue(positions):
        return positions + GAP * sum((positions >= end).astype(jnp.int32) for end in ends)

    band = where[0] * 8 + where[1] * 2 + where[2]
    first_row = band * HALF + pl.program_id(0) * ROWS
    levels = lax.broadcasted_iota(jnp.int32, (72, 8, TILE), 0)
    columns = residue(where[3] * TILE + lax.broadcasted_iota(jnp.int32, (8, TILE), 1))
    halves = []
    for half in range(ROWS // 8):
        rows = residue(first_row + half * 8 + lax.broadcasted_iota(jnp.int32, (8, TILE), 0))
        bins = jnp.clip(columns - rows, -CLIP, CLIP) + CLIP
        spread = (bins[None] == levels).astype(jnp.float32).reshape(72 * 8, TILE)
        part = jnp.dot(
            table[...], spread.astype(jnp.bfloat16), preferred_element_type=jnp.float32
        )
        halves.append(part.reshape(-1, 8, TILE))
    out[...] = jnp.concatenate(halves, axis=1).astype(jnp.bfloat16)


def pair_kernel(where, tiles, first, second, second_bias, relative, same, other, out, context):
    z = where[2]

    @pl.when(pl.program_id(0) == 0)
    def _():
        context[:, pl.ds(pl.multiple_of(z * WIDE, WIDE), WIDE)] = same[...]
        context[:, pl.ds(pl.multiple_of((1 - z) * WIDE, WIDE), WIDE)] = other[...]

    loaded = tiles[...].astype(jnp.float32)
    outs, hid = second.shape[0] // 8, first.shape[0] // 8
    upper = lax.broadcasted_iota(jnp.int32, (outs // 2, 8, TILE), 1) < 4
    ones = jnp.ones((ONES, TILE), jnp.bfloat16)
    halves = []
    for half in range(ROWS // 8):
        stacked = loaded[:, half * 8 : half * 8 + 8, :].reshape(-1, TILE).astype(jnp.bfloat16)
        stacked = jnp.concatenate([stacked, ones], axis=0)
        hidden = jnp.dot(first[...], stacked, preferred_element_type=jnp.float32)
        hidden = jnp.maximum(hidden, 0.0).astype(jnp.bfloat16)
        low, high = (
            jnp.dot(
                second[part * outs * 4 : (part + 1) * outs * 4],
                hidden[part * hid * 4 : (part + 1) * hid * 4],
                preferred_element_type=jnp.float32,
            ).reshape(outs // 2, 8, TILE)
            for part in range(2)
        )
        even = jnp.where(upper, low, high)
        odd = pltpu.roll(jnp.where(upper, high, low), 4, 1)
        projected = jnp.stack([even, odd], axis=1).reshape(outs, 8, TILE)
        halves.append(
            projected + jnp.concatenate([second_bias[...]] * 4, axis=1).reshape(outs, 8, TILE)
        )
    out[...] = (
        jnp.concatenate(halves, axis=1) + relative[...].astype(jnp.float32)
    ).astype(jnp.bfloat16)


SMEM = pl.BlockSpec(memory_space=pltpu.SMEM)
ANY = pl.BlockSpec(memory_space=pl.ANY)
HBM = pl.BlockSpec(memory_space=pltpu.HBM)
VMEM = pl.BlockSpec(memory_space=pltpu.VMEM)


def params(mib):
    return pltpu.CompilerParams(vmem_limit_bytes=mib * MIB)


def cost(flops, bytes_accessed, exponentials=0):
    return pl.CostEstimate(
        flops=int(flops), bytes_accessed=int(bytes_accessed), transcendentals=int(exponentials)
    )


def in_hbm(value):
    return pltpu.with_memory_space_constraint(value, pltpu.HBM)


def vmem(rows, columns):
    return pltpu.VMEM((rows, columns), jnp.bfloat16)


def shape(dims, kind=jnp.bfloat16):
    return jax.ShapeDtypeStruct(dims, kind)


def local(queries, keys, values, w_first, b_first, w_second, b_second, rel_table, chain_lengths):
    band, c = lax.axis_index("band"), lax.axis_index("head")
    y, x, z = band // 8, (band // 2) % 4, band % 2
    where = jnp.stack([y, x, z, c]).astype(jnp.int32)
    hid, outs = w_first.shape[1], w_second.shape[1]

    first, second, second_bias, table = pl.pallas_call(
        spread_kernel,
        in_specs=[VMEM] * 5,
        out_specs=[VMEM] * 4,
        out_shape=[
            pltpu.HBM((hid * 8, 8 * GROUP * 8 + ONES), jnp.bfloat16),
            pltpu.HBM((outs * 8, hid * 4), jnp.bfloat16),
            pltpu.HBM((outs * 8, 128), jnp.float32),
            shape((outs * 8, 72 * 8)),
        ],
        compiler_params=params(6),
        cost_estimate=cost(4e8, 6e6),
        name="spread",
    )(
        w_first,
        b_first[:, None],
        w_second,
        b_second[:, None],
        jnp.pad(rel_table, ((0, 72 - BINS), (0, 0))),
    )

    near = jnp.concatenate([queries[:, :WIDE], keys[:, :WIDE], values[:, :WIDE]], axis=1)
    far = jnp.concatenate([queries[:, WIDE:], keys[:, WIDE:], values[:, WIDE:]], axis=1)
    same = send(jnp.where(z == 0, near, far), lambda y, x, z, c: (c, x, z, y))
    other = send(jnp.where(z == 0, far, near), lambda y, x, z, c: (c, x, 1 - z, y))
    block = jnp.where(
        z == 0,
        jnp.concatenate([same, other], axis=0),
        jnp.concatenate([other, same], axis=0),
    )

    block, first, second, second_bias, table = lax.optimization_barrier(
        (block, first, second, second_bias, table)
    )
    narrow = block[:, : 2 * WIDE]

    across = send(block, lambda y, x, z, c: (y, x, z, c ^ 2))
    right = send(narrow, lambda y, x, z, c: (y, (x + 1) % 4, z, c))
    left = send(narrow, lambda y, x, z, c: (y, (x + 3) % 4, z, c))
    relative = pl.pallas_call(
        relative_kernel,
        grid=(HALF // ROWS,),
        in_specs=[SMEM, SMEM, pl.BlockSpec((outs * 8, 72 * 8), lambda i: (0, 0))],
        out_specs=pl.BlockSpec((outs, ROWS, TILE), lambda i: (0, i, 0)),
        out_shape=pltpu.HBM((outs, HALF, TILE), jnp.bfloat16),
        compiler_params=params(8),
        cost_estimate=cost(2.4e9, 6e6),
        name="relative",
    )(where, chain_lengths, table)
    where, relative, left, right = lax.optimization_barrier((where, relative, left, right))
    column_blocks = [
        narrow,
        right,
        left,
        send(right[:HALF], lambda y, x, z, c: (y, (x + 1) % 4, z, c)),
        send(left[HALF:], lambda y, x, z, c: (y, (x + 3) % 4, z, c)),
    ]
    relative, across, block = lax.optimization_barrier((relative, across, block))
    beside = send(block, lambda y, x, z, c: (y, x, z, c ^ 1))
    row_blocks = [block, beside, across, send(across, lambda y, x, z, c: (y, x, z, c ^ 1))]

    by_row, row_lifted = pl.pallas_call(
        row_kernel,
        in_specs=[SMEM] + [ANY] * 9,
        out_specs=[VMEM] * 2,
        out_shape=[shape((16, TILE), jnp.float32), shape((GROUP, TILE, TILE))],
        scratch_shapes=[vmem(TILE, WIDE)] * 2 + [pltpu.SemaphoreType.DMA((13,))],
        compiler_params=params(12),
        cost_estimate=cost(4e8, 8e6, 1.4e6),
        name="rows",
    )(where, *row_blocks, *column_blocks)
    by_column, column_lifted, *partials = pl.pallas_call(
        column_kernel,
        in_specs=[SMEM] + [ANY] * 9,
        out_specs=[VMEM] * 6,
        out_shape=[shape((16, TILE), jnp.float32), shape((GROUP, TILE, TILE))]
        + [shape((WIDE, BLOCK))] * 4,
        scratch_shapes=[vmem(TILE, WIDE)] * 3
        + [vmem(WIDE, TILE), pltpu.SemaphoreType.DMA((21,))],
        compiler_params=params(12),
        cost_estimate=cost(7e8, 9e6, 1.4e6),
        name="columns",
    )(where, *row_blocks, *column_blocks)
    row_stats = [by_row] + over_rows(by_row)
    column_stats = [by_column] + over_columns(by_column)

    tiles = pl.pallas_call(
        symmetric_kernel,
        in_specs=[SMEM] + [VMEM] * 10,
        out_specs=HBM,
        out_shape=shape((8, GROUP, HALF, TILE)),
        scratch_shapes=[
            pltpu.VMEM((8, GROUP, HALF, TILE), jnp.bfloat16),
            pltpu.SemaphoreType.DMA((8,)),
        ],
        compiler_params=params(8),
        cost_estimate=cost(1e7, 9e6),
        name="symmetric",
    )(where, *row_stats, *column_stats, row_lifted, column_lifted)
    where, tiles = lax.optimization_barrier((where, tiles))
    groups = [[y * 8 + x * 2 + z for y in range(4) for z in range(2)] for x in range(4)]
    received = lax.all_to_all(
        tiles, "band", split_axis=0, concat_axis=0, axis_index_groups=groups, tiled=True
    ).reshape(8 * GROUP, HALF, TILE)

    same, other = pl.pallas_call(
        context_kernel,
        in_specs=[SMEM] + [VMEM] * 8,
        out_specs=[VMEM] * 2,
        out_shape=[shape((HALF, WIDE))] * 2,
        scratch_shapes=[vmem(BLOCK, WIDE)],
        compiler_params=params(4),
        cost_estimate=cost(1e6, 2e6),
        name="context",
    )(where, *column_stats, partials[0], *over_columns_of(partials))
    same = send(same, lambda y, x, z, c: (c, x, z, y))
    other = send(other, lambda y, x, z, c: (c, x, 1 - z, y))

    pair, context = pl.pallas_call(
        pair_kernel,
        grid=(HALF // ROWS,),
        in_specs=[
            SMEM,
            pl.BlockSpec((8 * GROUP, ROWS, TILE), lambda i: (0, i, 0)),
            pl.BlockSpec((hid * 8, 8 * GROUP * 8 + ONES), lambda i: (0, 0)),
            pl.BlockSpec((outs * 8, hid * 4), lambda i: (0, 0)),
            pl.BlockSpec((outs * 8, 128), lambda i: (0, 0)),
            pl.BlockSpec((outs, ROWS, TILE), lambda i: (0, i, 0)),
            pl.BlockSpec((HALF, WIDE), lambda i: (0, 0)),
            pl.BlockSpec((HALF, WIDE), lambda i: (0, 0)),
        ],
        out_specs=[
            pl.BlockSpec((outs, ROWS, TILE), lambda i: (0, i, 0)),
            pl.BlockSpec((HALF, 2 * WIDE), lambda i: (0, 0)),
        ],
        out_shape=[shape((outs, HALF, TILE)), shape((HALF, 2 * WIDE))],
        compiler_params=params(14),
        cost_estimate=cost(5e9, 14e6),
        name="pair",
    )(
        where,
        received,
        *(in_hbm(a) for a in (first, second, second_bias, relative, same, other)),
    )
    return (context, pair)


def solution(mesh):
    return jax.shard_map(
        local,
        mesh=mesh,
        in_specs=(
            P("band", "head"),
            P("band", "head"),
            P("band", "head"),
            P(),
            P(),
            P(),
            P(),
            P(),
            P(),
        ),
        out_specs=(P("band", "head"), P(None, "band", "head")),
        check_vma=False,
    )
```

```python
import functools
import itertools
import math

import jax
import jax.numpy as jnp
from jax import lax
from jax.experimental import pallas as pl
from jax.experimental.pallas import tpu as pltpu
from jax.sharding import PartitionSpec as P

HEAD_DIM = 128
CLIP = 32
GAP = 512
BINS = 65
GROUP = 5
WIDE = GROUP * HEAD_DIM
BLOCK = 128
HALF = 64
TILE = 512
NEAR, FAR = (0, 1, 3), 2
ROWS = 16
ONES = 16
SCALE = math.log2(math.e) / math.sqrt(HEAD_DIM)
AXES = ("head", "band")
MIB = 1 << 20


def device(y, x, z, c):
    return c * 32 + y * 8 + x * 2 + z


def moves(to):
    return [
        (device(y, x, z, c), device(*to(y, x, z, c)))
        for c, y, x, z in itertools.product(range(4), range(4), range(4), range(2))
    ]


def send(value, to):
    return lax.ppermute(value, AXES, moves(to))


def over_columns_of(values):
    return [send(values[d], lambda y, x, z, c, d=d: (y, (x + d) % 4, z, c)) for d in (1, 2, 3)]


def over_columns(value):
    return over_columns_of([value] * 4)


def over_rows(value):
    return [send(value, lambda y, x, z, c, d=d: (y, x, z, c ^ d)) for d in (1, 2, 3)]


def nt(a, b):
    return lax.dot_general(a, b, (((1,), (1,)), ((), ())), preferred_element_type=jnp.float32)


def fetch(where, row_blocks, row_parts, column_blocks, column_part, sems):
    y, z, c = where[0], where[2], where[3]
    copies = []
    for d in range(4):
        away = lax.rem(lax.bitwise_xor(c, d) - y + 4, 4)
        for part in range(2):
            start = pl.multiple_of(away * BLOCK + lax.bitwise_xor(z, part) * HALF, HALF)
            for ref, at in row_parts:
                copies.append(
                    pltpu.make_async_copy(
                        row_blocks[d].at[pl.ds(part * HALF, HALF), pl.ds(at * WIDE, WIDE)],
                        ref.at[pl.ds(start, HALF)],
                        sems.at[len(copies)],
                    )
                )
    ref, at = column_part
    start = 0
    for block in column_blocks:
        copies.append(
            pltpu.make_async_copy(
                block.at[:, pl.ds(at * WIDE, WIDE)],
                ref.at[pl.ds(start, block.shape[0])],
                sems.at[len(copies)],
            )
        )
        start += block.shape[0]
    for copy in copies:
        copy.start()
    for copy in copies:
        copy.wait()


def head(ref, h):
    return ref[:, h * HEAD_DIM : (h + 1) * HEAD_DIM]


def row_kernel(where, *refs):
    by_row, lifted_out, queries, keys, sems = refs[9:]
    fetch(where, refs[0:4], [(queries, 0)], refs[4:9], (keys, 1), sems)
    lane = lax.broadcasted_iota(jnp.int32, (TILE, 128), 1)
    kept = jnp.zeros((TILE, 128), jnp.float32)
    for h in range(GROUP):
        scores = nt(head(queries, h), head(keys, h)) * SCALE
        top = jnp.max(scores, axis=1, keepdims=True)
        lifted = jnp.exp2(scores - top)
        lifted_out[h] = lifted.astype(jnp.bfloat16)
        kept = jnp.where(lane == h, top, kept)
        kept = jnp.where(lane == 8 + h, jnp.sum(lifted, axis=1, keepdims=True), kept)
    by_row[...] = jnp.transpose(kept)[0:16]


def place(x, d):
    return pl.ds(pl.multiple_of(lax.rem(x - d + 4, 4) * BLOCK, BLOCK), BLOCK)


def columns_of(keys, values, queries, by_column, lifted_out, partials):
    for h in range(GROUP):
        scores = nt(head(keys, h), head(queries, h)) * SCALE
        top = jnp.max(scores, axis=0, keepdims=True)
        lifted = jnp.exp2(scores - top)
        by_column[h : h + 1, :] = top
        by_column[8 + h : 9 + h, :] = jnp.sum(lifted, axis=0, keepdims=True)
        lifted = lifted.astype(jnp.bfloat16)
        lifted_out[h] = lifted
        part = lax.dot_general(
            head(values, h), lifted, (((0,), (0,)), ((), ())), preferred_element_type=jnp.float32
        ).astype(jnp.bfloat16)
        for i, out in enumerate(partials):
            out[h * HEAD_DIM : (h + 1) * HEAD_DIM, :] = part[:, i * BLOCK : (i + 1) * BLOCK]


def column_kernel(where, *refs):
    by_column, lifted_out, partials = refs[7], refs[8], refs[9:12]
    keys, values, queries, sems = refs[12:]
    fetch(where, refs[0:4], [(keys, 1), (values, 2)], refs[4:7], (queries, 0), sems)
    by_column[...] = jnp.zeros_like(by_column)
    columns_of(keys, values, queries, by_column, lifted_out, partials)


def last_column_kernel(where, *refs):
    others, by_column, lifted_out, partial = refs[6:10]
    keys, values, queries, own, sems = refs[10:]
    fetch(where, refs[0:4], [(keys, 1), (values, 2)], refs[4:6], (queries, 0), sems)
    own[...] = jnp.zeros_like(own)
    columns_of(keys, values, queries, own, lifted_out, [partial])
    x = where[1]
    for i, d in enumerate(NEAR):
        by_column[:, place(x, d)] = others[:, i * BLOCK : (i + 1) * BLOCK]
    by_column[:, place(x, FAR)] = own[...]


def factors(refs):
    top = functools.reduce(jnp.maximum, [ref[0:8, :] for ref in refs])
    total = sum(ref[8:16, :] * jnp.exp2(ref[0:8, :] - top) for ref in refs)
    return jnp.exp2(refs[0][0:8, :] - top) / total


def turned(value):
    return jnp.transpose(jnp.concatenate([value] * 16, axis=0))


def symmetric_kernel(where, *refs):
    row_stats, column_stats = refs[0:4], refs[4:8]
    row_lifted, near_lifted, far_lifted, out, by_column, held, sems = refs[8:]
    by_row = turned(factors(row_stats) * 1024.0)
    by_column[...] = factors(column_stats) * 1024.0
    y, x, z = (where[i] for i in range(3))
    places = [place(x, d) for d in (*NEAR, FAR)]
    gains = [by_column[:, at] for at in places]
    copies = []
    for p in range(8):
        owner = lax.rem(y + p // 2, 4) * 2 + lax.bitwise_xor(z, p % 2)
        here = slice(p * HALF, (p + 1) * HALF)
        for h in range(GROUP):
            for i, at in enumerate(places):
                columns = slice(i * BLOCK, (i + 1) * BLOCK)
                mirrored = near_lifted[h, here, columns] if i < len(NEAR) else far_lifted[h, here]
                held[p, h, :, at] = (
                    row_lifted[h, here, columns].astype(jnp.float32) * by_row[here, h : h + 1]
                    + mirrored.astype(jnp.float32) * gains[i][h : h + 1, :]
                ).astype(jnp.bfloat16)
        copies.append(pltpu.make_async_copy(held.at[p], out.at[owner], sems.at[p]))
        copies[p].start()
    for copy in copies:
        copy.wait()


def context_kernel(where, *refs):
    column_stats, partials = refs[0:4], refs[4:8]
    same, other, held = refs[8:]
    here = pl.ds(pl.multiple_of(where[1] * BLOCK, BLOCK), BLOCK)
    tops = [ref[0:8, here] for ref in column_stats]
    top = functools.reduce(jnp.maximum, tops)
    scales = [jnp.exp2(own - top) for own in tops]
    total = sum(ref[8:16, here] * scale for ref, scale in zip(column_stats, scales))
    scales = [scale / total for scale in scales]
    for h in range(GROUP):
        at = slice(h * HEAD_DIM, (h + 1) * HEAD_DIM)
        summed = sum(
            ref[at, :].astype(jnp.float32) * scale[h : h + 1, :]
            for ref, scale in zip(partials, scales)
        )
        held[:, at] = jnp.transpose(summed).astype(jnp.bfloat16)
    z = where[2]
    same[...] = held[pl.ds(pl.multiple_of(z * HALF, HALF), HALF), :]
    other[...] = held[pl.ds(pl.multiple_of((1 - z) * HALF, HALF), HALF), :]


def one_hot(indices, axis):
    return (indices == lax.broadcasted_iota(jnp.int32, indices.shape, axis)).astype(jnp.float32)


def expanded(matrix, row_of, row_lane, column_of, column_lane, left, right):
    k, m = matrix.shape
    one = one_hot(row_of(lax.broadcasted_iota(jnp.int32, (left, m), 0)), 1)
    tall = nt(one.astype(jnp.bfloat16), matrix).astype(jnp.bfloat16)
    one = one_hot(column_of(lax.broadcasted_iota(jnp.int32, (k, right), 1)), 0)
    wide = jnp.dot(tall, one.astype(jnp.bfloat16), preferred_element_type=jnp.float32)
    at_row = row_lane(lax.broadcasted_iota(jnp.int32, (left, right), 0))
    at_column = column_lane(lax.broadcasted_iota(jnp.int32, (left, right), 1))
    return jnp.where(at_row == at_column, wide, 0.0).astype(jnp.bfloat16)


def repeated(bias, row_of, left):
    one = one_hot(row_of(lax.broadcasted_iota(jnp.int32, (left, bias.shape[0]), 0)), 1)
    wide = jnp.broadcast_to(bias[...], (bias.shape[0], 128))
    return jnp.dot(one, wide, precision=lax.Precision.HIGHEST, preferred_element_type=jnp.float32)


def spread_kernel(
    first, first_bias, second, second_bias, table, first_out, second_out, second_bias_out, table_out
):
    by_eight, eight = lambda r: r // 8, lambda r: r % 8
    by_four, four = lambda r: r // 4, lambda r: r % 4
    hid, outs = first.shape[1], second.shape[1]
    channel = lambda r: r % (hid * 4) // 4
    width = first.shape[0] * 8
    first_out[:, :width] = expanded(
        first[...],
        channel,
        lambda r: r // (hid * 4) * 4 + r % 4,
        by_eight,
        eight,
        hid * 8,
        width,
    )
    rest, parts = repeated(first_bias, channel, hid * 8)[:, :ONES], []
    for _ in range(3):
        parts.append(rest.astype(jnp.bfloat16).astype(jnp.float32))
        rest = rest - parts[-1]
    lane = lax.broadcasted_iota(jnp.int32, (hid * 8, ONES), 1)
    first_out[:, width:] = sum(
        jnp.where(lane == i, part, 0.0) for i, part in enumerate(parts)
    ).astype(jnp.bfloat16)
    second_out[: outs * 4] = expanded(second[...], by_four, four, by_four, four, outs * 4, hid * 4)
    second_out[outs * 4 :] = expanded(
        second[...], lambda r: r // 4 + 1 - r // 4 % 2 * 2, four, by_four, four, outs * 4, hid * 4
    )
    second_bias_out[...] = repeated(second_bias, by_eight, outs * 8)
    table_out[...] = expanded(
        table[...], by_eight, eight, by_eight, eight, outs * 8, table_out.shape[1]
    )


def relative_kernel(where, lengths, table, out):
    ends = [lengths[0], lengths[0] + lengths[1], lengths[0] + lengths[1] + lengths[2]]

    def residue(positions):
        return positions + GAP * sum((positions >= end).astype(jnp.int32) for end in ends)

    band = where[0] * 8 + where[1] * 2 + where[2]
    first_row = band * HALF + pl.program_id(0) * ROWS
    levels = lax.broadcasted_iota(jnp.int32, (72, 8, TILE), 0)
    columns = residue(where[3] * TILE + lax.broadcasted_iota(jnp.int32, (8, TILE), 1))
    halves = []
    for half in range(ROWS // 8):
        rows = residue(first_row + half * 8 + lax.broadcasted_iota(jnp.int32, (8, TILE), 0))
        bins = jnp.clip(columns - rows, -CLIP, CLIP) + CLIP
        spread = (bins[None] == levels).astype(jnp.float32).reshape(72 * 8, TILE)
        part = jnp.dot(
            table[...], spread.astype(jnp.bfloat16), preferred_element_type=jnp.float32
        )
        halves.append(part.reshape(-1, 8, TILE))
    out[...] = jnp.concatenate(halves, axis=1).astype(jnp.bfloat16)


def pair_kernel(where, tiles, first, second, second_bias, relative, same, other, out, context):
    z = where[2]

    @pl.when(pl.program_id(0) == 0)
    def _():
        context[:, pl.ds(pl.multiple_of(z * WIDE, WIDE), WIDE)] = same[...]
        context[:, pl.ds(pl.multiple_of((1 - z) * WIDE, WIDE), WIDE)] = other[...]

    loaded = tiles[...].astype(jnp.float32)
    outs, hid = second.shape[0] // 8, first.shape[0] // 8
    upper = lax.broadcasted_iota(jnp.int32, (outs // 2, 8, TILE), 1) < 4
    ones = jnp.ones((ONES, TILE), jnp.bfloat16)
    halves = []
    for half in range(ROWS // 8):
        stacked = loaded[:, half * 8 : half * 8 + 8, :].reshape(-1, TILE).astype(jnp.bfloat16)
        stacked = jnp.concatenate([stacked, ones], axis=0)
        hidden = jnp.dot(first[...], stacked, preferred_element_type=jnp.float32)
        hidden = jnp.maximum(hidden, 0.0).astype(jnp.bfloat16)
        low, high = (
            jnp.dot(
                second[part * outs * 4 : (part + 1) * outs * 4],
                hidden[part * hid * 4 : (part + 1) * hid * 4],
                preferred_element_type=jnp.float32,
            ).reshape(outs // 2, 8, TILE)
            for part in range(2)
        )
        even = jnp.where(upper, low, high)
        odd = pltpu.roll(jnp.where(upper, high, low), 4, 1)
        projected = jnp.stack([even, odd], axis=1).reshape(outs, 8, TILE)
        halves.append(
            projected + jnp.concatenate([second_bias[...]] * 4, axis=1).reshape(outs, 8, TILE)
        )
    out[...] = (
        jnp.concatenate(halves, axis=1) + relative[...].astype(jnp.float32)
    ).astype(jnp.bfloat16)


SMEM = pl.BlockSpec(memory_space=pltpu.SMEM)
ANY = pl.BlockSpec(memory_space=pl.ANY)
HBM = pl.BlockSpec(memory_space=pltpu.HBM)
VMEM = pl.BlockSpec(memory_space=pltpu.VMEM)


def params(mib):
    return pltpu.CompilerParams(vmem_limit_bytes=mib * MIB)


def cost(flops, bytes_accessed, exponentials=0):
    return pl.CostEstimate(
        flops=int(flops), bytes_accessed=int(bytes_accessed), transcendentals=int(exponentials)
    )


def in_hbm(value):
    return pltpu.with_memory_space_constraint(value, pltpu.HBM)


def vmem(rows, columns):
    return pltpu.VMEM((rows, columns), jnp.bfloat16)


def shape(dims, kind=jnp.bfloat16):
    return jax.ShapeDtypeStruct(dims, kind)


def local(queries, keys, values, w_first, b_first, w_second, b_second, rel_table, chain_lengths):
    band, c = lax.axis_index("band"), lax.axis_index("head")
    y, x, z = band // 8, (band // 2) % 4, band % 2
    where = jnp.stack([y, x, z, c]).astype(jnp.int32)
    hid, outs = w_first.shape[1], w_second.shape[1]

    first, second, second_bias, table = pl.pallas_call(
        spread_kernel,
        in_specs=[VMEM] * 5,
        out_specs=[VMEM] * 4,
        out_shape=[
            pltpu.HBM((hid * 8, 8 * GROUP * 8 + ONES), jnp.bfloat16),
            pltpu.HBM((outs * 8, hid * 4), jnp.bfloat16),
            pltpu.HBM((outs * 8, 128), jnp.float32),
            shape((outs * 8, 72 * 8)),
        ],
        compiler_params=params(6),
        cost_estimate=cost(4e8, 6e6),
        name="spread",
    )(
        w_first,
        b_first[:, None],
        w_second,
        b_second[:, None],
        jnp.pad(rel_table, ((0, 72 - BINS), (0, 0))),
    )

    near = jnp.concatenate([queries[:, :WIDE], keys[:, :WIDE], values[:, :WIDE]], axis=1)
    far = jnp.concatenate([queries[:, WIDE:], keys[:, WIDE:], values[:, WIDE:]], axis=1)
    same = send(jnp.where(z == 0, near, far), lambda y, x, z, c: (c, x, z, y))
    other = send(jnp.where(z == 0, far, near), lambda y, x, z, c: (c, x, 1 - z, y))
    block = jnp.where(
        z == 0,
        jnp.concatenate([same, other], axis=0),
        jnp.concatenate([other, same], axis=0),
    )

    block, first, second, second_bias, table = lax.optimization_barrier(
        (block, first, second, second_bias, table)
    )
    narrow = block[:, : 2 * WIDE]

    across = send(block, lambda y, x, z, c: (y, x, z, c ^ 2))
    right = send(narrow, lambda y, x, z, c: (y, (x + 1) % 4, z, c))
    left = send(narrow, lambda y, x, z, c: (y, (x + 3) % 4, z, c))
    relative = pl.pallas_call(
        relative_kernel,
        grid=(HALF // ROWS,),
        in_specs=[SMEM, SMEM, pl.BlockSpec((outs * 8, 72 * 8), lambda i: (0, 0))],
        out_specs=pl.BlockSpec((outs, ROWS, TILE), lambda i: (0, i, 0)),
        out_shape=pltpu.HBM((outs, HALF, TILE), jnp.bfloat16),
        compiler_params=params(8),
        cost_estimate=cost(2.4e9, 6e6),
        name="relative",
    )(where, chain_lengths, table)
    where, relative, left, right = lax.optimization_barrier((where, relative, left, right))
    column_blocks = [
        narrow,
        right,
        left,
        send(right[:HALF], lambda y, x, z, c: (y, (x + 1) % 4, z, c)),
        send(left[HALF:], lambda y, x, z, c: (y, (x + 3) % 4, z, c)),
    ]
    relative, across, block = lax.optimization_barrier((relative, across, block))
    beside = send(block, lambda y, x, z, c: (y, x, z, c ^ 1))
    row_blocks = [block, beside, across, send(across, lambda y, x, z, c: (y, x, z, c ^ 1))]

    near_stats, near_lifted, own_partial, right_partial, left_partial = pl.pallas_call(
        column_kernel,
        in_specs=[SMEM] + [ANY] * 7,
        out_specs=[VMEM] * 5,
        out_shape=[
            shape((16, len(NEAR) * BLOCK), jnp.float32),
            shape((GROUP, TILE, len(NEAR) * BLOCK)),
        ]
        + [shape((WIDE, BLOCK))] * 3,
        scratch_shapes=[vmem(TILE, WIDE)] * 2
        + [vmem(len(NEAR) * BLOCK, WIDE), pltpu.SemaphoreType.DMA((19,))],
        compiler_params=params(12),
        cost_estimate=cost(5e8, 7e6, 1e6),
        name="columns",
    )(where, *row_blocks, *column_blocks[:3])
    near_stats, *column_blocks[3:] = lax.optimization_barrier((near_stats, *column_blocks[3:]))
    by_column, far_lifted, far_partial = pl.pallas_call(
        last_column_kernel,
        in_specs=[SMEM] + [ANY] * 6 + [VMEM],
        out_specs=[VMEM] * 3,
        out_shape=[
            shape((16, TILE), jnp.float32),
            shape((GROUP, TILE, BLOCK)),
            shape((WIDE, BLOCK)),
        ],
        scratch_shapes=[vmem(TILE, WIDE)] * 2
        + [
            vmem(BLOCK, WIDE),
            pltpu.VMEM((16, BLOCK), jnp.float32),
            pltpu.SemaphoreType.DMA((18,)),
        ],
        compiler_params=params(12),
        cost_estimate=cost(2e8, 3e6, 3e5),
        name="last_columns",
    )(where, *row_blocks, *column_blocks[3:], near_stats)
    by_row, row_lifted = pl.pallas_call(
        row_kernel,
        in_specs=[SMEM] + [ANY] * 9,
        out_specs=[VMEM] * 2,
        out_shape=[shape((16, TILE), jnp.float32), shape((GROUP, TILE, TILE))],
        scratch_shapes=[vmem(TILE, WIDE)] * 2 + [pltpu.SemaphoreType.DMA((13,))],
        compiler_params=params(12),
        cost_estimate=cost(4e8, 8e6, 1.4e6),
        name="rows",
    )(where, *row_blocks, *column_blocks)
    partials = [own_partial, left_partial, far_partial, right_partial]
    row_stats = [by_row] + over_rows(by_row)
    column_stats = [by_column] + over_columns(by_column)

    tiles = pl.pallas_call(
        symmetric_kernel,
        in_specs=[SMEM] + [VMEM] * 11,
        out_specs=HBM,
        out_shape=shape((8, GROUP, HALF, TILE)),
        scratch_shapes=[
            pltpu.VMEM((8, TILE), jnp.float32),
            pltpu.VMEM((8, GROUP, HALF, TILE), jnp.bfloat16),
            pltpu.SemaphoreType.DMA((8,)),
        ],
        compiler_params=params(8),
        cost_estimate=cost(1e7, 9e6),
        name="symmetric",
    )(where, *row_stats, *column_stats, row_lifted, near_lifted, far_lifted)
    where, tiles = lax.optimization_barrier((where, tiles))
    groups = [[y * 8 + x * 2 + z for y in range(4) for z in range(2)] for x in range(4)]
    received = lax.all_to_all(
        tiles, "band", split_axis=0, concat_axis=0, axis_index_groups=groups, tiled=True
    ).reshape(8 * GROUP, HALF, TILE)

    same, other = pl.pallas_call(
        context_kernel,
        in_specs=[SMEM] + [VMEM] * 8,
        out_specs=[VMEM] * 2,
        out_shape=[shape((HALF, WIDE))] * 2,
        scratch_shapes=[vmem(BLOCK, WIDE)],
        compiler_params=params(4),
        cost_estimate=cost(1e6, 2e6),
        name="context",
    )(where, *column_stats, partials[0], *over_columns_of(partials))
    same = send(same, lambda y, x, z, c: (c, x, z, y))
    other = send(other, lambda y, x, z, c: (c, x, 1 - z, y))

    pair, context = pl.pallas_call(
        pair_kernel,
        grid=(HALF // ROWS,),
        in_specs=[
            SMEM,
            pl.BlockSpec((8 * GROUP, ROWS, TILE), lambda i: (0, i, 0)),
            pl.BlockSpec((hid * 8, 8 * GROUP * 8 + ONES), lambda i: (0, 0)),
            pl.BlockSpec((outs * 8, hid * 4), lambda i: (0, 0)),
            pl.BlockSpec((outs * 8, 128), lambda i: (0, 0)),
            pl.BlockSpec((outs, ROWS, TILE), lambda i: (0, i, 0)),
            pl.BlockSpec((HALF, WIDE), lambda i: (0, 0)),
            pl.BlockSpec((HALF, WIDE), lambda i: (0, 0)),
        ],
        out_specs=[
            pl.BlockSpec((outs, ROWS, TILE), lambda i: (0, i, 0)),
            pl.BlockSpec((HALF, 2 * WIDE), lambda i: (0, 0)),
        ],
        out_shape=[shape((outs, HALF, TILE)), shape((HALF, 2 * WIDE))],
        compiler_params=params(14),
        cost_estimate=cost(5e9, 14e6),
        name="pair",
    )(
        where,
        received,
        *(in_hbm(a) for a in (first, second, second_bias, relative, same, other)),
    )
    return (context, pair)


def solution(mesh):
    return jax.shard_map(
        local,
        mesh=mesh,
        in_specs=(
            P("band", "head"),
            P("band", "head"),
            P("band", "head"),
            P(),
            P(),
            P(),
            P(),
            P(),
            P(),
        ),
        out_specs=(P("band", "head"), P(None, "band", "head")),
        check_vma=False,
    )
```

```python
import functools
import itertools
import math

import jax
import jax.numpy as jnp
from jax import lax
from jax.experimental import pallas as pl
from jax.experimental.pallas import tpu as pltpu
from jax.sharding import PartitionSpec as P

HEAD_DIM = 128
CLIP = 32
GAP = 512
BINS = 65
GROUP = 5
WIDE = GROUP * HEAD_DIM
BLOCK = 128
HALF = 64
TILE = 512
NEAR, FAR = (0, 1, 3), 2
ROWS = 16
ONES = 16
SCALE = math.log2(math.e) / math.sqrt(HEAD_DIM)
AXES = ("head", "band")
MIB = 1 << 20


def device(y, x, z, c):
    return c * 32 + y * 8 + x * 2 + z


def moves(to):
    return [
        (device(y, x, z, c), device(*to(y, x, z, c)))
        for c, y, x, z in itertools.product(range(4), range(4), range(4), range(2))
    ]


def send(value, to):
    return lax.ppermute(value, AXES, moves(to))


def over_columns_of(values):
    return [send(values[d], lambda y, x, z, c, d=d: (y, (x + d) % 4, z, c)) for d in (1, 2, 3)]


def over_columns(value):
    return over_columns_of([value] * 4)


def over_rows(value):
    return [send(value, lambda y, x, z, c, d=d: (y, x, z, c ^ d)) for d in (1, 2, 3)]


def nt(a, b):
    return lax.dot_general(a, b, (((1,), (1,)), ((), ())), preferred_element_type=jnp.float32)


def head(blocks, part, h):
    at = slice(part * WIDE + h * HEAD_DIM, part * WIDE + (h + 1) * HEAD_DIM)
    return jnp.concatenate([block[:, at] for block in blocks], axis=0)


def rows_of(rows, columns, lifted_out):
    lane = lax.broadcasted_iota(jnp.int32, (TILE, 128), 1)
    kept = jnp.zeros((TILE, 128), jnp.float32)
    for h in range(GROUP):
        scores = nt(head(rows, 0, h), head(columns, 1, h)) * SCALE
        top = jnp.max(scores, axis=1, keepdims=True)
        lifted = jnp.exp2(scores - top)
        lifted_out[h] = lifted.astype(jnp.bfloat16)
        kept = jnp.where(lane == h, top, kept)
        kept = jnp.where(lane == 8 + h, jnp.sum(lifted, axis=1, keepdims=True), kept)
    return jnp.transpose(kept)[0:16]


def place(x, d):
    return pl.ds(pl.multiple_of(lax.rem(x - d + 4, 4) * BLOCK, BLOCK), BLOCK)


def row_place(c, d):
    return pl.ds(pl.multiple_of(lax.bitwise_xor(c, d) * BLOCK, BLOCK), BLOCK)


def columns_of(rows, columns, by_column, lifted_out, partials):
    by_column[...] = jnp.zeros_like(by_column)
    for h in range(GROUP):
        scores = nt(head(rows, 1, h), head(columns, 0, h)) * SCALE
        top = jnp.max(scores, axis=0, keepdims=True)
        lifted = jnp.exp2(scores - top)
        by_column[h : h + 1, :] = top
        by_column[8 + h : 9 + h, :] = jnp.sum(lifted, axis=0, keepdims=True)
        lifted = lifted.astype(jnp.bfloat16)
        lifted_out[h] = lifted
        part = lax.dot_general(
            head(rows, 2, h),
            lifted,
            (((0,), (0,)), ((), ())),
            preferred_element_type=jnp.float32,
        ).astype(jnp.bfloat16)
        for i, out in enumerate(partials):
            out[h * HEAD_DIM : (h + 1) * HEAD_DIM, :] = part[:, i * BLOCK : (i + 1) * BLOCK]


def near_kernel(*refs):
    rows, columns = refs[0:4], refs[4:7]
    by_row, by_column, row_lifted, column_lifted = refs[7:11]
    columns_of(rows, columns, by_column, column_lifted, refs[11:14])
    by_row[...] = rows_of(rows, columns, row_lifted)


def far_kernel(where, *refs):
    rows, columns, near_by_row, near_by_column = refs[0:4], refs[4:6], refs[6], refs[7]
    by_row, top, by_column, row_lifted, column_lifted, partial, own = refs[8:]
    x, c = where[1], where[3]
    columns_of(rows, columns, own, column_lifted, [partial])
    for i, d in enumerate(NEAR):
        by_column[:, place(x, d)] = near_by_column[:, i * BLOCK : (i + 1) * BLOCK]
    by_column[:, place(x, FAR)] = own[...]
    far_by_row = rows_of(rows, columns, row_lifted)
    tops = near_by_row[0:8], far_by_row[0:8]
    both = jnp.maximum(*tops)
    total = near_by_row[8:16] * jnp.exp2(tops[0] - both) + far_by_row[8:16] * jnp.exp2(
        tops[1] - both
    )
    top[...] = tops[1]
    for d in range(4):
        by_row[0:8, row_place(c, d)] = both[:, d * BLOCK : (d + 1) * BLOCK]
        by_row[8:16, row_place(c, d)] = total[:, d * BLOCK : (d + 1) * BLOCK]


def merged(refs):
    top = functools.reduce(jnp.maximum, [ref[0:8, :] for ref in refs])
    return top, sum(ref[8:16, :] * jnp.exp2(ref[0:8, :] - top) for ref in refs)


def turned(value):
    return jnp.transpose(jnp.concatenate([value] * 16, axis=0))


def symmetric_kernel(where, *refs):
    row_stats, column_stats = refs[0:4], refs[4:8]
    row_tops, row_lifted, column_lifted = refs[8:10], refs[10:12], refs[12:14]
    out, totals, held, sems = refs[14:]
    x, z, c = (where[i] for i in range(1, 4))
    totals[0:8, :], totals[8:16, :] = merged(row_stats)
    top, total = (
        jnp.concatenate([totals[at : at + 8, row_place(c, d)] for d in range(4)], axis=1)
        for at in (0, 8)
    )
    by_row = [turned(jnp.exp2(ref[0:8, :] - top) * (1024.0 / total)) for ref in row_tops]
    top, total = merged(column_stats)
    totals[0:8, :] = jnp.exp2(column_stats[0][0:8, :] - top) * (1024.0 / total)
    places = [place(x, d) for d in (*NEAR, FAR)]
    gains = [totals[0:8, at] for at in places]
    copies = []
    for p in range(8):
        owner = lax.bitwise_xor(c, p // 2) * 2 + p % 2
        here = slice(p * HALF, (p + 1) * HALF)
        for h in range(GROUP):
            for i, at in enumerate(places):
                part, block = divmod(i, len(NEAR))
                columns = slice(block * BLOCK, (block + 1) * BLOCK)
                held[p, h, :, at] = (
                    row_lifted[part][h, here, columns].astype(jnp.float32)
                    * by_row[part][here, h : h + 1]
                    + column_lifted[part][h, here, columns].astype(jnp.float32)
                    * gains[i][h : h + 1, :]
                ).astype(jnp.bfloat16)
        copies.append(pltpu.make_async_copy(held.at[p], out.at[owner], sems.at[p]))
        copies[p].start()
    for copy in copies:
        copy.wait()


def context_kernel(where, *refs):
    column_stats, partials = refs[0:4], refs[4:8]
    same, other, held = refs[8:]
    here = pl.ds(pl.multiple_of(where[1] * BLOCK, BLOCK), BLOCK)
    tops = [ref[0:8, here] for ref in column_stats]
    top = functools.reduce(jnp.maximum, tops)
    scales = [jnp.exp2(own - top) for own in tops]
    total = sum(ref[8:16, here] * scale for ref, scale in zip(column_stats, scales))
    scales = [scale / total for scale in scales]
    for h in range(GROUP):
        at = slice(h * HEAD_DIM, (h + 1) * HEAD_DIM)
        summed = sum(
            ref[at, :].astype(jnp.float32) * scale[h : h + 1, :]
            for ref, scale in zip(partials, scales)
        )
        held[:, at] = jnp.transpose(summed).astype(jnp.bfloat16)
    z = where[2]
    same[...] = held[pl.ds(pl.multiple_of(z * HALF, HALF), HALF), :]
    other[...] = held[pl.ds(pl.multiple_of((1 - z) * HALF, HALF), HALF), :]


def one_hot(indices, axis):
    return (indices == lax.broadcasted_iota(jnp.int32, indices.shape, axis)).astype(jnp.float32)


def expanded(matrix, row_of, row_lane, column_of, column_lane, left, right):
    k, m = matrix.shape
    one = one_hot(row_of(lax.broadcasted_iota(jnp.int32, (left, m), 0)), 1)
    tall = nt(one.astype(jnp.bfloat16), matrix).astype(jnp.bfloat16)
    one = one_hot(column_of(lax.broadcasted_iota(jnp.int32, (k, right), 1)), 0)
    wide = jnp.dot(tall, one.astype(jnp.bfloat16), preferred_element_type=jnp.float32)
    at_row = row_lane(lax.broadcasted_iota(jnp.int32, (left, right), 0))
    at_column = column_lane(lax.broadcasted_iota(jnp.int32, (left, right), 1))
    return jnp.where(at_row == at_column, wide, 0.0).astype(jnp.bfloat16)


def repeated(bias, row_of, left):
    one = one_hot(row_of(lax.broadcasted_iota(jnp.int32, (left, bias.shape[0]), 0)), 1)
    wide = jnp.broadcast_to(bias[...], (bias.shape[0], 128))
    return jnp.dot(one, wide, precision=lax.Precision.HIGHEST, preferred_element_type=jnp.float32)


def spread_kernel(
    first, first_bias, second, second_bias, table, first_out, second_out, second_bias_out, table_out
):
    by_eight, eight = lambda r: r // 8, lambda r: r % 8
    by_four, four = lambda r: r // 4, lambda r: r % 4
    hid, outs = first.shape[1], second.shape[1]
    channel = lambda r: r % (hid * 4) // 4
    width = first.shape[0] * 8
    first_out[:, :width] = expanded(
        first[...],
        channel,
        lambda r: r // (hid * 4) * 4 + r % 4,
        by_eight,
        eight,
        hid * 8,
        width,
    )
    rest, parts = repeated(first_bias, channel, hid * 8)[:, :ONES], []
    for _ in range(3):
        parts.append(rest.astype(jnp.bfloat16).astype(jnp.float32))
        rest = rest - parts[-1]
    lane = lax.broadcasted_iota(jnp.int32, (hid * 8, ONES), 1)
    first_out[:, width:] = sum(
        jnp.where(lane == i, part, 0.0) for i, part in enumerate(parts)
    ).astype(jnp.bfloat16)
    second_out[: outs * 4] = expanded(second[...], by_four, four, by_four, four, outs * 4, hid * 4)
    second_out[outs * 4 :] = expanded(
        second[...], lambda r: r // 4 + 1 - r // 4 % 2 * 2, four, by_four, four, outs * 4, hid * 4
    )
    second_bias_out[...] = repeated(second_bias, by_eight, outs * 8)
    table_out[...] = expanded(
        table[...], by_eight, eight, by_eight, eight, outs * 8, table_out.shape[1]
    )


def relative_kernel(where, lengths, table, out):
    ends = [lengths[0], lengths[0] + lengths[1], lengths[0] + lengths[1] + lengths[2]]

    def residue(positions):
        return positions + GAP * sum((positions >= end).astype(jnp.int32) for end in ends)

    band = where[0] * 8 + where[1] * 2 + where[2]
    first_row = band * HALF + pl.program_id(0) * ROWS
    levels = lax.broadcasted_iota(jnp.int32, (72, 8, TILE), 0)
    columns = residue(where[3] * TILE + lax.broadcasted_iota(jnp.int32, (8, TILE), 1))
    halves = []
    for half in range(ROWS // 8):
        rows = residue(first_row + half * 8 + lax.broadcasted_iota(jnp.int32, (8, TILE), 0))
        bins = jnp.clip(columns - rows, -CLIP, CLIP) + CLIP
        spread = (bins[None] == levels).astype(jnp.float32).reshape(72 * 8, TILE)
        part = jnp.dot(
            table[...], spread.astype(jnp.bfloat16), preferred_element_type=jnp.float32
        )
        halves.append(part.reshape(-1, 8, TILE))
    out[...] = jnp.concatenate(halves, axis=1).astype(jnp.bfloat16)


def pair_kernel(where, tiles, first, second, second_bias, relative, same, other, out, context):
    z = where[2]

    @pl.when(pl.program_id(0) == 0)
    def _():
        context[:, pl.ds(pl.multiple_of(z * WIDE, WIDE), WIDE)] = same[...]
        context[:, pl.ds(pl.multiple_of((1 - z) * WIDE, WIDE), WIDE)] = other[...]

    loaded = tiles[...].astype(jnp.float32)
    outs, hid = second.shape[0] // 8, first.shape[0] // 8
    upper = lax.broadcasted_iota(jnp.int32, (outs // 2, 8, TILE), 1) < 4
    ones = jnp.ones((ONES, TILE), jnp.bfloat16)
    halves = []
    for half in range(ROWS // 8):
        stacked = loaded[:, half * 8 : half * 8 + 8, :].reshape(-1, TILE).astype(jnp.bfloat16)
        stacked = jnp.concatenate([stacked, ones], axis=0)
        hidden = jnp.dot(first[...], stacked, preferred_element_type=jnp.float32)
        hidden = jnp.maximum(hidden, 0.0).astype(jnp.bfloat16)
        low, high = (
            jnp.dot(
                second[part * outs * 4 : (part + 1) * outs * 4],
                hidden[part * hid * 4 : (part + 1) * hid * 4],
                preferred_element_type=jnp.float32,
            ).reshape(outs // 2, 8, TILE)
            for part in range(2)
        )
        even = jnp.where(upper, low, high)
        odd = pltpu.roll(jnp.where(upper, high, low), 4, 1)
        projected = jnp.stack([even, odd], axis=1).reshape(outs, 8, TILE)
        halves.append(
            projected + jnp.concatenate([second_bias[...]] * 4, axis=1).reshape(outs, 8, TILE)
        )
    out[...] = (
        jnp.concatenate(halves, axis=1) + relative[...].astype(jnp.float32)
    ).astype(jnp.bfloat16)


SMEM = pl.BlockSpec(memory_space=pltpu.SMEM)
ANY = pl.BlockSpec(memory_space=pl.ANY)
HBM = pl.BlockSpec(memory_space=pltpu.HBM)
VMEM = pl.BlockSpec(memory_space=pltpu.VMEM)


def params(mib):
    return pltpu.CompilerParams(vmem_limit_bytes=mib * MIB)


def cost(flops, bytes_accessed, exponentials=0):
    return pl.CostEstimate(
        flops=int(flops), bytes_accessed=int(bytes_accessed), transcendentals=int(exponentials)
    )


def in_hbm(value):
    return pltpu.with_memory_space_constraint(value, pltpu.HBM)


def vmem(rows, columns):
    return pltpu.VMEM((rows, columns), jnp.bfloat16)


def shape(dims, kind=jnp.bfloat16):
    return jax.ShapeDtypeStruct(dims, kind)


def local(queries, keys, values, w_first, b_first, w_second, b_second, rel_table, chain_lengths):
    band, c = lax.axis_index("band"), lax.axis_index("head")
    y, x, z = band // 8, (band // 2) % 4, band % 2
    where = jnp.stack([y, x, z, c]).astype(jnp.int32)
    hid, outs = w_first.shape[1], w_second.shape[1]

    first, second, second_bias, table = pl.pallas_call(
        spread_kernel,
        in_specs=[VMEM] * 5,
        out_specs=[VMEM] * 4,
        out_shape=[
            pltpu.HBM((hid * 8, 8 * GROUP * 8 + ONES), jnp.bfloat16),
            pltpu.HBM((outs * 8, hid * 4), jnp.bfloat16),
            pltpu.HBM((outs * 8, 128), jnp.float32),
            shape((outs * 8, 72 * 8)),
        ],
        compiler_params=params(6),
        cost_estimate=cost(4e8, 6e6),
        name="spread",
    )(
        w_first,
        b_first[:, None],
        w_second,
        b_second[:, None],
        jnp.pad(rel_table, ((0, 72 - BINS), (0, 0))),
    )

    def half(at):
        near, far = (
            jnp.concatenate([a[:, lo : lo + WIDE] for a in (queries, keys, values)], axis=1)
            for lo in (0, WIDE)
        )
        return jnp.where(at == 0, near, far)

    crossing = half(1 - z)
    crossing, z = lax.optimization_barrier((crossing, z))
    other = send(crossing, lambda y, x, z, c: (c, x, 1 - z, y))
    same = send(half(z), lambda y, x, z, c: (c, x, z, y))
    block = jnp.where(
        z == 0,
        jnp.concatenate([same, other], axis=0),
        jnp.concatenate([other, same], axis=0),
    )

    block, first, second, second_bias, table = lax.optimization_barrier(
        (block, first, second, second_bias, table)
    )
    narrow = block[:, : 2 * WIDE]

    across = send(block, lambda y, x, z, c: (y, x, z, c ^ 2))
    right = send(narrow, lambda y, x, z, c: (y, (x + 1) % 4, z, c))
    left = send(narrow, lambda y, x, z, c: (y, (x + 3) % 4, z, c))
    relative = pl.pallas_call(
        relative_kernel,
        grid=(HALF // ROWS,),
        in_specs=[SMEM, SMEM, pl.BlockSpec((outs * 8, 72 * 8), lambda i: (0, 0))],
        out_specs=pl.BlockSpec((outs, ROWS, TILE), lambda i: (0, i, 0)),
        out_shape=pltpu.HBM((outs, HALF, TILE), jnp.bfloat16),
        compiler_params=params(8),
        cost_estimate=cost(2.4e9, 6e6),
        name="relative",
    )(where, chain_lengths, table)
    where, relative, left, right = lax.optimization_barrier((where, relative, left, right))
    column_blocks = [
        narrow,
        right,
        left,
        send(right[:HALF], lambda y, x, z, c: (y, (x + 1) % 4, z, c)),
        send(left[HALF:], lambda y, x, z, c: (y, (x + 3) % 4, z, c)),
    ]
    relative, across, block = lax.optimization_barrier((relative, across, block))
    beside = send(block, lambda y, x, z, c: (y, x, z, c ^ 1))
    row_blocks = [block, beside, across, send(across, lambda y, x, z, c: (y, x, z, c ^ 1))]

    near = len(NEAR) * BLOCK
    near_outs = [
        shape((16, TILE), jnp.float32),
        shape((16, near), jnp.float32),
        *[shape((GROUP, TILE, near))] * 2,
        *[shape((WIDE, BLOCK))] * 3,
    ]
    near_by_row, near_by_column, *near_lifted, own_partial, right_partial, left_partial = (
        pl.pallas_call(
            near_kernel,
            in_specs=[VMEM] * 7,
            out_specs=[VMEM] * len(near_outs),
            out_shape=near_outs,
            compiler_params=params(16),
            cost_estimate=cost(8e8, 12e6, 2e6),
            name="near",
        )(*row_blocks, *column_blocks[:3])
    )
    near_by_row, *column_blocks[3:] = lax.optimization_barrier((near_by_row, *column_blocks[3:]))
    far_outs = [
        shape((16, TILE), jnp.float32),
        shape((8, TILE), jnp.float32),
        shape((16, TILE), jnp.float32),
        *[shape((GROUP, TILE, BLOCK))] * 2,
        shape((WIDE, BLOCK)),
    ]
    by_row, far_top, by_column, *far_lifted, far_partial = pl.pallas_call(
        far_kernel,
        in_specs=[SMEM] + [VMEM] * 8,
        out_specs=[VMEM] * len(far_outs),
        out_shape=far_outs,
        scratch_shapes=[pltpu.VMEM((16, BLOCK), jnp.float32)],
        compiler_params=params(12),
        cost_estimate=cost(3e8, 5e6, 7e5),
        name="far",
    )(where, *row_blocks, *column_blocks[3:], near_by_row, near_by_column)
    partials = [own_partial, left_partial, far_partial, right_partial]
    row_stats = [by_row] + over_rows(by_row)
    column_stats = [by_column] + over_columns(by_column)

    tiles = pl.pallas_call(
        symmetric_kernel,
        in_specs=[SMEM] + [VMEM] * 14,
        out_specs=HBM,
        out_shape=shape((8, GROUP, HALF, TILE)),
        scratch_shapes=[
            pltpu.VMEM((16, TILE), jnp.float32),
            pltpu.VMEM((8, GROUP, HALF, TILE), jnp.bfloat16),
            pltpu.SemaphoreType.DMA((8,)),
        ],
        compiler_params=params(8),
        cost_estimate=cost(1e7, 9e6),
        name="symmetric",
    )(
        where,
        *row_stats,
        *column_stats,
        near_by_row,
        far_top,
        *(part for parts in zip(near_lifted, far_lifted) for part in parts),
    )
    where, tiles = lax.optimization_barrier((where, tiles))
    groups = [[y * 8 + x * 2 + z for y in range(4) for z in range(2)] for x in range(4)]
    received = lax.all_to_all(
        tiles, "band", split_axis=0, concat_axis=0, axis_index_groups=groups, tiled=True
    ).reshape(8 * GROUP, HALF, TILE)

    same, other = pl.pallas_call(
        context_kernel,
        in_specs=[SMEM] + [VMEM] * 8,
        out_specs=[VMEM] * 2,
        out_shape=[shape((HALF, WIDE))] * 2,
        scratch_shapes=[vmem(BLOCK, WIDE)],
        compiler_params=params(4),
        cost_estimate=cost(1e6, 2e6),
        name="context",
    )(where, *column_stats, partials[0], *over_columns_of(partials))
    same = send(same, lambda y, x, z, c: (c, x, z, y))
    other = send(other, lambda y, x, z, c: (c, x, 1 - z, y))

    pair, context = pl.pallas_call(
        pair_kernel,
        grid=(HALF // ROWS,),
        in_specs=[
            SMEM,
            pl.BlockSpec((8 * GROUP, ROWS, TILE), lambda i: (0, i, 0)),
            pl.BlockSpec((hid * 8, 8 * GROUP * 8 + ONES), lambda i: (0, 0)),
            pl.BlockSpec((outs * 8, hid * 4), lambda i: (0, 0)),
            pl.BlockSpec((outs * 8, 128), lambda i: (0, 0)),
            pl.BlockSpec((outs, ROWS, TILE), lambda i: (0, i, 0)),
            pl.BlockSpec((HALF, WIDE), lambda i: (0, 0)),
            pl.BlockSpec((HALF, WIDE), lambda i: (0, 0)),
        ],
        out_specs=[
            pl.BlockSpec((outs, ROWS, TILE), lambda i: (0, i, 0)),
            pl.BlockSpec((HALF, 2 * WIDE), lambda i: (0, 0)),
        ],
        out_shape=[shape((outs, HALF, TILE)), shape((HALF, 2 * WIDE))],
        compiler_params=params(14),
        cost_estimate=cost(5e9, 14e6),
        name="pair",
    )(
        where,
        received,
        *(in_hbm(a) for a in (first, second, second_bias, relative, same, other)),
    )
    return (context, pair)


def solution(mesh):
    return jax.shard_map(
        local,
        mesh=mesh,
        in_specs=(
            P("band", "head"),
            P("band", "head"),
            P("band", "head"),
            P(),
            P(),
            P(),
            P(),
            P(),
            P(),
        ),
        out_specs=(P("band", "head"), P(None, "band", "head")),
        check_vma=False,
    )
```

```python
import functools
import itertools
import math

import jax
import jax.numpy as jnp
from jax import lax
from jax.experimental import pallas as pl
from jax.experimental.pallas import tpu as pltpu
from jax.sharding import PartitionSpec as P

HEAD_DIM = 128
CLIP = 32
GAP = 512
BINS = 65
GROUP = 5
WIDE = GROUP * HEAD_DIM
BLOCK = 128
HALF = 64
TILE = 512
NEAR, FAR = (0, 1, 3), 2
ROWS = 16
ONES = 16
SCALE = math.log2(math.e) / math.sqrt(HEAD_DIM)
AXES = ("head", "band")
MIB = 1 << 20


def device(y, x, z, c):
    return c * 32 + y * 8 + x * 2 + z


def moves(to):
    return [
        (device(y, x, z, c), device(*to(y, x, z, c)))
        for c, y, x, z in itertools.product(range(4), range(4), range(4), range(2))
    ]


def send(value, to):
    return lax.ppermute(value, AXES, moves(to))


def over_columns_of(values):
    return [send(values[d], lambda y, x, z, c, d=d: (y, (x + d) % 4, z, c)) for d in (1, 2, 3)]


def over_columns(value):
    return over_columns_of([value] * 4)


def nt(a, b):
    return lax.dot_general(a, b, (((1,), (1,)), ((), ())), preferred_element_type=jnp.float32)


def head(blocks, part, h):
    at = slice(part * WIDE + h * HEAD_DIM, part * WIDE + (h + 1) * HEAD_DIM)
    return jnp.concatenate([block[:, at] for block in blocks], axis=0)


def rows_of(rows, columns, lifted_out):
    lane = lax.broadcasted_iota(jnp.int32, (TILE, 128), 1)
    kept = jnp.zeros((TILE, 128), jnp.float32)
    for h in range(GROUP):
        scores = nt(head(rows, 0, h), head(columns, 1, h)) * SCALE
        top = jnp.max(scores, axis=1, keepdims=True)
        lifted = jnp.exp2(scores - top)
        lifted_out[h] = lifted.astype(jnp.bfloat16)
        kept = jnp.where(lane == h, top, kept)
        kept = jnp.where(lane == 8 + h, jnp.sum(lifted, axis=1, keepdims=True), kept)
    return jnp.transpose(kept)[0:16]


def place(x, d):
    return pl.ds(pl.multiple_of(lax.rem(x - d + 4, 4) * BLOCK, BLOCK), BLOCK)


def row_place(c, d):
    return pl.ds(pl.multiple_of(lax.bitwise_xor(c, d) * BLOCK, BLOCK), BLOCK)


def columns_of(rows, columns, by_column, lifted_out):
    by_column[...] = jnp.zeros_like(by_column)
    for h in range(GROUP):
        scores = nt(head(rows, 1, h), head(columns, 0, h)) * SCALE
        top = jnp.max(scores, axis=0, keepdims=True)
        lifted = jnp.exp2(scores - top)
        by_column[h : h + 1, :] = top
        by_column[8 + h : 9 + h, :] = jnp.sum(lifted, axis=0, keepdims=True)
        lifted_out[h] = lifted.astype(jnp.bfloat16)


def near_kernel(*refs):
    rows, columns = refs[0:4], refs[4:7]
    by_row, by_column, row_lifted, column_lifted = refs[7:]
    columns_of(rows, columns, by_column, column_lifted)
    by_row[...] = rows_of(rows, columns, row_lifted)


def far_kernel(where, *refs):
    rows, columns, near_by_row, near_by_column = refs[0:4], refs[4:6], refs[6], refs[7]
    by_row, top, by_column, row_lifted, column_lifted, own = refs[8:]
    x, c = where[1], where[3]
    columns_of(rows, columns, own, column_lifted)
    for i, d in enumerate(NEAR):
        by_column[:, place(x, d)] = near_by_column[:, i * BLOCK : (i + 1) * BLOCK]
    by_column[:, place(x, FAR)] = own[...]
    far_by_row = rows_of(rows, columns, row_lifted)
    tops = near_by_row[0:8], far_by_row[0:8]
    both = jnp.maximum(*tops)
    total = near_by_row[8:16] * jnp.exp2(tops[0] - both) + far_by_row[8:16] * jnp.exp2(
        tops[1] - both
    )
    top[...] = tops[1]
    for d in range(4):
        by_row[0:8, row_place(c, d)] = both[:, d * BLOCK : (d + 1) * BLOCK]
        by_row[8:16, row_place(c, d)] = total[:, d * BLOCK : (d + 1) * BLOCK]


def partial_kernel(*refs):
    values, lifted, outs = refs[0:4], refs[4:6], refs[6:10]
    for h in range(GROUP):
        at = slice(h * HEAD_DIM, (h + 1) * HEAD_DIM)
        own = head(values, 2, h)
        for half, held in zip(lifted, (outs[:3], outs[3:])):
            part = lax.dot_general(
                own, half[h], (((0,), (0,)), ((), ())), preferred_element_type=jnp.float32
            ).astype(jnp.bfloat16)
            for i, out in enumerate(held):
                out[at, :] = part[:, i * BLOCK : (i + 1) * BLOCK]


def merged(refs):
    top = functools.reduce(jnp.maximum, [ref[0:8, :] for ref in refs])
    return top, sum(ref[8:16, :] * jnp.exp2(ref[0:8, :] - top) for ref in refs)


def merge_kernel(one, other, both):
    both[0:8, :], both[8:16, :] = merged([one, other])


def turned(value):
    return jnp.transpose(jnp.concatenate([value] * 16, axis=0))


def symmetric_kernel(where, *refs):
    row_stats, column_stats = refs[0:2], refs[2:6]
    row_tops, row_lifted, column_lifted = refs[6:8], refs[8:10], refs[10:12]
    out, totals, held, sems = refs[12:]
    x, z, c = (where[i] for i in range(1, 4))
    totals[0:8, :], totals[8:16, :] = merged(row_stats)
    top, total = (
        jnp.concatenate([totals[at : at + 8, row_place(c, d)] for d in range(4)], axis=1)
        for at in (0, 8)
    )
    by_row = [turned(jnp.exp2(ref[0:8, :] - top) * (1024.0 / total)) for ref in row_tops]
    top, total = merged(column_stats)
    totals[0:8, :] = jnp.exp2(column_stats[0][0:8, :] - top) * (1024.0 / total)
    places = [place(x, d) for d in (*NEAR, FAR)]
    gains = [totals[0:8, at] for at in places]
    copies = []
    for p in range(8):
        owner = lax.bitwise_xor(c, p // 2) * 2 + p % 2
        here = slice(p * HALF, (p + 1) * HALF)
        for h in range(GROUP):
            for i, at in enumerate(places):
                part, block = divmod(i, len(NEAR))
                columns = slice(block * BLOCK, (block + 1) * BLOCK)
                held[p, h, :, at] = (
                    row_lifted[part][h, here, columns].astype(jnp.float32)
                    * by_row[part][here, h : h + 1]
                    + column_lifted[part][h, here, columns].astype(jnp.float32)
                    * gains[i][h : h + 1, :]
                ).astype(jnp.bfloat16)
        copies.append(pltpu.make_async_copy(held.at[p], out.at[owner], sems.at[p]))
        copies[p].start()
    for copy in copies:
        copy.wait()


def context_kernel(where, *refs):
    column_stats, partials = refs[0:4], refs[4:8]
    same, other, held = refs[8:]
    here = pl.ds(pl.multiple_of(where[1] * BLOCK, BLOCK), BLOCK)
    tops = [ref[0:8, here] for ref in column_stats]
    top = functools.reduce(jnp.maximum, tops)
    scales = [jnp.exp2(own - top) for own in tops]
    total = sum(ref[8:16, here] * scale for ref, scale in zip(column_stats, scales))
    scales = [scale / total for scale in scales]
    for h in range(GROUP):
        at = slice(h * HEAD_DIM, (h + 1) * HEAD_DIM)
        summed = sum(
            ref[at, :].astype(jnp.float32) * scale[h : h + 1, :]
            for ref, scale in zip(partials, scales)
        )
        held[:, at] = jnp.transpose(summed).astype(jnp.bfloat16)
    z = where[2]
    same[...] = held[pl.ds(pl.multiple_of(z * HALF, HALF), HALF), :]
    other[...] = held[pl.ds(pl.multiple_of((1 - z) * HALF, HALF), HALF), :]


def one_hot(indices, axis):
    return (indices == lax.broadcasted_iota(jnp.int32, indices.shape, axis)).astype(jnp.float32)


def expanded(matrix, row_of, row_lane, column_of, column_lane, left, right):
    k, m = matrix.shape
    one = one_hot(row_of(lax.broadcasted_iota(jnp.int32, (left, m), 0)), 1)
    tall = nt(one.astype(jnp.bfloat16), matrix).astype(jnp.bfloat16)
    one = one_hot(column_of(lax.broadcasted_iota(jnp.int32, (k, right), 1)), 0)
    wide = jnp.dot(tall, one.astype(jnp.bfloat16), preferred_element_type=jnp.float32)
    at_row = row_lane(lax.broadcasted_iota(jnp.int32, (left, right), 0))
    at_column = column_lane(lax.broadcasted_iota(jnp.int32, (left, right), 1))
    return jnp.where(at_row == at_column, wide, 0.0).astype(jnp.bfloat16)


def repeated(bias, row_of, left):
    one = one_hot(row_of(lax.broadcasted_iota(jnp.int32, (left, bias.shape[0]), 0)), 1)
    wide = jnp.broadcast_to(bias[...], (bias.shape[0], 128))
    return jnp.dot(one, wide, precision=lax.Precision.HIGHEST, preferred_element_type=jnp.float32)


def spread_kernel(
    first, first_bias, second, second_bias, table, first_out, second_out, second_bias_out, table_out
):
    by_eight, eight = lambda r: r // 8, lambda r: r % 8
    by_four, four = lambda r: r // 4, lambda r: r % 4
    hid, outs = first.shape[1], second.shape[1]
    channel = lambda r: r % (hid * 4) // 4
    width = first.shape[0] * 8
    first_out[:, :width] = expanded(
        first[...],
        channel,
        lambda r: r // (hid * 4) * 4 + r % 4,
        by_eight,
        eight,
        hid * 8,
        width,
    )
    rest, parts = repeated(first_bias, channel, hid * 8)[:, :ONES], []
    for _ in range(3):
        parts.append(rest.astype(jnp.bfloat16).astype(jnp.float32))
        rest = rest - parts[-1]
    lane = lax.broadcasted_iota(jnp.int32, (hid * 8, ONES), 1)
    first_out[:, width:] = sum(
        jnp.where(lane == i, part, 0.0) for i, part in enumerate(parts)
    ).astype(jnp.bfloat16)
    second_out[: outs * 4] = expanded(second[...], by_four, four, by_four, four, outs * 4, hid * 4)
    second_out[outs * 4 :] = expanded(
        second[...], lambda r: r // 4 + 1 - r // 4 % 2 * 2, four, by_four, four, outs * 4, hid * 4
    )
    second_bias_out[...] = repeated(second_bias, by_eight, outs * 8)
    table_out[...] = expanded(
        table[...], by_eight, eight, by_eight, eight, outs * 8, table_out.shape[1]
    )


def relative_kernel(where, lengths, table, out):
    ends = [lengths[0], lengths[0] + lengths[1], lengths[0] + lengths[1] + lengths[2]]

    def residue(positions):
        return positions + GAP * sum((positions >= end).astype(jnp.int32) for end in ends)

    band = where[0] * 8 + where[1] * 2 + where[2]
    first_row = band * HALF + pl.program_id(0) * ROWS
    levels = lax.broadcasted_iota(jnp.int32, (72, 8, TILE), 0)
    columns = residue(where[3] * TILE + lax.broadcasted_iota(jnp.int32, (8, TILE), 1))
    halves = []
    for half in range(ROWS // 8):
        rows = residue(first_row + half * 8 + lax.broadcasted_iota(jnp.int32, (8, TILE), 0))
        bins = jnp.clip(columns - rows, -CLIP, CLIP) + CLIP
        spread = (bins[None] == levels).astype(jnp.float32).reshape(72 * 8, TILE)
        part = jnp.dot(
            table[...], spread.astype(jnp.bfloat16), preferred_element_type=jnp.float32
        )
        halves.append(part.reshape(-1, 8, TILE))
    out[...] = jnp.concatenate(halves, axis=1).astype(jnp.bfloat16)


def pair_kernel(where, tiles, first, second, second_bias, relative, same, other, out, context):
    z = where[2]

    @pl.when(pl.program_id(0) == 0)
    def _():
        context[:, pl.ds(pl.multiple_of(z * WIDE, WIDE), WIDE)] = same[...]
        context[:, pl.ds(pl.multiple_of((1 - z) * WIDE, WIDE), WIDE)] = other[...]

    start = pl.multiple_of(pl.program_id(0) * ROWS, ROWS)
    loaded = tiles[:, pl.ds(start, ROWS), :].astype(jnp.float32)
    outs, hid = second.shape[0] // 8, first.shape[0] // 8
    upper = lax.broadcasted_iota(jnp.int32, (outs // 2, 8, TILE), 1) < 4
    ones = jnp.ones((ONES, TILE), jnp.bfloat16)
    halves = []
    for half in range(ROWS // 8):
        stacked = loaded[:, half * 8 : half * 8 + 8, :].reshape(-1, TILE).astype(jnp.bfloat16)
        stacked = jnp.concatenate([stacked, ones], axis=0)
        hidden = jnp.dot(first[...], stacked, preferred_element_type=jnp.float32)
        hidden = jnp.maximum(hidden, 0.0).astype(jnp.bfloat16)
        low, high = (
            jnp.dot(
                second[part * outs * 4 : (part + 1) * outs * 4],
                hidden[part * hid * 4 : (part + 1) * hid * 4],
                preferred_element_type=jnp.float32,
            ).reshape(outs // 2, 8, TILE)
            for part in range(2)
        )
        even = jnp.where(upper, low, high)
        odd = pltpu.roll(jnp.where(upper, high, low), 4, 1)
        projected = jnp.stack([even, odd], axis=1).reshape(outs, 8, TILE)
        halves.append(
            projected + jnp.concatenate([second_bias[...]] * 4, axis=1).reshape(outs, 8, TILE)
        )
    out[...] = (
        jnp.concatenate(halves, axis=1) + relative[...].astype(jnp.float32)
    ).astype(jnp.bfloat16)


SMEM = pl.BlockSpec(memory_space=pltpu.SMEM)
ANY = pl.BlockSpec(memory_space=pl.ANY)
HBM = pl.BlockSpec(memory_space=pltpu.HBM)
VMEM = pl.BlockSpec(memory_space=pltpu.VMEM)


def params(mib):
    return pltpu.CompilerParams(vmem_limit_bytes=mib * MIB)


def cost(flops, bytes_accessed, exponentials=0):
    return pl.CostEstimate(
        flops=int(flops), bytes_accessed=int(bytes_accessed), transcendentals=int(exponentials)
    )


def in_hbm(value):
    return pltpu.with_memory_space_constraint(value, pltpu.HBM)


def vmem(rows, columns):
    return pltpu.VMEM((rows, columns), jnp.bfloat16)


def shape(dims, kind=jnp.bfloat16):
    return jax.ShapeDtypeStruct(dims, kind)


def local(queries, keys, values, w_first, b_first, w_second, b_second, rel_table, chain_lengths):
    band, c = lax.axis_index("band"), lax.axis_index("head")
    y, x, z = band // 8, (band // 2) % 4, band % 2
    where = jnp.stack([y, x, z, c]).astype(jnp.int32)
    hid, outs = w_first.shape[1], w_second.shape[1]

    first, second, second_bias, table = pl.pallas_call(
        spread_kernel,
        in_specs=[VMEM] * 5,
        out_specs=[VMEM] * 4,
        out_shape=[
            pltpu.HBM((hid * 8, 8 * GROUP * 8 + ONES), jnp.bfloat16),
            pltpu.HBM((outs * 8, hid * 4), jnp.bfloat16),
            pltpu.HBM((outs * 8, 128), jnp.float32),
            shape((outs * 8, 72 * 8)),
        ],
        compiler_params=params(6),
        cost_estimate=cost(4e8, 6e6),
        name="spread",
    )(
        w_first,
        b_first[:, None],
        w_second,
        b_second[:, None],
        jnp.pad(rel_table, ((0, 72 - BINS), (0, 0))),
    )

    def half(at):
        near, far = (
            jnp.concatenate([a[:, lo : lo + WIDE] for a in (queries, keys, values)], axis=1)
            for lo in (0, WIDE)
        )
        return jnp.where(at == 0, near, far)

    crossing = half(1 - z)
    crossing, z = lax.optimization_barrier((crossing, z))
    other = send(crossing, lambda y, x, z, c: (c, x, 1 - z, y))
    same = send(half(z), lambda y, x, z, c: (c, x, z, y))
    block = jnp.where(
        z == 0,
        jnp.concatenate([same, other], axis=0),
        jnp.concatenate([other, same], axis=0),
    )

    block, first, second, second_bias, table = lax.optimization_barrier(
        (block, first, second, second_bias, table)
    )
    narrow = block[:, : 2 * WIDE]

    across = send(block, lambda y, x, z, c: (y, x, z, c ^ 2))
    right = send(narrow, lambda y, x, z, c: (y, (x + 1) % 4, z, c))
    left = send(narrow, lambda y, x, z, c: (y, (x + 3) % 4, z, c))
    relative = pl.pallas_call(
        relative_kernel,
        grid=(HALF // ROWS,),
        in_specs=[SMEM, SMEM, pl.BlockSpec((outs * 8, 72 * 8), lambda i: (0, 0))],
        out_specs=pl.BlockSpec((outs, ROWS, TILE), lambda i: (0, i, 0)),
        out_shape=pltpu.HBM((outs, HALF, TILE), jnp.bfloat16),
        compiler_params=params(8),
        cost_estimate=cost(2.4e9, 6e6),
        name="relative",
    )(where, chain_lengths, table)
    where, relative, left, right = lax.optimization_barrier((where, relative, left, right))
    column_blocks = [
        narrow,
        right,
        left,
        send(right[:HALF], lambda y, x, z, c: (y, (x + 1) % 4, z, c)),
        send(left[HALF:], lambda y, x, z, c: (y, (x + 3) % 4, z, c)),
    ]
    relative, across, block = lax.optimization_barrier((relative, across, block))
    beside = send(block, lambda y, x, z, c: (y, x, z, c ^ 1))
    row_blocks = [block, beside, across, send(across, lambda y, x, z, c: (y, x, z, c ^ 1))]

    near = len(NEAR) * BLOCK
    near_outs = [
        shape((16, TILE), jnp.float32),
        shape((16, near), jnp.float32),
        *[shape((GROUP, TILE, near))] * 2,
    ]
    near_by_row, near_by_column, *near_lifted = pl.pallas_call(
        near_kernel,
        in_specs=[VMEM] * 7,
        out_specs=[VMEM] * len(near_outs),
        out_shape=near_outs,
        compiler_params=params(16),
        cost_estimate=cost(6e8, 11e6, 2e6),
        name="near",
    )(*row_blocks, *column_blocks[:3])
    near_by_row, *column_blocks[3:] = lax.optimization_barrier((near_by_row, *column_blocks[3:]))
    far_outs = [
        shape((16, TILE), jnp.float32),
        shape((8, TILE), jnp.float32),
        shape((16, TILE), jnp.float32),
        *[shape((GROUP, TILE, BLOCK))] * 2,
    ]
    by_row, far_top, by_column, *far_lifted = pl.pallas_call(
        far_kernel,
        in_specs=[SMEM] + [VMEM] * 8,
        out_specs=[VMEM] * len(far_outs),
        out_shape=far_outs,
        scratch_shapes=[pltpu.VMEM((16, BLOCK), jnp.float32)],
        compiler_params=params(12),
        cost_estimate=cost(3e8, 5e6, 7e5),
        name="far",
    )(where, *row_blocks, *column_blocks[3:], near_by_row, near_by_column)
    own_partial, right_partial, left_partial, far_partial = pl.pallas_call(
        partial_kernel,
        in_specs=[VMEM] * 6,
        out_specs=[VMEM] * 4,
        out_shape=[shape((WIDE, BLOCK))] * 4,
        compiler_params=params(12),
        cost_estimate=cost(3.4e8, 4e6),
        name="partials",
    )(*row_blocks, near_lifted[1], far_lifted[1])
    partials = [own_partial, left_partial, far_partial, right_partial]
    beside_by_row = send(by_row, lambda y, x, z, c: (y, x, z, c ^ 1))
    both_by_row = pl.pallas_call(
        merge_kernel,
        in_specs=[VMEM] * 2,
        out_specs=VMEM,
        out_shape=shape((16, TILE), jnp.float32),
        compiler_params=params(2),
        cost_estimate=cost(0, 1e5),
        name="merge",
    )(by_row, beside_by_row)
    row_stats = [both_by_row, send(both_by_row, lambda y, x, z, c: (y, x, z, c ^ 2))]
    column_stats = [by_column] + over_columns(by_column)

    where, *partials = lax.optimization_barrier((where, *partials))
    tiles = pl.pallas_call(
        symmetric_kernel,
        in_specs=[SMEM] + [VMEM] * 12,
        out_specs=HBM,
        out_shape=shape((8, GROUP, HALF, TILE)),
        scratch_shapes=[
            pltpu.VMEM((16, TILE), jnp.float32),
            pltpu.VMEM((8, GROUP, HALF, TILE), jnp.bfloat16),
            pltpu.SemaphoreType.DMA((8,)),
        ],
        compiler_params=params(8),
        cost_estimate=cost(1e7, 9e6),
        name="symmetric",
    )(
        where,
        *row_stats,
        *column_stats,
        near_by_row,
        far_top,
        *(part for parts in zip(near_lifted, far_lifted) for part in parts),
    )
    where, tiles = lax.optimization_barrier((where, tiles))
    groups = [[y * 8 + x * 2 + z for y in range(4) for z in range(2)] for x in range(4)]
    received = lax.all_to_all(
        tiles, "band", split_axis=0, concat_axis=0, axis_index_groups=groups, tiled=True
    ).reshape(8 * GROUP, HALF, TILE)

    same, other = pl.pallas_call(
        context_kernel,
        in_specs=[SMEM] + [VMEM] * 8,
        out_specs=[VMEM] * 2,
        out_shape=[shape((HALF, WIDE))] * 2,
        scratch_shapes=[vmem(BLOCK, WIDE)],
        compiler_params=params(4),
        cost_estimate=cost(1e6, 2e6),
        name="context",
    )(where, *column_stats, partials[0], *over_columns_of(partials))
    same = send(same, lambda y, x, z, c: (c, x, z, y))
    other = send(other, lambda y, x, z, c: (c, x, 1 - z, y))

    pair, context = pl.pallas_call(
        pair_kernel,
        grid=(HALF // ROWS,),
        in_specs=[
            SMEM,
            VMEM,
            pl.BlockSpec((hid * 8, 8 * GROUP * 8 + ONES), lambda i: (0, 0)),
            pl.BlockSpec((outs * 8, hid * 4), lambda i: (0, 0)),
            pl.BlockSpec((outs * 8, 128), lambda i: (0, 0)),
            pl.BlockSpec((outs, ROWS, TILE), lambda i: (0, i, 0)),
            pl.BlockSpec((HALF, WIDE), lambda i: (0, 0)),
            pl.BlockSpec((HALF, WIDE), lambda i: (0, 0)),
        ],
        out_specs=[
            pl.BlockSpec((outs, ROWS, TILE), lambda i: (0, i, 0)),
            pl.BlockSpec((HALF, 2 * WIDE), lambda i: (0, 0)),
        ],
        out_shape=[shape((outs, HALF, TILE)), shape((HALF, 2 * WIDE))],
        compiler_params=params(14),
        cost_estimate=cost(5e9, 14e6),
        name="pair",
    )(
        where,
        received,
        *(in_hbm(a) for a in (first, second, second_bias, relative, same, other)),
    )
    return (context, pair)


def solution(mesh):
    return jax.shard_map(
        local,
        mesh=mesh,
        in_specs=(
            P("band", "head"),
            P("band", "head"),
            P("band", "head"),
            P(),
            P(),
            P(),
            P(),
            P(),
            P(),
        ),
        out_specs=(P("band", "head"), P(None, "band", "head")),
        check_vma=False,
    )
```

```python
import functools
import itertools
import math

import jax
import jax.numpy as jnp
from jax import lax
from jax.experimental import pallas as pl
from jax.experimental.pallas import tpu as pltpu
from jax.sharding import PartitionSpec as P

HEAD_DIM = 128
CLIP = 32
GAP = 512
BINS = 65
GROUP = 5
WIDE = GROUP * HEAD_DIM
BLOCK = 128
HALF = 64
TILE = 512
NEAR, FAR = (0, 1, 3), 2
ROWS = 16
ONES = 16
SCALE = math.log2(math.e) / math.sqrt(HEAD_DIM)
AXES = ("head", "band")
MIB = 1 << 20


def device(y, x, z, c):
    return c * 32 + y * 8 + x * 2 + z


def moves(to):
    return [
        (device(y, x, z, c), device(*to(y, x, z, c)))
        for c, y, x, z in itertools.product(range(4), range(4), range(4), range(2))
    ]


def send(value, to):
    return lax.ppermute(value, AXES, moves(to))


def over_columns_of(values):
    return [send(values[d], lambda y, x, z, c, d=d: (y, (x + d) % 4, z, c)) for d in (1, 2, 3)]


def over_columns(value):
    return over_columns_of([value] * 4)


def nt(a, b):
    return lax.dot_general(a, b, (((1,), (1,)), ((), ())), preferred_element_type=jnp.float32)


def head(blocks, part, h):
    at = slice(part * WIDE + h * HEAD_DIM, part * WIDE + (h + 1) * HEAD_DIM)
    return jnp.concatenate([block[:, at] for block in blocks], axis=0)


def rows_of(rows, columns, lifted_out):
    lane = lax.broadcasted_iota(jnp.int32, (TILE, 128), 1)
    kept = jnp.zeros((TILE, 128), jnp.float32)
    for h in range(GROUP):
        scores = nt(head(rows, 0, h), head(columns, 1, h)) * SCALE
        top = jnp.max(scores, axis=1, keepdims=True)
        lifted = jnp.exp2(scores - top)
        lifted_out[h] = lifted.astype(jnp.bfloat16)
        kept = jnp.where(lane == h, top, kept)
        kept = jnp.where(lane == 8 + h, jnp.sum(lifted, axis=1, keepdims=True), kept)
    return jnp.transpose(kept)[0:16]


def place(x, d):
    return pl.ds(pl.multiple_of(lax.rem(x - d + 4, 4) * BLOCK, BLOCK), BLOCK)


def row_place(c, d):
    return pl.ds(pl.multiple_of(lax.bitwise_xor(c, d) * BLOCK, BLOCK), BLOCK)


def columns_of(rows, columns, by_column, lifted_out):
    by_column[...] = jnp.zeros_like(by_column)
    for h in range(GROUP):
        scores = nt(head(rows, 1, h), head(columns, 0, h)) * SCALE
        top = jnp.max(scores, axis=0, keepdims=True)
        lifted = jnp.exp2(scores - top)
        by_column[h : h + 1, :] = top
        by_column[8 + h : 9 + h, :] = jnp.sum(lifted, axis=0, keepdims=True)
        lifted_out[h] = lifted.astype(jnp.bfloat16)


def near_kernel(*refs):
    rows, columns = refs[0:4], refs[4:7]
    by_row, by_column, row_lifted, column_lifted = refs[7:]
    columns_of(rows, columns, by_column, column_lifted)
    by_row[...] = rows_of(rows, columns, row_lifted)


def far_kernel(where, *refs):
    rows, columns, near_by_row, near_by_column = refs[0:4], refs[4:6], refs[6], refs[7]
    by_row, top, by_column, row_lifted, column_lifted, own = refs[8:]
    x, c = where[1], where[3]
    columns_of(rows, columns, own, column_lifted)
    for i, d in enumerate(NEAR):
        by_column[:, place(x, d)] = near_by_column[:, i * BLOCK : (i + 1) * BLOCK]
    by_column[:, place(x, FAR)] = own[...]
    far_by_row = rows_of(rows, columns, row_lifted)
    tops = near_by_row[0:8], far_by_row[0:8]
    both = jnp.maximum(*tops)
    total = near_by_row[8:16] * jnp.exp2(tops[0] - both) + far_by_row[8:16] * jnp.exp2(
        tops[1] - both
    )
    top[...] = tops[1]
    for d in range(4):
        by_row[0:8, row_place(c, d)] = both[:, d * BLOCK : (d + 1) * BLOCK]
        by_row[8:16, row_place(c, d)] = total[:, d * BLOCK : (d + 1) * BLOCK]


def partial_kernel(*refs):
    values, lifted, outs = refs[0:4], refs[4:6], refs[6:10]
    for h in range(GROUP):
        at = slice(h * HEAD_DIM, (h + 1) * HEAD_DIM)
        own = head(values, 2, h)
        for half, held in zip(lifted, (outs[:3], outs[3:])):
            part = lax.dot_general(
                own, half[h], (((0,), (0,)), ((), ())), preferred_element_type=jnp.float32
            ).astype(jnp.bfloat16)
            for i, out in enumerate(held):
                out[at, :] = part[:, i * BLOCK : (i + 1) * BLOCK]


def merged(refs):
    top = functools.reduce(jnp.maximum, [ref[0:8, :] for ref in refs])
    return top, sum(ref[8:16, :] * jnp.exp2(ref[0:8, :] - top) for ref in refs)


def merge_kernel(one, other, both):
    both[0:8, :], both[8:16, :] = merged([one, other])


def turned(value):
    return jnp.transpose(jnp.concatenate([value] * 16, axis=0))


def symmetric_kernel(where, *refs):
    row_stats, column_stats = refs[0:2], refs[2:6]
    row_tops, row_lifted, column_lifted = refs[6:8], refs[8:10], refs[10:12]
    out, totals, held, sems = refs[12:]
    x, z, c = (where[i] for i in range(1, 4))
    totals[0:8, :], totals[8:16, :] = merged(row_stats)
    top, total = (
        jnp.concatenate([totals[at : at + 8, row_place(c, d)] for d in range(4)], axis=1)
        for at in (0, 8)
    )
    by_row = [turned(jnp.exp2(ref[0:8, :] - top) * (1024.0 / total)) for ref in row_tops]
    top, total = merged(column_stats)
    totals[0:8, :] = jnp.exp2(column_stats[0][0:8, :] - top) * (1024.0 / total)
    places = [place(x, d) for d in (*NEAR, FAR)]
    gains = [totals[0:8, at] for at in places]
    copies = []
    for p in range(8):
        owner = lax.bitwise_xor(c, p // 2) * 2 + p % 2
        here = slice(p * HALF, (p + 1) * HALF)
        for h in range(GROUP):
            for i, at in enumerate(places):
                part, block = divmod(i, len(NEAR))
                columns = slice(block * BLOCK, (block + 1) * BLOCK)
                held[p, h, :, at] = (
                    row_lifted[part][h, here, columns].astype(jnp.float32)
                    * by_row[part][here, h : h + 1]
                    + column_lifted[part][h, here, columns].astype(jnp.float32)
                    * gains[i][h : h + 1, :]
                ).astype(jnp.bfloat16)
        copies.append(pltpu.make_async_copy(held.at[p], out.at[owner], sems.at[p]))
        copies[p].start()
    for copy in copies:
        copy.wait()


def context_kernel(where, *refs):
    column_stats, partials = refs[0:4], refs[4:8]
    same, other, held = refs[8:]
    here = pl.ds(pl.multiple_of(where[1] * BLOCK, BLOCK), BLOCK)
    tops = [ref[0:8, here] for ref in column_stats]
    top = functools.reduce(jnp.maximum, tops)
    scales = [jnp.exp2(own - top) for own in tops]
    total = sum(ref[8:16, here] * scale for ref, scale in zip(column_stats, scales))
    scales = [scale / total for scale in scales]
    for h in range(GROUP):
        at = slice(h * HEAD_DIM, (h + 1) * HEAD_DIM)
        summed = sum(
            ref[at, :].astype(jnp.float32) * scale[h : h + 1, :]
            for ref, scale in zip(partials, scales)
        )
        held[:, at] = jnp.transpose(summed).astype(jnp.bfloat16)
    z = where[2]
    same[...] = held[pl.ds(pl.multiple_of(z * HALF, HALF), HALF), :]
    other[...] = held[pl.ds(pl.multiple_of((1 - z) * HALF, HALF), HALF), :]


def one_hot(indices, axis):
    return (indices == lax.broadcasted_iota(jnp.int32, indices.shape, axis)).astype(jnp.float32)


def expanded(matrix, row_of, row_lane, column_of, column_lane, left, right):
    k, m = matrix.shape
    one = one_hot(row_of(lax.broadcasted_iota(jnp.int32, (left, m), 0)), 1)
    tall = nt(one.astype(jnp.bfloat16), matrix).astype(jnp.bfloat16)
    one = one_hot(column_of(lax.broadcasted_iota(jnp.int32, (k, right), 1)), 0)
    wide = jnp.dot(tall, one.astype(jnp.bfloat16), preferred_element_type=jnp.float32)
    at_row = row_lane(lax.broadcasted_iota(jnp.int32, (left, right), 0))
    at_column = column_lane(lax.broadcasted_iota(jnp.int32, (left, right), 1))
    return jnp.where(at_row == at_column, wide, 0.0).astype(jnp.bfloat16)


def repeated(bias, row_of, left):
    one = one_hot(row_of(lax.broadcasted_iota(jnp.int32, (left, bias.shape[0]), 0)), 1)
    wide = jnp.broadcast_to(bias[...], (bias.shape[0], 128))
    return jnp.dot(one, wide, precision=lax.Precision.HIGHEST, preferred_element_type=jnp.float32)


def spread_kernel(
    first, first_bias, second, second_bias, table, first_out, second_out, second_bias_out, table_out
):
    by_eight, eight = lambda r: r // 8, lambda r: r % 8
    by_four, four = lambda r: r // 4, lambda r: r % 4
    hid, outs = first.shape[1], second.shape[1]
    channel = lambda r: r % (hid * 4) // 4
    width = first.shape[0] * 8
    first_out[:, :width] = expanded(
        first[...],
        channel,
        lambda r: r // (hid * 4) * 4 + r % 4,
        by_eight,
        eight,
        hid * 8,
        width,
    )
    rest, parts = repeated(first_bias, channel, hid * 8)[:, :ONES], []
    for _ in range(3):
        parts.append(rest.astype(jnp.bfloat16).astype(jnp.float32))
        rest = rest - parts[-1]
    lane = lax.broadcasted_iota(jnp.int32, (hid * 8, ONES), 1)
    first_out[:, width:] = sum(
        jnp.where(lane == i, part, 0.0) for i, part in enumerate(parts)
    ).astype(jnp.bfloat16)
    second_out[: outs * 4] = expanded(second[...], by_four, four, by_four, four, outs * 4, hid * 4)
    second_out[outs * 4 :] = expanded(
        second[...], lambda r: r // 4 + 1 - r // 4 % 2 * 2, four, by_four, four, outs * 4, hid * 4
    )
    second_bias_out[...] = repeated(second_bias, by_eight, outs * 8)
    table_out[...] = expanded(
        table[...], by_eight, eight, by_eight, eight, outs * 8, table_out.shape[1]
    )


def relative_kernel(where, lengths, table, out):
    ends = [lengths[0], lengths[0] + lengths[1], lengths[0] + lengths[1] + lengths[2]]

    def residue(positions):
        return positions + GAP * sum((positions >= end).astype(jnp.int32) for end in ends)

    band = where[0] * 8 + where[1] * 2 + where[2]
    first_row = band * HALF + pl.program_id(0) * ROWS
    levels = lax.broadcasted_iota(jnp.int32, (72, 8, TILE), 0)
    columns = residue(where[3] * TILE + lax.broadcasted_iota(jnp.int32, (8, TILE), 1))
    halves = []
    for half in range(ROWS // 8):
        rows = residue(first_row + half * 8 + lax.broadcasted_iota(jnp.int32, (8, TILE), 0))
        bins = jnp.clip(columns - rows, -CLIP, CLIP) + CLIP
        spread = (bins[None] == levels).astype(jnp.float32).reshape(72 * 8, TILE)
        part = jnp.dot(
            table[...], spread.astype(jnp.bfloat16), preferred_element_type=jnp.float32
        )
        halves.append(part.reshape(-1, 8, TILE))
    out[...] = jnp.concatenate(halves, axis=1).astype(jnp.bfloat16)


def pair_kernel(tiles, first, second, second_bias, relative, out):
    start = pl.multiple_of(pl.program_id(0) * ROWS, ROWS)
    loaded = tiles[:, pl.ds(start, ROWS), :].astype(jnp.float32)
    outs, hid = second.shape[0] // 8, first.shape[0] // 8
    upper = lax.broadcasted_iota(jnp.int32, (outs // 2, 8, TILE), 1) < 4
    ones = jnp.ones((ONES, TILE), jnp.bfloat16)
    halves = []
    for half in range(ROWS // 8):
        stacked = loaded[:, half * 8 : half * 8 + 8, :].reshape(-1, TILE).astype(jnp.bfloat16)
        stacked = jnp.concatenate([stacked, ones], axis=0)
        hidden = jnp.dot(first[...], stacked, preferred_element_type=jnp.float32)
        hidden = jnp.maximum(hidden, 0.0).astype(jnp.bfloat16)
        low, high = (
            jnp.dot(
                second[part * outs * 4 : (part + 1) * outs * 4],
                hidden[part * hid * 4 : (part + 1) * hid * 4],
                preferred_element_type=jnp.float32,
            ).reshape(outs // 2, 8, TILE)
            for part in range(2)
        )
        even = jnp.where(upper, low, high)
        odd = pltpu.roll(jnp.where(upper, high, low), 4, 1)
        projected = jnp.stack([even, odd], axis=1).reshape(outs, 8, TILE)
        halves.append(
            projected + jnp.concatenate([second_bias[...]] * 4, axis=1).reshape(outs, 8, TILE)
        )
    out[...] = (
        jnp.concatenate(halves, axis=1) + relative[...].astype(jnp.float32)
    ).astype(jnp.bfloat16)


SMEM = pl.BlockSpec(memory_space=pltpu.SMEM)
ANY = pl.BlockSpec(memory_space=pl.ANY)
HBM = pl.BlockSpec(memory_space=pltpu.HBM)
VMEM = pl.BlockSpec(memory_space=pltpu.VMEM)


def params(mib):
    return pltpu.CompilerParams(vmem_limit_bytes=mib * MIB)


def cost(flops, bytes_accessed, exponentials=0):
    return pl.CostEstimate(
        flops=int(flops), bytes_accessed=int(bytes_accessed), transcendentals=int(exponentials)
    )


def in_hbm(value):
    return pltpu.with_memory_space_constraint(value, pltpu.HBM)


def vmem(rows, columns):
    return pltpu.VMEM((rows, columns), jnp.bfloat16)


def shape(dims, kind=jnp.bfloat16):
    return jax.ShapeDtypeStruct(dims, kind)


def local(queries, keys, values, w_first, b_first, w_second, b_second, rel_table, chain_lengths):
    band, c = lax.axis_index("band"), lax.axis_index("head")
    y, x, z = band // 8, (band // 2) % 4, band % 2
    where = jnp.stack([y, x, z, c]).astype(jnp.int32)
    hid, outs = w_first.shape[1], w_second.shape[1]

    first, second, second_bias, table = pl.pallas_call(
        spread_kernel,
        in_specs=[VMEM] * 5,
        out_specs=[VMEM] * 4,
        out_shape=[
            pltpu.HBM((hid * 8, 8 * GROUP * 8 + ONES), jnp.bfloat16),
            pltpu.HBM((outs * 8, hid * 4), jnp.bfloat16),
            pltpu.HBM((outs * 8, 128), jnp.float32),
            shape((outs * 8, 72 * 8)),
        ],
        compiler_params=params(6),
        cost_estimate=cost(4e8, 6e6),
        name="spread",
    )(
        w_first,
        b_first[:, None],
        w_second,
        b_second[:, None],
        jnp.pad(rel_table, ((0, 72 - BINS), (0, 0))),
    )

    def half(at):
        near, far = (
            jnp.concatenate([a[:, lo : lo + WIDE] for a in (queries, keys, values)], axis=1)
            for lo in (0, WIDE)
        )
        return jnp.where(at == 0, near, far)

    crossing = half(1 - z)
    crossing, z = lax.optimization_barrier((crossing, z))
    other = send(crossing, lambda y, x, z, c: (c, x, 1 - z, y))
    same = send(half(z), lambda y, x, z, c: (c, x, z, y))
    block = jnp.where(
        z == 0,
        jnp.concatenate([same, other], axis=0),
        jnp.concatenate([other, same], axis=0),
    )

    block, first, second, second_bias, table = lax.optimization_barrier(
        (block, first, second, second_bias, table)
    )
    narrow = block[:, : 2 * WIDE]

    across = send(block, lambda y, x, z, c: (y, x, z, c ^ 2))
    right = send(narrow, lambda y, x, z, c: (y, (x + 1) % 4, z, c))
    left = send(narrow, lambda y, x, z, c: (y, (x + 3) % 4, z, c))
    relative = pl.pallas_call(
        relative_kernel,
        grid=(HALF // ROWS,),
        in_specs=[SMEM, SMEM, pl.BlockSpec((outs * 8, 72 * 8), lambda i: (0, 0))],
        out_specs=pl.BlockSpec((outs, ROWS, TILE), lambda i: (0, i, 0)),
        out_shape=pltpu.HBM((outs, HALF, TILE), jnp.bfloat16),
        compiler_params=params(8),
        cost_estimate=cost(2.4e9, 6e6),
        name="relative",
    )(where, chain_lengths, table)
    where, relative, left, right = lax.optimization_barrier((where, relative, left, right))
    column_blocks = [
        narrow,
        right,
        left,
        send(right[:HALF], lambda y, x, z, c: (y, (x + 1) % 4, z, c)),
        send(left[HALF:], lambda y, x, z, c: (y, (x + 3) % 4, z, c)),
    ]
    relative, across, block = lax.optimization_barrier((relative, across, block))
    beside = send(block, lambda y, x, z, c: (y, x, z, c ^ 1))
    row_blocks = [block, beside, across, send(across, lambda y, x, z, c: (y, x, z, c ^ 1))]

    near = len(NEAR) * BLOCK
    near_outs = [
        shape((16, TILE), jnp.float32),
        shape((16, near), jnp.float32),
        *[shape((GROUP, TILE, near))] * 2,
    ]
    near_by_row, near_by_column, *near_lifted = pl.pallas_call(
        near_kernel,
        in_specs=[VMEM] * 7,
        out_specs=[VMEM] * len(near_outs),
        out_shape=near_outs,
        compiler_params=params(16),
        cost_estimate=cost(6e8, 11e6, 2e6),
        name="near",
    )(*row_blocks, *column_blocks[:3])
    near_by_row, *column_blocks[3:] = lax.optimization_barrier((near_by_row, *column_blocks[3:]))
    far_outs = [
        shape((16, TILE), jnp.float32),
        shape((8, TILE), jnp.float32),
        shape((16, TILE), jnp.float32),
        *[shape((GROUP, TILE, BLOCK))] * 2,
    ]
    by_row, far_top, by_column, *far_lifted = pl.pallas_call(
        far_kernel,
        in_specs=[SMEM] + [VMEM] * 8,
        out_specs=[VMEM] * len(far_outs),
        out_shape=far_outs,
        scratch_shapes=[pltpu.VMEM((16, BLOCK), jnp.float32)],
        compiler_params=params(12),
        cost_estimate=cost(3e8, 5e6, 7e5),
        name="far",
    )(where, *row_blocks, *column_blocks[3:], near_by_row, near_by_column)
    own_partial, right_partial, left_partial, far_partial = pl.pallas_call(
        partial_kernel,
        in_specs=[VMEM] * 6,
        out_specs=[VMEM] * 4,
        out_shape=[shape((WIDE, BLOCK))] * 4,
        compiler_params=params(12),
        cost_estimate=cost(3.4e8, 4e6),
        name="partials",
    )(*row_blocks, near_lifted[1], far_lifted[1])
    partials = [own_partial, left_partial, far_partial, right_partial]
    beside_by_row = send(by_row, lambda y, x, z, c: (y, x, z, c ^ 1))
    both_by_row = pl.pallas_call(
        merge_kernel,
        in_specs=[VMEM] * 2,
        out_specs=VMEM,
        out_shape=shape((16, TILE), jnp.float32),
        compiler_params=params(2),
        cost_estimate=cost(0, 1e5),
        name="merge",
    )(by_row, beside_by_row)
    row_stats = [both_by_row, send(both_by_row, lambda y, x, z, c: (y, x, z, c ^ 2))]
    column_stats = [by_column] + over_columns(by_column)

    where, *partials = lax.optimization_barrier((where, *partials))
    tiles = pl.pallas_call(
        symmetric_kernel,
        in_specs=[SMEM] + [VMEM] * 12,
        out_specs=HBM,
        out_shape=shape((8, GROUP, HALF, TILE)),
        scratch_shapes=[
            pltpu.VMEM((16, TILE), jnp.float32),
            pltpu.VMEM((8, GROUP, HALF, TILE), jnp.bfloat16),
            pltpu.SemaphoreType.DMA((8,)),
        ],
        compiler_params=params(8),
        cost_estimate=cost(1e7, 9e6),
        name="symmetric",
    )(
        where,
        *row_stats,
        *column_stats,
        near_by_row,
        far_top,
        *(part for parts in zip(near_lifted, far_lifted) for part in parts),
    )
    where, tiles = lax.optimization_barrier((where, tiles))
    groups = [[y * 8 + x * 2 + z for y in range(4) for z in range(2)] for x in range(4)]
    received = lax.all_to_all(
        tiles, "band", split_axis=0, concat_axis=0, axis_index_groups=groups, tiled=True
    ).reshape(8 * GROUP, HALF, TILE)

    same, other = pl.pallas_call(
        context_kernel,
        in_specs=[SMEM] + [VMEM] * 8,
        out_specs=[VMEM] * 2,
        out_shape=[shape((HALF, WIDE))] * 2,
        scratch_shapes=[vmem(BLOCK, WIDE)],
        compiler_params=params(4),
        cost_estimate=cost(1e6, 2e6),
        name="context",
    )(where, *column_stats, partials[0], *over_columns_of(partials))
    same = send(same, lambda y, x, z, c: (c, x, z, y))
    other = send(other, lambda y, x, z, c: (c, x, 1 - z, y))

    pair = pl.pallas_call(
        pair_kernel,
        grid=(HALF // ROWS,),
        in_specs=[
            VMEM,
            pl.BlockSpec((hid * 8, 8 * GROUP * 8 + ONES), lambda i: (0, 0)),
            pl.BlockSpec((outs * 8, hid * 4), lambda i: (0, 0)),
            pl.BlockSpec((outs * 8, 128), lambda i: (0, 0)),
            pl.BlockSpec((outs, ROWS, TILE), lambda i: (0, i, 0)),
        ],
        out_specs=pl.BlockSpec((outs, ROWS, TILE), lambda i: (0, i, 0)),
        out_shape=shape((outs, HALF, TILE)),
        compiler_params=params(14),
        cost_estimate=cost(5e9, 14e6),
        name="pair",
    )(received, *(in_hbm(a) for a in (first, second, second_bias, relative)))
    same, other, pair = lax.optimization_barrier((same, other, pair))
    context = jnp.where(
        z == 0,
        jnp.concatenate([same, other], axis=1),
        jnp.concatenate([other, same], axis=1),
    )
    return (context, pair)


def solution(mesh):
    return jax.shard_map(
        local,
        mesh=mesh,
        in_specs=(
            P("band", "head"),
            P("band", "head"),
            P("band", "head"),
            P(),
            P(),
            P(),
            P(),
            P(),
            P(),
        ),
        out_specs=(P("band", "head"), P(None, "band", "head")),
        check_vma=False,
    )
```

```python
import functools
import itertools
import math

import jax
import jax.numpy as jnp
from jax import lax
from jax.experimental import pallas as pl
from jax.experimental.pallas import tpu as pltpu
from jax.sharding import PartitionSpec as P

HEAD_DIM = 128
CLIP = 32
GAP = 512
BINS = 65
GROUP = 5
WIDE = GROUP * HEAD_DIM
BLOCK = 128
HALF = 64
TILE = 512
NEAR, FAR = (0, 1, 3), 2
ROWS = 16
ONES = 16
SCALE = math.log2(math.e) / math.sqrt(HEAD_DIM)
AXES = ("head", "band")
MIB = 1 << 20


def device(y, x, z, c):
    return c * 32 + y * 8 + x * 2 + z


def moves(to):
    return [
        (device(y, x, z, c), device(*to(y, x, z, c)))
        for c, y, x, z in itertools.product(range(4), range(4), range(4), range(2))
    ]


def send(value, to):
    return lax.ppermute(value, AXES, moves(to))


def over_columns_of(values):
    return [send(values[d], lambda y, x, z, c, d=d: (y, (x + d) % 4, z, c)) for d in (1, 2, 3)]


def over_columns(value):
    return over_columns_of([value] * 4)


def nt(a, b):
    return lax.dot_general(a, b, (((1,), (1,)), ((), ())), preferred_element_type=jnp.float32)


def head(blocks, part, h):
    at = slice(part * WIDE + h * HEAD_DIM, part * WIDE + (h + 1) * HEAD_DIM)
    return jnp.concatenate([block[:, at] for block in blocks], axis=0)


def rows_of(rows, columns, lifted_out):
    lane = lax.broadcasted_iota(jnp.int32, (TILE, 128), 1)
    kept = jnp.zeros((TILE, 128), jnp.float32)
    for h in range(GROUP):
        scores = nt(head(rows, 0, h), head(columns, 1, h)) * SCALE
        top = jnp.max(scores, axis=1, keepdims=True)
        lifted = jnp.exp2(scores - top)
        lifted_out[h] = lifted.astype(jnp.bfloat16)
        kept = jnp.where(lane == h, top, kept)
        kept = jnp.where(lane == 8 + h, jnp.sum(lifted, axis=1, keepdims=True), kept)
    return jnp.transpose(kept)[0:16]


def place(x, d):
    return pl.ds(pl.multiple_of(lax.rem(x - d + 4, 4) * BLOCK, BLOCK), BLOCK)


def row_place(c, d):
    return pl.ds(pl.multiple_of(lax.bitwise_xor(c, d) * BLOCK, BLOCK), BLOCK)


def columns_of(rows, columns, by_column, lifted_out):
    by_column[...] = jnp.zeros_like(by_column)
    for h in range(GROUP):
        scores = nt(head(rows, 1, h), head(columns, 0, h)) * SCALE
        top = jnp.max(scores, axis=0, keepdims=True)
        lifted = jnp.exp2(scores - top)
        by_column[h : h + 1, :] = top
        by_column[8 + h : 9 + h, :] = jnp.sum(lifted, axis=0, keepdims=True)
        lifted_out[h] = lifted.astype(jnp.bfloat16)


def near_kernel(*refs):
    rows, columns = refs[0:4], refs[4:7]
    by_row, by_column, row_lifted, column_lifted = refs[7:]
    columns_of(rows, columns, by_column, column_lifted)
    by_row[...] = rows_of(rows, columns, row_lifted)


def far_kernel(where, *refs):
    rows, columns, near_by_row, near_by_column = refs[0:4], refs[4:6], refs[6], refs[7]
    by_row, top, by_column, row_lifted, column_lifted, own = refs[8:]
    x, c = where[1], where[3]
    columns_of(rows, columns, own, column_lifted)
    for i, d in enumerate(NEAR):
        by_column[:, place(x, d)] = near_by_column[:, i * BLOCK : (i + 1) * BLOCK]
    by_column[:, place(x, FAR)] = own[...]
    far_by_row = rows_of(rows, columns, row_lifted)
    tops = near_by_row[0:8], far_by_row[0:8]
    both = jnp.maximum(*tops)
    total = near_by_row[8:16] * jnp.exp2(tops[0] - both) + far_by_row[8:16] * jnp.exp2(
        tops[1] - both
    )
    top[...] = tops[1]
    for d in range(4):
        by_row[0:8, row_place(c, d)] = both[:, d * BLOCK : (d + 1) * BLOCK]
        by_row[8:16, row_place(c, d)] = total[:, d * BLOCK : (d + 1) * BLOCK]


def partial_kernel(*refs):
    values, lifted, outs = refs[0:4], refs[4:6], refs[6:10]
    for h in range(GROUP):
        at = slice(h * HEAD_DIM, (h + 1) * HEAD_DIM)
        own = head(values, 2, h)
        for half, held in zip(lifted, (outs[:3], outs[3:])):
            part = lax.dot_general(
                own, half[h], (((0,), (0,)), ((), ())), preferred_element_type=jnp.float32
            ).astype(jnp.bfloat16)
            for i, out in enumerate(held):
                out[at, :] = part[:, i * BLOCK : (i + 1) * BLOCK]


def merged(refs):
    top = functools.reduce(jnp.maximum, [ref[0:8, :] for ref in refs])
    return top, sum(ref[8:16, :] * jnp.exp2(ref[0:8, :] - top) for ref in refs)


def merge_kernel(one, other, both):
    both[0:8, :], both[8:16, :] = merged([one, other])


def turned(value):
    return jnp.transpose(jnp.concatenate([value] * 8, axis=0))


def symmetric_kernel(where, *refs):
    row_stats, column_stats = refs[0:2], refs[2:6]
    row_tops, row_lifted, column_lifted = refs[6:8], refs[8:10], refs[10:12]
    out, totals, held, sems = refs[12:]
    x, z, c = (where[i] for i in range(1, 4))
    totals[0:8, :], totals[8:16, :] = merged(row_stats)
    top, total = (
        jnp.concatenate([totals[at : at + 8, row_place(c, d)] for d in range(4)], axis=1)
        for at in (0, 8)
    )
    gain = 1024.0 / total
    by_row = turned(
        jnp.concatenate([jnp.exp2(ref[0:8, :] - top) * gain for ref in row_tops], axis=0)
    )
    top, total = merged(column_stats)
    totals[0:8, :] = jnp.exp2(column_stats[0][0:8, :] - top) * (1024.0 / total)
    places = [place(x, d) for d in (*NEAR, FAR)]
    gains = [totals[0:8, at] for at in places]
    copies = []
    for p in range(8):
        owner = lax.bitwise_xor(c, p // 2) * 2 + p % 2
        here = slice(p * HALF, (p + 1) * HALF)
        for h in range(GROUP):
            for i, at in enumerate(places):
                part, block = divmod(i, len(NEAR))
                columns = slice(block * BLOCK, (block + 1) * BLOCK)
                held[p, h, :, at] = (
                    row_lifted[part][h, here, columns].astype(jnp.float32)
                    * by_row[here, part * 8 + h : part * 8 + h + 1]
                    + column_lifted[part][h, here, columns].astype(jnp.float32)
                    * gains[i][h : h + 1, :]
                ).astype(jnp.bfloat16)
        copies.append(pltpu.make_async_copy(held.at[p], out.at[owner], sems.at[p]))
        copies[p].start()
    for copy in copies:
        copy.wait()


def context_kernel(where, *refs):
    column_stats, partials = refs[0:4], refs[4:8]
    same, other, held = refs[8:]
    here = pl.ds(pl.multiple_of(where[1] * BLOCK, BLOCK), BLOCK)
    tops = [ref[0:8, here] for ref in column_stats]
    top = functools.reduce(jnp.maximum, tops)
    scales = [jnp.exp2(own - top) for own in tops]
    total = sum(ref[8:16, here] * scale for ref, scale in zip(column_stats, scales))
    scales = [scale / total for scale in scales]
    for h in range(GROUP):
        at = slice(h * HEAD_DIM, (h + 1) * HEAD_DIM)
        summed = sum(
            ref[at, :].astype(jnp.float32) * scale[h : h + 1, :]
            for ref, scale in zip(partials, scales)
        )
        held[:, at] = jnp.transpose(summed).astype(jnp.bfloat16)
    z = where[2]
    same[...] = held[pl.ds(pl.multiple_of(z * HALF, HALF), HALF), :]
    other[...] = held[pl.ds(pl.multiple_of((1 - z) * HALF, HALF), HALF), :]


def one_hot(indices, axis):
    return (indices == lax.broadcasted_iota(jnp.int32, indices.shape, axis)).astype(jnp.float32)


def expanded(matrix, row_of, row_lane, column_of, column_lane, left, right):
    k, m = matrix.shape
    one = one_hot(row_of(lax.broadcasted_iota(jnp.int32, (left, m), 0)), 1)
    tall = nt(one.astype(jnp.bfloat16), matrix).astype(jnp.bfloat16)
    one = one_hot(column_of(lax.broadcasted_iota(jnp.int32, (k, right), 1)), 0)
    wide = jnp.dot(tall, one.astype(jnp.bfloat16), preferred_element_type=jnp.float32)
    at_row = row_lane(lax.broadcasted_iota(jnp.int32, (left, right), 0))
    at_column = column_lane(lax.broadcasted_iota(jnp.int32, (left, right), 1))
    return jnp.where(at_row == at_column, wide, 0.0).astype(jnp.bfloat16)


def repeated(bias, row_of, left):
    one = one_hot(row_of(lax.broadcasted_iota(jnp.int32, (left, bias.shape[0]), 0)), 1)
    wide = jnp.broadcast_to(bias[...], (bias.shape[0], 128))
    return jnp.dot(one, wide, precision=lax.Precision.HIGHEST, preferred_element_type=jnp.float32)


def spread_kernel(
    first, first_bias, second, second_bias, table, first_out, second_out, second_bias_out, table_out
):
    by_eight, eight = lambda r: r // 8, lambda r: r % 8
    by_four, four = lambda r: r // 4, lambda r: r % 4
    hid, outs = first.shape[1], second.shape[1]
    channel = lambda r: r % (hid * 4) // 4
    width = first.shape[0] * 8
    first_out[:, :width] = expanded(
        first[...],
        channel,
        lambda r: r // (hid * 4) * 4 + r % 4,
        by_eight,
        eight,
        hid * 8,
        width,
    )
    rest, parts = repeated(first_bias, channel, hid * 8)[:, :ONES], []
    for _ in range(3):
        parts.append(rest.astype(jnp.bfloat16).astype(jnp.float32))
        rest = rest - parts[-1]
    lane = lax.broadcasted_iota(jnp.int32, (hid * 8, ONES), 1)
    first_out[:, width:] = sum(
        jnp.where(lane == i, part, 0.0) for i, part in enumerate(parts)
    ).astype(jnp.bfloat16)
    second_out[: outs * 4] = expanded(second[...], by_four, four, by_four, four, outs * 4, hid * 4)
    second_out[outs * 4 :] = expanded(
        second[...], lambda r: r // 4 + 1 - r // 4 % 2 * 2, four, by_four, four, outs * 4, hid * 4
    )
    second_bias_out[...] = repeated(second_bias, by_eight, outs * 8)
    table_out[...] = expanded(
        table[...], by_eight, eight, by_eight, eight, outs * 8, table_out.shape[1]
    )


def relative_kernel(where, lengths, table, out):
    ends = [lengths[0], lengths[0] + lengths[1], lengths[0] + lengths[1] + lengths[2]]

    def residue(positions):
        return positions + GAP * sum((positions >= end).astype(jnp.int32) for end in ends)

    band = where[0] * 8 + where[1] * 2 + where[2]
    first_row = band * HALF + pl.program_id(0) * ROWS
    levels = lax.broadcasted_iota(jnp.int32, (72, 8, TILE), 0)
    columns = residue(where[3] * TILE + lax.broadcasted_iota(jnp.int32, (8, TILE), 1))
    halves = []
    for half in range(ROWS // 8):
        rows = residue(first_row + half * 8 + lax.broadcasted_iota(jnp.int32, (8, TILE), 0))
        bins = jnp.clip(columns - rows, -CLIP, CLIP) + CLIP
        spread = (bins[None] == levels).astype(jnp.float32).reshape(72 * 8, TILE)
        part = jnp.dot(
            table[...], spread.astype(jnp.bfloat16), preferred_element_type=jnp.float32
        )
        halves.append(part.reshape(-1, 8, TILE))
    out[...] = jnp.concatenate(halves, axis=1).astype(jnp.bfloat16)


def pair_kernel(tiles, first, second, second_bias, relative, out):
    start = pl.multiple_of(pl.program_id(0) * ROWS, ROWS)
    loaded = tiles[:, pl.ds(start, ROWS), :].astype(jnp.float32)
    outs, hid = second.shape[0] // 8, first.shape[0] // 8
    upper = lax.broadcasted_iota(jnp.int32, (outs // 2, 8, TILE), 1) < 4
    ones = jnp.ones((ONES, TILE), jnp.bfloat16)
    halves = []
    for half in range(ROWS // 8):
        stacked = loaded[:, half * 8 : half * 8 + 8, :].reshape(-1, TILE).astype(jnp.bfloat16)
        stacked = jnp.concatenate([stacked, ones], axis=0)
        hidden = jnp.dot(first[...], stacked, preferred_element_type=jnp.float32)
        hidden = jnp.maximum(hidden, 0.0).astype(jnp.bfloat16)
        low, high = (
            jnp.dot(
                second[part * outs * 4 : (part + 1) * outs * 4],
                hidden[part * hid * 4 : (part + 1) * hid * 4],
                preferred_element_type=jnp.float32,
            ).reshape(outs // 2, 8, TILE)
            for part in range(2)
        )
        even = jnp.where(upper, low, high)
        odd = pltpu.roll(jnp.where(upper, high, low), 4, 1)
        projected = jnp.stack([even, odd], axis=1).reshape(outs, 8, TILE)
        halves.append(
            projected + jnp.concatenate([second_bias[...]] * 4, axis=1).reshape(outs, 8, TILE)
        )
    out[...] = (
        jnp.concatenate(halves, axis=1) + relative[...].astype(jnp.float32)
    ).astype(jnp.bfloat16)


SMEM = pl.BlockSpec(memory_space=pltpu.SMEM)
ANY = pl.BlockSpec(memory_space=pl.ANY)
HBM = pl.BlockSpec(memory_space=pltpu.HBM)
VMEM = pl.BlockSpec(memory_space=pltpu.VMEM)


def params(mib):
    return pltpu.CompilerParams(vmem_limit_bytes=mib * MIB)


def cost(flops, bytes_accessed, exponentials=0):
    return pl.CostEstimate(
        flops=int(flops), bytes_accessed=int(bytes_accessed), transcendentals=int(exponentials)
    )


def in_hbm(value):
    return pltpu.with_memory_space_constraint(value, pltpu.HBM)


def vmem(rows, columns):
    return pltpu.VMEM((rows, columns), jnp.bfloat16)


def shape(dims, kind=jnp.bfloat16):
    return jax.ShapeDtypeStruct(dims, kind)


def local(queries, keys, values, w_first, b_first, w_second, b_second, rel_table, chain_lengths):
    band, c = lax.axis_index("band"), lax.axis_index("head")
    y, x, z = band // 8, (band // 2) % 4, band % 2
    where = jnp.stack([y, x, z, c]).astype(jnp.int32)
    hid, outs = w_first.shape[1], w_second.shape[1]

    first, second, second_bias, table = pl.pallas_call(
        spread_kernel,
        in_specs=[VMEM] * 5,
        out_specs=[VMEM] * 4,
        out_shape=[
            pltpu.HBM((hid * 8, 8 * GROUP * 8 + ONES), jnp.bfloat16),
            pltpu.HBM((outs * 8, hid * 4), jnp.bfloat16),
            pltpu.HBM((outs * 8, 128), jnp.float32),
            shape((outs * 8, 72 * 8)),
        ],
        compiler_params=params(6),
        cost_estimate=cost(4e8, 6e6),
        name="spread",
    )(
        w_first,
        b_first[:, None],
        w_second,
        b_second[:, None],
        jnp.pad(rel_table, ((0, 72 - BINS), (0, 0))),
    )

    def half(at):
        near, far = (
            jnp.concatenate([a[:, lo : lo + WIDE] for a in (queries, keys, values)], axis=1)
            for lo in (0, WIDE)
        )
        return jnp.where(at == 0, near, far)

    crossing = half(1 - z)
    crossing, z = lax.optimization_barrier((crossing, z))
    other = send(crossing, lambda y, x, z, c: (c, x, 1 - z, y))
    same = send(half(z), lambda y, x, z, c: (c, x, z, y))
    block = jnp.where(
        z == 0,
        jnp.concatenate([same, other], axis=0),
        jnp.concatenate([other, same], axis=0),
    )

    block, first, second, second_bias, table = lax.optimization_barrier(
        (block, first, second, second_bias, table)
    )
    narrow = block[:, : 2 * WIDE]

    across = send(block, lambda y, x, z, c: (y, x, z, c ^ 2))
    right = send(narrow, lambda y, x, z, c: (y, (x + 1) % 4, z, c))
    left = send(narrow, lambda y, x, z, c: (y, (x + 3) % 4, z, c))
    relative = pl.pallas_call(
        relative_kernel,
        grid=(HALF // ROWS,),
        in_specs=[SMEM, SMEM, pl.BlockSpec((outs * 8, 72 * 8), lambda i: (0, 0))],
        out_specs=pl.BlockSpec((outs, ROWS, TILE), lambda i: (0, i, 0)),
        out_shape=pltpu.HBM((outs, HALF, TILE), jnp.bfloat16),
        compiler_params=params(8),
        cost_estimate=cost(2.4e9, 6e6),
        name="relative",
    )(where, chain_lengths, table)
    where, relative, left, right = lax.optimization_barrier((where, relative, left, right))
    column_blocks = [
        narrow,
        right,
        left,
        send(right[:HALF], lambda y, x, z, c: (y, (x + 1) % 4, z, c)),
        send(left[HALF:], lambda y, x, z, c: (y, (x + 3) % 4, z, c)),
    ]
    relative, across, block = lax.optimization_barrier((relative, across, block))
    beside = send(block, lambda y, x, z, c: (y, x, z, c ^ 1))
    row_blocks = [block, beside, across, send(across, lambda y, x, z, c: (y, x, z, c ^ 1))]

    near = len(NEAR) * BLOCK
    near_outs = [
        shape((16, TILE), jnp.float32),
        shape((16, near), jnp.float32),
        *[shape((GROUP, TILE, near))] * 2,
    ]
    near_by_row, near_by_column, *near_lifted = pl.pallas_call(
        near_kernel,
        in_specs=[VMEM] * 7,
        out_specs=[VMEM] * len(near_outs),
        out_shape=near_outs,
        compiler_params=params(16),
        cost_estimate=cost(6e8, 11e6, 2e6),
        name="near",
    )(*row_blocks, *column_blocks[:3])
    near_by_row, *column_blocks[3:] = lax.optimization_barrier((near_by_row, *column_blocks[3:]))
    far_outs = [
        shape((16, TILE), jnp.float32),
        shape((8, TILE), jnp.float32),
        shape((16, TILE), jnp.float32),
        *[shape((GROUP, TILE, BLOCK))] * 2,
    ]
    by_row, far_top, by_column, *far_lifted = pl.pallas_call(
        far_kernel,
        in_specs=[SMEM] + [VMEM] * 8,
        out_specs=[VMEM] * len(far_outs),
        out_shape=far_outs,
        scratch_shapes=[pltpu.VMEM((16, BLOCK), jnp.float32)],
        compiler_params=params(12),
        cost_estimate=cost(3e8, 5e6, 7e5),
        name="far",
    )(where, *row_blocks, *column_blocks[3:], near_by_row, near_by_column)
    own_partial, right_partial, left_partial, far_partial = pl.pallas_call(
        partial_kernel,
        in_specs=[VMEM] * 6,
        out_specs=[VMEM] * 4,
        out_shape=[shape((WIDE, BLOCK))] * 4,
        compiler_params=params(12),
        cost_estimate=cost(3.4e8, 4e6),
        name="partials",
    )(*row_blocks, near_lifted[1], far_lifted[1])
    partials = [own_partial, left_partial, far_partial, right_partial]
    beside_by_row = send(by_row, lambda y, x, z, c: (y, x, z, c ^ 1))
    both_by_row = pl.pallas_call(
        merge_kernel,
        in_specs=[VMEM] * 2,
        out_specs=VMEM,
        out_shape=shape((16, TILE), jnp.float32),
        compiler_params=params(2),
        cost_estimate=cost(0, 1e5),
        name="merge",
    )(by_row, beside_by_row)
    row_stats = [both_by_row, send(both_by_row, lambda y, x, z, c: (y, x, z, c ^ 2))]
    column_stats = [by_column] + over_columns(by_column)

    where, *partials = lax.optimization_barrier((where, *partials))
    tiles = pl.pallas_call(
        symmetric_kernel,
        in_specs=[SMEM] + [VMEM] * 12,
        out_specs=HBM,
        out_shape=shape((8, GROUP, HALF, TILE)),
        scratch_shapes=[
            pltpu.VMEM((16, TILE), jnp.float32),
            pltpu.VMEM((8, GROUP, HALF, TILE), jnp.bfloat16),
            pltpu.SemaphoreType.DMA((8,)),
        ],
        compiler_params=params(8),
        cost_estimate=cost(1e7, 9e6),
        name="symmetric",
    )(
        where,
        *row_stats,
        *column_stats,
        near_by_row,
        far_top,
        *(part for parts in zip(near_lifted, far_lifted) for part in parts),
    )
    where, tiles = lax.optimization_barrier((where, tiles))
    groups = [[y * 8 + x * 2 + z for y in range(4) for z in range(2)] for x in range(4)]
    received = lax.all_to_all(
        tiles, "band", split_axis=0, concat_axis=0, axis_index_groups=groups, tiled=True
    ).reshape(8 * GROUP, HALF, TILE)

    same, other = pl.pallas_call(
        context_kernel,
        in_specs=[SMEM] + [VMEM] * 8,
        out_specs=[VMEM] * 2,
        out_shape=[shape((HALF, WIDE))] * 2,
        scratch_shapes=[vmem(BLOCK, WIDE)],
        compiler_params=params(4),
        cost_estimate=cost(1e6, 2e6),
        name="context",
    )(where, *column_stats, partials[0], *over_columns_of(partials))
    same = send(same, lambda y, x, z, c: (c, x, z, y))
    other = send(other, lambda y, x, z, c: (c, x, 1 - z, y))

    pair = pl.pallas_call(
        pair_kernel,
        grid=(HALF // ROWS,),
        in_specs=[
            VMEM,
            pl.BlockSpec((hid * 8, 8 * GROUP * 8 + ONES), lambda i: (0, 0)),
            pl.BlockSpec((outs * 8, hid * 4), lambda i: (0, 0)),
            pl.BlockSpec((outs * 8, 128), lambda i: (0, 0)),
            pl.BlockSpec((outs, ROWS, TILE), lambda i: (0, i, 0)),
        ],
        out_specs=pl.BlockSpec((outs, ROWS, TILE), lambda i: (0, i, 0)),
        out_shape=shape((outs, HALF, TILE)),
        compiler_params=params(14),
        cost_estimate=cost(5e9, 14e6),
        name="pair",
    )(received, *(in_hbm(a) for a in (first, second, second_bias, relative)))
    same, other, pair = lax.optimization_barrier((same, other, pair))
    context = jnp.where(
        z == 0,
        jnp.concatenate([same, other], axis=1),
        jnp.concatenate([other, same], axis=1),
    )
    return (context, pair)


def solution(mesh):
    return jax.shard_map(
        local,
        mesh=mesh,
        in_specs=(
            P("band", "head"),
            P("band", "head"),
            P("band", "head"),
            P(),
            P(),
            P(),
            P(),
            P(),
            P(),
        ),
        out_specs=(P("band", "head"), P(None, "band", "head")),
        check_vma=False,
    )
```

```python
import functools
import itertools
import math

import jax
import jax.numpy as jnp
from jax import lax
from jax.experimental import pallas as pl
from jax.experimental.pallas import tpu as pltpu
from jax.sharding import PartitionSpec as P

HEAD_DIM = 128
CLIP = 32
GAP = 512
BINS = 65
GROUP = 5
WIDE = GROUP * HEAD_DIM
BLOCK = 128
HALF = 64
TILE = 512
NEAR, FAR = (0, 1, 3), 2
ROWS = 16
ONES = 16
SCALE = math.log2(math.e) / math.sqrt(HEAD_DIM)
AXES = ("head", "band")
MIB = 1 << 20


def device(y, x, z, c):
    return c * 32 + y * 8 + x * 2 + z


def moves(to):
    return [
        (device(y, x, z, c), device(*to(y, x, z, c)))
        for c, y, x, z in itertools.product(range(4), range(4), range(4), range(2))
    ]


def send(value, to):
    return lax.ppermute(value, AXES, moves(to))


def over_columns_of(values):
    return [send(values[d], lambda y, x, z, c, d=d: (y, (x + d) % 4, z, c)) for d in (1, 2, 3)]


def over_columns(value):
    return over_columns_of([value] * 4)


def nt(a, b):
    return lax.dot_general(a, b, (((1,), (1,)), ((), ())), preferred_element_type=jnp.float32)


def head(blocks, part, h):
    at = slice(part * WIDE + h * HEAD_DIM, part * WIDE + (h + 1) * HEAD_DIM)
    return jnp.concatenate([block[:, at] for block in blocks], axis=0)


def rows_of(rows, columns, lifted_out):
    lane = lax.broadcasted_iota(jnp.int32, (TILE, 128), 1)
    kept = jnp.zeros((TILE, 128), jnp.float32)
    for h in range(GROUP):
        scores = nt(head(rows, 0, h), head(columns, 1, h)) * SCALE
        top = jnp.max(scores, axis=1, keepdims=True)
        lifted = jnp.exp2(scores - top)
        lifted_out[h] = lifted.astype(jnp.bfloat16)
        kept = jnp.where(lane == h, top, kept)
        kept = jnp.where(lane == 8 + h, jnp.sum(lifted, axis=1, keepdims=True), kept)
    return jnp.transpose(kept)[0:16]


def place(x, d):
    return pl.ds(pl.multiple_of(lax.rem(x - d + 4, 4) * BLOCK, BLOCK), BLOCK)


def row_place(c, d):
    return pl.ds(pl.multiple_of(lax.bitwise_xor(c, d) * BLOCK, BLOCK), BLOCK)


def columns_of(rows, columns, by_column, lifted_out):
    by_column[...] = jnp.zeros_like(by_column)
    for h in range(GROUP):
        scores = nt(head(rows, 1, h), head(columns, 0, h)) * SCALE
        top = jnp.max(scores, axis=0, keepdims=True)
        lifted = jnp.exp2(scores - top)
        by_column[h : h + 1, :] = top
        by_column[8 + h : 9 + h, :] = jnp.sum(lifted, axis=0, keepdims=True)
        lifted_out[h] = lifted.astype(jnp.bfloat16)


def near_kernel(*refs):
    rows, columns = refs[0:4], refs[4:7]
    by_row, by_column, row_lifted, column_lifted = refs[7:]
    columns_of(rows, columns, by_column, column_lifted)
    by_row[...] = rows_of(rows, columns, row_lifted)


def far_kernel(where, *refs):
    rows, columns, near_by_row, near_by_column = refs[0:4], refs[4:6], refs[6], refs[7]
    by_row, top, by_column, row_lifted, column_lifted, own = refs[8:]
    x, c = where[1], where[3]
    columns_of(rows, columns, own, column_lifted)
    for i, d in enumerate(NEAR):
        by_column[:, place(x, d)] = near_by_column[:, i * BLOCK : (i + 1) * BLOCK]
    by_column[:, place(x, FAR)] = own[...]
    far_by_row = rows_of(rows, columns, row_lifted)
    tops = near_by_row[0:8], far_by_row[0:8]
    both = jnp.maximum(*tops)
    total = near_by_row[8:16] * jnp.exp2(tops[0] - both) + far_by_row[8:16] * jnp.exp2(
        tops[1] - both
    )
    top[...] = tops[1]
    for d in range(4):
        by_row[0:8, row_place(c, d)] = both[:, d * BLOCK : (d + 1) * BLOCK]
        by_row[8:16, row_place(c, d)] = total[:, d * BLOCK : (d + 1) * BLOCK]


def partial_kernel(*refs):
    values, lifted, outs = refs[0:4], refs[4:6], refs[6:10]
    for h in range(GROUP):
        at = slice(h * HEAD_DIM, (h + 1) * HEAD_DIM)
        own = head(values, 2, h)
        for half, held in zip(lifted, (outs[:3], outs[3:])):
            part = lax.dot_general(
                own, half[h], (((0,), (0,)), ((), ())), preferred_element_type=jnp.float32
            ).astype(jnp.bfloat16)
            for i, out in enumerate(held):
                out[at, :] = part[:, i * BLOCK : (i + 1) * BLOCK]


def merged(refs):
    top = functools.reduce(jnp.maximum, [ref[0:8, :] for ref in refs])
    return top, sum(ref[8:16, :] * jnp.exp2(ref[0:8, :] - top) for ref in refs)


def merge_kernel(one, other, both):
    both[0:8, :], both[8:16, :] = merged([one, other])


def turned(value):
    return jnp.transpose(jnp.concatenate([value] * 16, axis=0))


def symmetric_kernel(where, *refs):
    row_stats, column_stats = refs[0:2], refs[2:6]
    row_tops, row_lifted, column_lifted = refs[6:8], refs[8:10], refs[10:12]
    out, totals, held, sems = refs[12:]
    x, z, c = (where[i] for i in range(1, 4))
    totals[0:8, :], totals[8:16, :] = merged(row_stats)
    top, total = (
        jnp.concatenate([totals[at : at + 8, row_place(c, d)] for d in range(4)], axis=1)
        for at in (0, 8)
    )
    by_row = [turned(jnp.exp2(ref[0:8, :] - top) * (1024.0 / total)) for ref in row_tops]
    top, total = merged(column_stats)
    totals[0:8, :] = jnp.exp2(column_stats[0][0:8, :] - top) * (1024.0 / total)
    places = [place(x, d) for d in (*NEAR, FAR)]
    gains = [totals[0:8, at] for at in places]
    copies = []
    for p in range(8):
        owner = lax.bitwise_xor(c, p // 2) * 2 + p % 2
        here = slice(p * HALF, (p + 1) * HALF)
        for h in range(GROUP):
            for i, at in enumerate(places):
                part, block = divmod(i, len(NEAR))
                columns = slice(block * BLOCK, (block + 1) * BLOCK)
                row_gain, column_gain = (
                    jnp.broadcast_to(gain, (HALF, BLOCK)).astype(jnp.bfloat16)
                    for gain in (by_row[part][here, h : h + 1], gains[i][h : h + 1, :])
                )
                held[p, h, :, at] = (
                    row_lifted[part][h, here, columns] * row_gain
                    + column_lifted[part][h, here, columns] * column_gain
                )
        copies.append(pltpu.make_async_copy(held.at[p], out.at[owner], sems.at[p]))
        copies[p].start()
    for copy in copies:
        copy.wait()


def context_kernel(where, *refs):
    column_stats, partials = refs[0:4], refs[4:8]
    same, other, held = refs[8:]
    here = pl.ds(pl.multiple_of(where[1] * BLOCK, BLOCK), BLOCK)
    tops = [ref[0:8, here] for ref in column_stats]
    top = functools.reduce(jnp.maximum, tops)
    scales = [jnp.exp2(own - top) for own in tops]
    total = sum(ref[8:16, here] * scale for ref, scale in zip(column_stats, scales))
    scales = [scale / total for scale in scales]
    for h in range(GROUP):
        at = slice(h * HEAD_DIM, (h + 1) * HEAD_DIM)
        summed = sum(
            ref[at, :].astype(jnp.float32) * scale[h : h + 1, :]
            for ref, scale in zip(partials, scales)
        )
        held[:, at] = jnp.transpose(summed).astype(jnp.bfloat16)
    z = where[2]
    same[...] = held[pl.ds(pl.multiple_of(z * HALF, HALF), HALF), :]
    other[...] = held[pl.ds(pl.multiple_of((1 - z) * HALF, HALF), HALF), :]


def one_hot(indices, axis):
    return (indices == lax.broadcasted_iota(jnp.int32, indices.shape, axis)).astype(jnp.float32)


def expanded(matrix, row_of, row_lane, column_of, column_lane, left, right):
    k, m = matrix.shape
    one = one_hot(row_of(lax.broadcasted_iota(jnp.int32, (left, m), 0)), 1)
    tall = nt(one.astype(jnp.bfloat16), matrix).astype(jnp.bfloat16)
    one = one_hot(column_of(lax.broadcasted_iota(jnp.int32, (k, right), 1)), 0)
    wide = jnp.dot(tall, one.astype(jnp.bfloat16), preferred_element_type=jnp.float32)
    at_row = row_lane(lax.broadcasted_iota(jnp.int32, (left, right), 0))
    at_column = column_lane(lax.broadcasted_iota(jnp.int32, (left, right), 1))
    return jnp.where(at_row == at_column, wide, 0.0).astype(jnp.bfloat16)


def repeated(bias, row_of, left):
    one = one_hot(row_of(lax.broadcasted_iota(jnp.int32, (left, bias.shape[0]), 0)), 1)
    wide = jnp.broadcast_to(bias[...], (bias.shape[0], 128))
    return jnp.dot(one, wide, precision=lax.Precision.HIGHEST, preferred_element_type=jnp.float32)


def spread_kernel(
    first, first_bias, second, second_bias, table, first_out, second_out, second_bias_out, table_out
):
    by_eight, eight = lambda r: r // 8, lambda r: r % 8
    by_four, four = lambda r: r // 4, lambda r: r % 4
    hid, outs = first.shape[1], second.shape[1]
    channel = lambda r: r % (hid * 4) // 4
    width = first.shape[0] * 8
    first_out[:, :width] = expanded(
        first[...],
        channel,
        lambda r: r // (hid * 4) * 4 + r % 4,
        by_eight,
        eight,
        hid * 8,
        width,
    )
    rest, parts = repeated(first_bias, channel, hid * 8)[:, :ONES], []
    for _ in range(3):
        parts.append(rest.astype(jnp.bfloat16).astype(jnp.float32))
        rest = rest - parts[-1]
    lane = lax.broadcasted_iota(jnp.int32, (hid * 8, ONES), 1)
    first_out[:, width:] = sum(
        jnp.where(lane == i, part, 0.0) for i, part in enumerate(parts)
    ).astype(jnp.bfloat16)
    second_out[: outs * 4] = expanded(second[...], by_four, four, by_four, four, outs * 4, hid * 4)
    second_out[outs * 4 :] = expanded(
        second[...], lambda r: r // 4 + 1 - r // 4 % 2 * 2, four, by_four, four, outs * 4, hid * 4
    )
    second_bias_out[...] = repeated(second_bias, by_eight, outs * 8)
    table_out[...] = expanded(
        table[...], by_eight, eight, by_eight, eight, outs * 8, table_out.shape[1]
    )


def relative_kernel(where, lengths, table, out):
    ends = [lengths[0], lengths[0] + lengths[1], lengths[0] + lengths[1] + lengths[2]]

    def residue(positions):
        return positions + GAP * sum((positions >= end).astype(jnp.int32) for end in ends)

    band = where[0] * 8 + where[1] * 2 + where[2]
    first_row = band * HALF + pl.program_id(0) * ROWS
    levels = lax.broadcasted_iota(jnp.int32, (72, 8, TILE), 0)
    columns = residue(where[3] * TILE + lax.broadcasted_iota(jnp.int32, (8, TILE), 1))
    halves = []
    for half in range(ROWS // 8):
        rows = residue(first_row + half * 8 + lax.broadcasted_iota(jnp.int32, (8, TILE), 0))
        bins = jnp.clip(columns - rows, -CLIP, CLIP) + CLIP
        spread = (bins[None] == levels).astype(jnp.float32).reshape(72 * 8, TILE)
        part = jnp.dot(
            table[...], spread.astype(jnp.bfloat16), preferred_element_type=jnp.float32
        )
        halves.append(part.reshape(-1, 8, TILE))
    out[...] = jnp.concatenate(halves, axis=1).astype(jnp.bfloat16)


def pair_kernel(tiles, first, second, second_bias, relative, out):
    start = pl.multiple_of(pl.program_id(0) * ROWS, ROWS)
    loaded = tiles[:, pl.ds(start, ROWS), :].astype(jnp.float32)
    outs, hid = second.shape[0] // 8, first.shape[0] // 8
    upper = lax.broadcasted_iota(jnp.int32, (outs // 2, 8, TILE), 1) < 4
    ones = jnp.ones((ONES, TILE), jnp.bfloat16)
    halves = []
    for half in range(ROWS // 8):
        stacked = loaded[:, half * 8 : half * 8 + 8, :].reshape(-1, TILE).astype(jnp.bfloat16)
        stacked = jnp.concatenate([stacked, ones], axis=0)
        hidden = jnp.dot(first[...], stacked, preferred_element_type=jnp.float32)
        hidden = jnp.maximum(hidden, 0.0).astype(jnp.bfloat16)
        low, high = (
            jnp.dot(
                second[part * outs * 4 : (part + 1) * outs * 4],
                hidden[part * hid * 4 : (part + 1) * hid * 4],
                preferred_element_type=jnp.float32,
            ).reshape(outs // 2, 8, TILE)
            for part in range(2)
        )
        even = jnp.where(upper, low, high)
        odd = pltpu.roll(jnp.where(upper, high, low), 4, 1)
        projected = jnp.stack([even, odd], axis=1).reshape(outs, 8, TILE)
        halves.append(
            projected + jnp.concatenate([second_bias[...]] * 4, axis=1).reshape(outs, 8, TILE)
        )
    out[...] = (
        jnp.concatenate(halves, axis=1) + relative[...].astype(jnp.float32)
    ).astype(jnp.bfloat16)


SMEM = pl.BlockSpec(memory_space=pltpu.SMEM)
ANY = pl.BlockSpec(memory_space=pl.ANY)
HBM = pl.BlockSpec(memory_space=pltpu.HBM)
VMEM = pl.BlockSpec(memory_space=pltpu.VMEM)


def params(mib):
    return pltpu.CompilerParams(vmem_limit_bytes=mib * MIB)


def cost(flops, bytes_accessed, exponentials=0):
    return pl.CostEstimate(
        flops=int(flops), bytes_accessed=int(bytes_accessed), transcendentals=int(exponentials)
    )


def in_hbm(value):
    return pltpu.with_memory_space_constraint(value, pltpu.HBM)


def vmem(rows, columns):
    return pltpu.VMEM((rows, columns), jnp.bfloat16)


def shape(dims, kind=jnp.bfloat16):
    return jax.ShapeDtypeStruct(dims, kind)


def local(queries, keys, values, w_first, b_first, w_second, b_second, rel_table, chain_lengths):
    band, c = lax.axis_index("band"), lax.axis_index("head")
    y, x, z = band // 8, (band // 2) % 4, band % 2
    where = jnp.stack([y, x, z, c]).astype(jnp.int32)
    hid, outs = w_first.shape[1], w_second.shape[1]

    first, second, second_bias, table = pl.pallas_call(
        spread_kernel,
        in_specs=[VMEM] * 5,
        out_specs=[VMEM] * 4,
        out_shape=[
            pltpu.HBM((hid * 8, 8 * GROUP * 8 + ONES), jnp.bfloat16),
            pltpu.HBM((outs * 8, hid * 4), jnp.bfloat16),
            pltpu.HBM((outs * 8, 128), jnp.float32),
            shape((outs * 8, 72 * 8)),
        ],
        compiler_params=params(6),
        cost_estimate=cost(4e8, 6e6),
        name="spread",
    )(
        w_first,
        b_first[:, None],
        w_second,
        b_second[:, None],
        jnp.pad(rel_table, ((0, 72 - BINS), (0, 0))),
    )

    def half(at):
        near, far = (
            jnp.concatenate([a[:, lo : lo + WIDE] for a in (queries, keys, values)], axis=1)
            for lo in (0, WIDE)
        )
        return jnp.where(at == 0, near, far)

    crossing = half(1 - z)
    crossing, z = lax.optimization_barrier((crossing, z))
    other = send(crossing, lambda y, x, z, c: (c, x, 1 - z, y))
    same = send(half(z), lambda y, x, z, c: (c, x, z, y))
    block = jnp.where(
        z == 0,
        jnp.concatenate([same, other], axis=0),
        jnp.concatenate([other, same], axis=0),
    )

    block, first, second, second_bias, table = lax.optimization_barrier(
        (block, first, second, second_bias, table)
    )
    narrow = block[:, : 2 * WIDE]

    across = send(block, lambda y, x, z, c: (y, x, z, c ^ 2))
    right = send(narrow, lambda y, x, z, c: (y, (x + 1) % 4, z, c))
    left = send(narrow, lambda y, x, z, c: (y, (x + 3) % 4, z, c))
    relative = pl.pallas_call(
        relative_kernel,
        grid=(HALF // ROWS,),
        in_specs=[SMEM, SMEM, pl.BlockSpec((outs * 8, 72 * 8), lambda i: (0, 0))],
        out_specs=pl.BlockSpec((outs, ROWS, TILE), lambda i: (0, i, 0)),
        out_shape=pltpu.HBM((outs, HALF, TILE), jnp.bfloat16),
        compiler_params=params(8),
        cost_estimate=cost(2.4e9, 6e6),
        name="relative",
    )(where, chain_lengths, table)
    where, relative, left, right = lax.optimization_barrier((where, relative, left, right))
    column_blocks = [
        narrow,
        right,
        left,
        send(right[:HALF], lambda y, x, z, c: (y, (x + 1) % 4, z, c)),
        send(left[HALF:], lambda y, x, z, c: (y, (x + 3) % 4, z, c)),
    ]
    relative, across, block = lax.optimization_barrier((relative, across, block))
    beside = send(block, lambda y, x, z, c: (y, x, z, c ^ 1))
    row_blocks = [block, beside, across, send(across, lambda y, x, z, c: (y, x, z, c ^ 1))]

    near = len(NEAR) * BLOCK
    near_outs = [
        shape((16, TILE), jnp.float32),
        shape((16, near), jnp.float32),
        *[shape((GROUP, TILE, near))] * 2,
    ]
    near_by_row, near_by_column, *near_lifted = pl.pallas_call(
        near_kernel,
        in_specs=[VMEM] * 7,
        out_specs=[VMEM] * len(near_outs),
        out_shape=near_outs,
        compiler_params=params(16),
        cost_estimate=cost(6e8, 11e6, 2e6),
        name="near",
    )(*row_blocks, *column_blocks[:3])
    near_by_row, *column_blocks[3:] = lax.optimization_barrier((near_by_row, *column_blocks[3:]))
    far_outs = [
        shape((16, TILE), jnp.float32),
        shape((8, TILE), jnp.float32),
        shape((16, TILE), jnp.float32),
        *[shape((GROUP, TILE, BLOCK))] * 2,
    ]
    by_row, far_top, by_column, *far_lifted = pl.pallas_call(
        far_kernel,
        in_specs=[SMEM] + [VMEM] * 8,
        out_specs=[VMEM] * len(far_outs),
        out_shape=far_outs,
        scratch_shapes=[pltpu.VMEM((16, BLOCK), jnp.float32)],
        compiler_params=params(12),
        cost_estimate=cost(3e8, 5e6, 7e5),
        name="far",
    )(where, *row_blocks, *column_blocks[3:], near_by_row, near_by_column)
    own_partial, right_partial, left_partial, far_partial = pl.pallas_call(
        partial_kernel,
        in_specs=[VMEM] * 6,
        out_specs=[VMEM] * 4,
        out_shape=[shape((WIDE, BLOCK))] * 4,
        compiler_params=params(12),
        cost_estimate=cost(3.4e8, 4e6),
        name="partials",
    )(*row_blocks, near_lifted[1], far_lifted[1])
    partials = [own_partial, left_partial, far_partial, right_partial]
    beside_by_row = send(by_row, lambda y, x, z, c: (y, x, z, c ^ 1))
    both_by_row = pl.pallas_call(
        merge_kernel,
        in_specs=[VMEM] * 2,
        out_specs=VMEM,
        out_shape=shape((16, TILE), jnp.float32),
        compiler_params=params(2),
        cost_estimate=cost(0, 1e5),
        name="merge",
    )(by_row, beside_by_row)
    row_stats = [both_by_row, send(both_by_row, lambda y, x, z, c: (y, x, z, c ^ 2))]
    column_stats = [by_column] + over_columns(by_column)

    where, *partials = lax.optimization_barrier((where, *partials))
    tiles = pl.pallas_call(
        symmetric_kernel,
        in_specs=[SMEM] + [VMEM] * 12,
        out_specs=HBM,
        out_shape=shape((8, GROUP, HALF, TILE)),
        scratch_shapes=[
            pltpu.VMEM((16, TILE), jnp.float32),
            pltpu.VMEM((8, GROUP, HALF, TILE), jnp.bfloat16),
            pltpu.SemaphoreType.DMA((8,)),
        ],
        compiler_params=params(8),
        cost_estimate=cost(1e7, 9e6),
        name="symmetric",
    )(
        where,
        *row_stats,
        *column_stats,
        near_by_row,
        far_top,
        *(part for parts in zip(near_lifted, far_lifted) for part in parts),
    )
    where, tiles = lax.optimization_barrier((where, tiles))
    groups = [[y * 8 + x * 2 + z for y in range(4) for z in range(2)] for x in range(4)]
    received = lax.all_to_all(
        tiles, "band", split_axis=0, concat_axis=0, axis_index_groups=groups, tiled=True
    ).reshape(8 * GROUP, HALF, TILE)

    same, other = pl.pallas_call(
        context_kernel,
        in_specs=[SMEM] + [VMEM] * 8,
        out_specs=[VMEM] * 2,
        out_shape=[shape((HALF, WIDE))] * 2,
        scratch_shapes=[vmem(BLOCK, WIDE)],
        compiler_params=params(4),
        cost_estimate=cost(1e6, 2e6),
        name="context",
    )(where, *column_stats, partials[0], *over_columns_of(partials))
    same = send(same, lambda y, x, z, c: (c, x, z, y))
    other = send(other, lambda y, x, z, c: (c, x, 1 - z, y))

    pair = pl.pallas_call(
        pair_kernel,
        grid=(HALF // ROWS,),
        in_specs=[
            VMEM,
            pl.BlockSpec((hid * 8, 8 * GROUP * 8 + ONES), lambda i: (0, 0)),
            pl.BlockSpec((outs * 8, hid * 4), lambda i: (0, 0)),
            pl.BlockSpec((outs * 8, 128), lambda i: (0, 0)),
            pl.BlockSpec((outs, ROWS, TILE), lambda i: (0, i, 0)),
        ],
        out_specs=pl.BlockSpec((outs, ROWS, TILE), lambda i: (0, i, 0)),
        out_shape=shape((outs, HALF, TILE)),
        compiler_params=params(14),
        cost_estimate=cost(5e9, 14e6),
        name="pair",
    )(received, *(in_hbm(a) for a in (first, second, second_bias, relative)))
    same, other, pair = lax.optimization_barrier((same, other, pair))
    context = jnp.where(
        z == 0,
        jnp.concatenate([same, other], axis=1),
        jnp.concatenate([other, same], axis=1),
    )
    return (context, pair)


def solution(mesh):
    return jax.shard_map(
        local,
        mesh=mesh,
        in_specs=(
            P("band", "head"),
            P("band", "head"),
            P("band", "head"),
            P(),
            P(),
            P(),
            P(),
            P(),
            P(),
        ),
        out_specs=(P("band", "head"), P(None, "band", "head")),
        check_vma=False,
    )
```
